32 devices in a mesh: section: 4 (over y, x), dp: 8 (over z, core).
Axes of the slice: x: 2, y: 2, z: 4, core: 2. Of those that a mesh axis runs over, the one named last changes fastest.
Arguments:
- inputs: bfloat16 [4, 4096, 768], P('section', 'dp'), may hold values from -6 to 6
- cotangent: bfloat16 [4, 4096, 768], P('section', 'dp'), may hold values from -6 to 6
- wide: bfloat16 [4, 768, 3072], P('section'), may hold values from -0.21875 to 0.21875
- down: bfloat16 [4, 3072, 768], P('section'), may hold values from -0.109375 to 0.109375
- vectors: float32 [4, 7, 768], P('section'), may hold values from -1.6 to 2.6
- seg_counts: int32 [8, 4, 4], P('dp'), may hold values from 0 to 4, as said below
Outputs:
- layer_out: bfloat16 [4, 4096, 768], P('section', 'dp')
- input_grad: bfloat16 [4, 4096, 768], P('section', 'dp')
- wide_grad: float32 [4, 768, 3072], P('section')
- down_grad: float32 [4, 3072, 768], P('section')
- vectors_grad: float32 [4, 7, 768], P('section')
The draws below stay inside these ranges and needn't reach their ends.
Inputs may be any that keep to these rules, and one draw needn't show every extreme that they name: seg_counts[r, m] are the segment counts of the documents of micro-batch m on dp index r, in order; they sum to 4, trailing ones may be 0, and on every dp index one micro-batch holds a single document of 4 segments.
All inputs are finite; a program needn't handle non-finite values.
Results may differ from the reference program's by a relative error of at most 0.009.
Values may be sent and summed in bfloat16 or wider, within the bound.
No kernel may reach another device: no remote copies, remote signals or barrier semaphores. Data moves between devices by JAX's collectives and lax.ppermute only.
A program may use at most 256 MiB of HBM per device.

```python
import jax
import jax.numpy as jnp
from jax import lax

D = 768
HEADS = 12
FF = 3072
SEG = 128
SEGS = 4
DOCS = 4
MB = 4
N_SECTION = 4
N_DP = 8


def draw_vectors(key, part):
    key = jax.random.fold_in(key, 11)
    shape_all = (N_SECTION, 3 + SEGS, D)
    base_draw = jnp.clip(jax.random.normal(key, shape_all, jnp.float32) * 0.4, -1.6, 1.6)
    lifted = (jnp.arange(3 + SEGS) == 0).astype(jnp.float32)[None, :, None]
    return base_draw + lifted


def draw_seg_counts(key, part):
    key = jax.random.fold_in(key, 23)
    row_keys = jax.random.split(key, N_DP * MB)

    def compose(row_key):
        cut_points = jnp.sort(jax.random.permutation(row_key, SEGS - 1)[:DOCS - 1]).astype(jnp.int32) + 1
        bounds = jnp.concatenate([jnp.zeros((1,), jnp.int32), cut_points, jnp.full((1,), SEGS, jnp.int32)])
        return bounds[1:] - bounds[:-1]
    pieces = jax.vmap(compose)(row_keys).reshape(N_DP, MB, DOCS)
    chosen = jax.random.randint(jax.random.fold_in(key, 5), (N_DP, 1), 0, MB)
    single = jnp.where(jnp.arange(DOCS) == 0, SEGS, 0).astype(jnp.int32)
    is_long = (jnp.arange(MB)[None, :] == chosen)[:, :, None]
    return jnp.where(is_long, single[None, None, :], pieces).astype(jnp.int32)


def block_scale(stream_key, shape, cuts, low, top_value):
    gain, own = 1.0, jax.random.fold_in(stream_key, 6)
    for dim, blocks in cuts:
        heights = jnp.exp(jax.random.uniform(jax.random.fold_in(own, dim), (blocks,), jnp.float32, low / len(cuts), top_value / len(cuts)))
        gain = gain * jnp.repeat(heights, shape[dim] // blocks).reshape([-1 if axis == dim else 1 for axis in range(len(shape))])
    return gain


def normal_values(own_key, shape, deviation, most, cuts=(), held_as=jnp.bfloat16):
    factor_of = block_scale(own_key, shape, cuts, -0.22, 0.18) if cuts else 1.0
    result = jax.random.normal(own_key, shape, jnp.float32) * deviation * factor_of
    return jnp.minimum(jnp.maximum(result, -most), most).astype(held_as)


def setup_inputs(seed: int = 0) -> dict:
    keys = jax.random.split(jax.random.key(seed), 7)
    inputs = normal_values(keys[0], (MB, N_DP * SEG * SEGS, D), 1.0, 6.0, ((0, 4), (1, 8)))
    cotangent = normal_values(keys[1], (MB, N_DP * SEG * SEGS, D), 1.0, 6.0, ((0, 4), (1, 8)))
    wide = normal_values(keys[2], (N_SECTION, D, FF), D ** -0.5, 0.21875, ((0, 4),))
    down = normal_values(keys[3], (N_SECTION, FF, D), FF ** -0.5, 0.109375, ((0, 4),))
    vectors = draw_vectors(jax.random.fold_in(keys[6], 71), 0)
    seg_counts = draw_seg_counts(jax.random.fold_in(keys[6], 71), 0)
    return dict(inputs=inputs, cotangent=cotangent, wide=wide, down=down, vectors=vectors, seg_counts=seg_counts)


@jax.custom_vjp
def low(v):
    return lax.optimization_barrier(v.astype(jnp.bfloat16)).astype(jnp.float32)

@jax.custom_vjp
def low_back(v):
    return v

def low_keep(v):
    return (low(v), None)

def low_pass(kept, grad):
    return (grad,)

def back_keep(v):
    return (v, None)

def back_low(kept, grad):
    return (low(grad),)
low.defvjp(low_keep, low_pass)
low_back.defvjp(back_keep, back_low)
EPSILON = 1e-05
SCORE_SCALE = 0.125
MASKED = -1e+30
PRECISE = lax.Precision.HIGHEST

def sent_value(values):
    return low_back(low(values))

def matmul(left_side, right_side):
    return jnp.dot(left_side, right_side, precision=PRECISE)

def norm_rows(values, gain_row, shift_row):
    center = values - lax.optimization_barrier(jnp.mean(values, -1, keepdims=True))
    spread = lax.optimization_barrier(jnp.mean(center * center, -1, keepdims=True))
    return center * lax.rsqrt(spread + EPSILON) * gain_row + shift_row

def segment_layout(counts):
    places = jnp.arange(SEGS, dtype=jnp.int32)
    doc_ends = jnp.cumsum(counts).astype(jnp.int32)
    doc_index = lax.optimization_barrier(jnp.sum((places[:, None] >= doc_ends[None, :]).astype(jnp.int32), 1))
    starts = (doc_ends - counts).astype(jnp.int32)
    doc_slots = jnp.arange(counts.shape[0], dtype=jnp.int32)
    doc_first = lax.optimization_barrier(jnp.sum(jnp.where(doc_index[:, None] == doc_slots[None, :], starts[None, :], 0), 1))
    position = places - doc_first
    same_doc = doc_index[:, None] == doc_index[None, :]
    onehot = (position[:, None] == places[None, :]).astype(jnp.float32)
    return (same_doc, onehot)

def attention_block(values, wide_w, vector, allowed, groups, length):
    features = values.shape[-1]
    normed = low(norm_rows(values, vector[0], vector[1]))
    query_rows = sent_value(matmul(normed, wide_w[:, :features])).reshape(groups, length, HEADS, -1)
    key_rows = sent_value(matmul(normed, wide_w[:, features:2 * features])).reshape(groups, length, HEADS, -1)
    value_rows = sent_value(matmul(normed, wide_w[:, 2 * features:3 * features])).reshape(groups, length, HEADS, -1)
    scores = low_back(jnp.einsum('glhe,gmhe->ghlm', query_rows, key_rows, precision=PRECISE) * SCORE_SCALE)
    scores = jnp.where(allowed[:, None], scores, MASKED)
    maxima = lax.optimization_barrier(jnp.max(scores, -1, keepdims=True))
    powers = jnp.exp(scores - maxima)
    weights = low(powers / lax.optimization_barrier(jnp.sum(powers, -1, keepdims=True)))
    mixture = sent_value(jnp.einsum('ghlm,gmhe->glhe', weights, value_rows, precision=PRECISE))
    mixture = mixture.reshape(groups * length, features)
    return values + low_back(matmul(mixture, wide_w[:, 3 * features:])) + vector[2]

def mlp_block(values, wide_w, down_w, vector):
    normed = low(norm_rows(values, vector[0], vector[1]))
    hidden = low_back(matmul(normed, wide_w))
    active = low(jax.nn.gelu(hidden, approximate=True))
    return values + low_back(matmul(active, down_w)) + vector[2]

def two_layers(tokens, wide_all, down_all, vector_all, same_doc, onehot):
    features = tokens.shape[-1]
    allowed = jnp.ones((1, SEG, SEG), bool)
    first_out = sent_value(attention_block(tokens, wide_all[0], vector_all[0], allowed, SEGS, SEG))
    second_out = sent_value(mlp_block(first_out, wide_all[1], down_all[1], vector_all[1]))
    seg_grid = second_out.reshape(SEGS, SEG, features)
    lifted = seg_grid[:, 0] + matmul(onehot, vector_all[2, 3:])
    crossed = attention_block(lifted, wide_all[2], vector_all[2], same_doc[None], 1, SEGS)
    third_out = sent_value(seg_grid.at[:, 0].set(crossed).reshape(SEGS * SEG, features))
    seg_grid = third_out.reshape(SEGS, SEG, features)
    final_rows = mlp_block(seg_grid[:, 0], wide_all[3], down_all[3], vector_all[3])
    return seg_grid.at[:, 0].set(final_rows).reshape(SEGS * SEG, features)

def reference(inputs, cotangent, wide, down, vectors, seg_counts):
    row_count = SEG * SEGS
    pack_rows = inputs.reshape(MB * N_DP, row_count, D)
    pack_cots = cotangent.reshape(MB * N_DP, row_count, D)
    pack_counts = jnp.transpose(seg_counts, (1, 0, 2)).reshape(MB * N_DP, DOCS)
    wide_all = wide.astype(jnp.float32)
    down_all = down.astype(jnp.float32)
    vector_all = vectors.astype(jnp.float32)

    def one_pack(totals, pack_item):
        tokens, cotan_rows, counts = pack_item
        same_doc, onehot = segment_layout(counts)

        def forward(token_rows, wide_in, down_in, vector_in):
            return two_layers(token_rows, wide_in, down_in, vector_in, same_doc, onehot)
        layer_rows, pull_back = jax.vjp(forward, tokens.astype(jnp.float32), wide_all, down_all, vector_all)
        grads_all = pull_back(cotan_rows.astype(jnp.float32))
        totals = (totals[0] + grads_all[1], totals[1] + grads_all[2], totals[2] + grads_all[3])
        return (totals, (layer_rows.astype(jnp.bfloat16), grads_all[0].astype(jnp.bfloat16)))
    zero_sums = (jnp.zeros_like(wide_all), jnp.zeros_like(down_all), jnp.zeros_like(vector_all))
    totals, (out_rows, back_rows) = lax.scan(one_pack, zero_sums, (pack_rows, pack_cots, pack_counts))
    layer_out = out_rows.reshape(MB, N_DP * row_count, D)
    input_grad = back_rows.reshape(MB, N_DP * row_count, D)
    return (layer_out, input_grad, totals[0], totals[1], totals[2])
```

```python
from functools import partial

import jax
import jax.numpy as jnp
from jax import lax
from jax.experimental import pallas as pl
from jax.experimental.pallas import tpu as pltpu
from jax.sharding import PartitionSpec as P

HEADS = 12
SEG = 128
SEGS = 4
EPSILON = 1e-05
SCORE_SCALE = 0.125
MASKED = -1e30
AXES = ("section", "dp")
BF = jnp.bfloat16
F32 = jnp.float32

NN = (((1,), (0,)), ((), ()))
NT = (((1,), (1,)), ((), ()))
TN = (((0,), (0,)), ((), ()))

GELU_A = 0.7978845608028654
GELU_B = 0.044715

ATT_RINGS = ((0, 1, 3, 2), (0, 2, 3, 1))
MLP_RINGS = ((1, 3, 2, 0), (1, 0, 2, 3))


def mm(left, right, dims=NN):
    return lax.dot_general(left, right, dims, preferred_element_type=F32)


def permute(shard, move, keep=lambda s, r: True):
    sections, replicas = lax.axis_size("section"), lax.axis_size("dp")
    pairs = []
    for s in range(sections):
        for r in range(replicas):
            if keep(s, r):
                t, q = move(s, r)
                pairs.append((s * replicas + r, t * replicas + q))
    return lax.ppermute(shard, AXES, pairs)


def swap_core(shard):
    return permute(shard, lambda s, r: (s, r ^ 1))


def swap_section(shard, bits):
    return permute(shard, lambda s, r: (s ^ bits, r))


def swap_dp(shard, bits):
    return permute(shard, lambda s, r: (s, r ^ bits))


def broadcast(parts, rings, position):
    result = []
    for part in parts:
        hops = [part]
        for stage in range(3):
            hops.append(
                permute(
                    hops[-1],
                    lambda s, r: (rings[r & 1][stage + 1], r),
                    lambda s, r: rings[r & 1][stage] == s,
                )
            )
        value = hops[3]
        for stage in (2, 1, 0):
            value = jnp.where(position == stage, hops[stage], value)
        result.append(value)
    return result


def ring_position(rings, section, core):
    position = jnp.int32(0)
    for c in range(2):
        for k, s in enumerate(rings[c]):
            position = jnp.where((section == s) & (core == c), k, position)
    return position


def pick(stack, index):
    return lax.dynamic_index_in_dim(stack, index, 0, keepdims=False)


def reduce_pieces(grad, section, owner):
    replicas = lax.axis_size("dp")
    total = pick(grad, section).astype(F32)
    others = [swap_section(pick(grad, section ^ bits), bits) for bits in (1, 2, 3)]
    for other in others:
        total = total + other.astype(F32)
    total = total.astype(BF)
    bits = 2
    while bits < replicas:
        total = (total.astype(F32) + swap_dp(total, bits).astype(F32)).astype(BF)
        bits *= 2
    arrived = [
        permute(total, lambda s, r: (owner, r), lambda s, r: s == owner ^ bits) for bits in (1, 2, 3)
    ]
    quarters = [None] * 4
    quarters[owner] = total
    for bits, value in zip((1, 2, 3), arrived):
        quarters[owner ^ bits] = value
    return jnp.stack(quarters)


def norm_parts(values):
    center = values - jnp.mean(values, -1, keepdims=True)
    spread = jnp.mean(center * center, -1, keepdims=True)
    scale = lax.rsqrt(spread + EPSILON)
    return center * scale, scale


def norm_rows(values, vec_ref):
    hat, _ = norm_parts(values)
    return hat * vec_ref[0:1, :] + vec_ref[1:2, :]


def norm_back(values, grad_normed, vec_ref):
    hat, scale = norm_parts(values)
    inner = grad_normed * vec_ref[0:1, :]
    first = jnp.mean(inner, -1, keepdims=True)
    second = jnp.mean(inner * hat, -1, keepdims=True)
    return scale * (inner - first - hat * second), grad_normed * hat


def column_sum(values):
    return jnp.sum(values, 0, keepdims=True)


def gelu_parts(hidden):
    square = hidden * hidden
    inner = GELU_A * hidden * (1.0 + GELU_B * square)
    t = jnp.tanh(inner)
    half = 0.5 * (1.0 + t)
    slope = half + 0.5 * hidden * (1.0 - t * t) * (GELU_A * (1.0 + 3.0 * GELU_B * square))
    return hidden * half, slope


def two_heads(pair):
    low = lax.broadcasted_iota(jnp.int32, pair.shape, 1) < 64
    zero = jnp.zeros_like(pair)
    return jnp.concatenate([jnp.where(low, pair, zero), jnp.where(low, zero, pair)], 0)


def join_heads(both):
    rows = both.shape[0] // 2
    low = lax.broadcasted_iota(jnp.int32, (rows, both.shape[1]), 1) < 64
    return jnp.where(low, both[:rows], both[rows:])


def softmax_rows(scores):
    powers = jnp.exp(scores - jnp.max(scores, -1, keepdims=True))
    return powers / jnp.sum(powers, -1, keepdims=True)


def att_fwd_kernel(own_ref, sib_ref, wq, wk, wv, wo, vec_ref, q_ref, k_ref, v_ref, a_ref, p_ref, u_ref):
    rows = own_ref.shape[0]
    for pack, ref in enumerate((own_ref, sib_ref)):

        @pl.loop(0, rows // SEG)
        def _(i):
            at = pl.multiple_of(i * SEG, SEG)
            u_ref[pl.ds(pack * rows + at, SEG), :] = norm_rows(ref[pl.ds(at, SEG), :].astype(F32), vec_ref).astype(BF)

    for pack in range(2):
        span = slice(pack * rows, (pack + 1) * rows)
        u = u_ref[span, :]
        q_ref[span, :] = mm(u, wq[...]).astype(BF)
        k_ref[span, :] = mm(u, wk[...]).astype(BF)
        v_ref[span, :] = mm(u, wv[...]).astype(BF)

    @pl.loop(0, 2 * rows // SEG)
    def _(i):
        at = pl.ds(pl.multiple_of(i * SEG, SEG), SEG)
        for pair in range(q_ref.shape[1] // 128):
            lanes = slice(pair * 128, (pair + 1) * 128)
            scores = mm(two_heads(q_ref[at, lanes]), k_ref[at, lanes], NT) * SCORE_SCALE
            weights = softmax_rows(scores).astype(BF)
            a_ref[at, lanes] = join_heads(mm(weights, v_ref[at, lanes])).astype(BF)

    for pack in range(2):
        span = slice(pack * rows, (pack + 1) * rows)
        p_ref[span, :] = mm(a_ref[span, :], wo[...]).astype(BF)


def att_bwd_kernel(
    own_ref, sib_ref, gown_ref, gsib_ref, q_ref, k_ref, v_ref, a_ref, wq, wk, wv, wo, vec_ref,
    grad_ref, duown_ref, dusib_ref, u_ref, da_ref, dq_ref, dk_ref, dv_ref,
):
    rows = own_ref.shape[0]
    half = q_ref.shape[1]
    for pack, ref in enumerate((own_ref, sib_ref)):

        @pl.loop(0, rows // SEG)
        def _(i):
            at = pl.multiple_of(i * SEG, SEG)
            u_ref[pl.ds(pack * rows + at, SEG), :] = norm_rows(ref[pl.ds(at, SEG), :].astype(F32), vec_ref).astype(BF)

    for pack, ref in enumerate((gown_ref, gsib_ref)):
        da_ref[pack * rows : (pack + 1) * rows, :] = mm(ref[...], wo[...], NT).astype(BF)
    dwo = mm(a_ref[:rows, :], gown_ref[...], TN) + mm(a_ref[rows:, :], gsib_ref[...], TN)
    part = half // 4
    for quarter in range(4):
        grad_ref[quarter, 3 * part :, :] = dwo[quarter * part : (quarter + 1) * part, :].astype(BF)

    @pl.loop(0, 2 * rows // SEG)
    def _(i):
        at = pl.ds(pl.multiple_of(i * SEG, SEG), SEG)
        for pair in range(half // 128):
            lanes = slice(pair * 128, (pair + 1) * 128)
            q2 = two_heads(q_ref[at, lanes])
            da2 = two_heads(da_ref[at, lanes])
            k = k_ref[at, lanes]
            v = v_ref[at, lanes]
            probs = softmax_rows(mm(q2, k, NT) * SCORE_SCALE)
            dy = mm(da2, v, NT)
            ds = (probs * (dy - jnp.sum(dy * probs, -1, keepdims=True))).astype(BF)
            dv_ref[at, lanes] = mm(probs.astype(BF), da2, TN).astype(BF)
            dq_ref[at, lanes] = (join_heads(mm(ds, k)) * SCORE_SCALE).astype(BF)
            dk_ref[at, lanes] = (mm(ds, q2, TN) * SCORE_SCALE).astype(BF)

    for pack, out in enumerate((duown_ref, dusib_ref)):
        span = slice(pack * rows, (pack + 1) * rows)
        du = mm(dq_ref[span, :], wq[...], NT) + mm(dk_ref[span, :], wk[...], NT) + mm(dv_ref[span, :], wv[...], NT)
        out[...] = du.astype(out.dtype)
    dwq = mm(u_ref[...], dq_ref[...], TN)
    for quarter in range(4):
        grad_ref[quarter, : 2 * part, :half] = dwq[quarter * 2 * part : (quarter + 1) * 2 * part, :].astype(BF)
    dwk = mm(u_ref[...], dk_ref[...], TN)
    for quarter in range(4):
        grad_ref[quarter, : 2 * part, half:] = dwk[quarter * 2 * part : (quarter + 1) * 2 * part, :].astype(BF)
    dwv = mm(u_ref[...], dv_ref[...], TN)
    for quarter in range(4):
        grad_ref[quarter, 2 * part : 3 * part, :half] = dwv[quarter * part : (quarter + 1) * part, :].astype(BF)
        grad_ref[quarter, 2 * part : 3 * part, half:] = dwv[half + quarter * part : half + (quarter + 1) * part, :].astype(BF)


def att_done_kernel(x_ref, g_ref, duown_ref, dusib_ref, vec_ref, out_ref, small_ref):
    small_ref[...] = jnp.zeros_like(small_ref)

    @pl.loop(0, x_ref.shape[0] // SEG)
    def _(i):
        at = pl.ds(pl.multiple_of(i * SEG, SEG), SEG)
        du = duown_ref[at, :] + dusib_ref[at, :].astype(F32)
        grad = g_ref[at, :].astype(F32)
        back, gain = norm_back(x_ref[at, :].astype(F32), du, vec_ref)
        out_ref[at, :] = (grad + back).astype(BF)
        small_ref[0:1, :] += column_sum(gain)
        small_ref[1:2, :] += column_sum(du)
        small_ref[2:3, :] += column_sum(grad)


def att_join_kernel(own_ref, sib_ref, p_ref, r_ref, avec_ref, mvec_ref, h_ref, u_ref):
    rows = own_ref.shape[0]
    for pack, ref in enumerate((own_ref, sib_ref)):

        @pl.loop(0, rows // SEG)
        def _(i):
            at = pl.multiple_of(i * SEG, SEG)
            here, there = pl.ds(pack * rows + at, SEG), pl.ds((1 - pack) * rows + at, SEG)
            branch = p_ref[here, :].astype(F32) + r_ref[there, :].astype(F32)
            out = (ref[pl.ds(at, SEG), :].astype(F32) + branch + avec_ref[2:3, :]).astype(BF)
            h_ref[here, :] = out
            u_ref[here, :] = norm_rows(out.astype(F32), mvec_ref).astype(BF)


def mlp_kernel(first, tile, u_ref, b_ref, w_ref, v_ref, *refs):
    if first:
        out_ref, du_ref, grad_ref = refs
        out_ref[...] = jnp.zeros_like(out_ref)
        du_ref[...] = jnp.zeros_like(du_ref)
    else:
        outin_ref, duin_ref, out_ref, du_ref, grad_ref = refs
        out_ref[...] = outin_ref[...]
        du_ref[...] = duin_ref[...]
    u = u_ref[...]
    b = b_ref[...]
    features, hidden = w_ref.shape
    quarter_w, quarter_v = features // 4, hidden // 4
    for j in range(hidden // tile):
        at = slice(j * tile, (j + 1) * tile)
        w, v = w_ref[:, at], v_ref[at, :]
        active, slope = gelu_parts(mm(u, w))
        active = active.astype(BF)
        out_ref[...] += mm(active, v)
        dh = (mm(b, v, NT) * slope).astype(BF)
        du_ref[...] += mm(dh, w, NT)
        dw = mm(u, dh, TN)
        for quarter in range(4):
            grad_ref[quarter, :quarter_w, at] = dw[quarter * quarter_w : (quarter + 1) * quarter_w, :].astype(BF)
        dv = mm(active, b, TN).astype(BF)
        done = 0
        while done < tile:
            row = j * tile + done
            quarter, inside = row // quarter_v, row % quarter_v
            count = min(quarter_v - inside, tile - done)
            grad_ref[quarter, quarter_w + inside : quarter_w + inside + count, :] = dv[done : done + count, :]
            done += count


def mlp_done_kernel(h_ref, b_ref, out_ref, outr_ref, du_ref, dur_ref, vec_ref, next_ref, grad_ref, small_ref):
    small_ref[...] = jnp.zeros_like(small_ref)

    @pl.loop(0, h_ref.shape[0] // SEG)
    def _(i):
        at = pl.ds(pl.multiple_of(i * SEG, SEG), SEG)
        values = h_ref[at, :].astype(F32)
        branch = out_ref[at, :] + outr_ref[at, :].astype(F32)
        next_ref[at, :] = (values + branch + vec_ref[2:3, :]).astype(BF)
        du = du_ref[at, :] + dur_ref[at, :].astype(F32)
        grad = b_ref[at, :].astype(F32)
        back, gain = norm_back(values, du, vec_ref)
        grad_ref[at, :] = (grad + back).astype(BF)
        small_ref[0:1, :] += column_sum(gain)
        small_ref[1:2, :] += column_sum(du)
        small_ref[2:3, :] += column_sum(grad)


def cls_mlp_kernel(weights_too, h_ref, b_ref, w_ref, v_ref, vec_ref, *refs):
    if weights_too:
        mainw_ref, mainv_ref, small_ref, dw_ref, dv_ref, u_ref, out_acc, du_acc = refs
    else:
        out_ref, grad_ref, u_ref, out_acc, du_acc = refs
    j = pl.program_id(0)

    @pl.when(j == 0)
    def _():
        u_ref[...] = norm_rows(h_ref[...].astype(F32), vec_ref).astype(BF)
        out_acc[...] = jnp.zeros_like(out_acc)
        du_acc[...] = jnp.zeros_like(du_acc)

    u = u_ref[...]
    b = b_ref[...]
    active, slope = gelu_parts(mm(u, w_ref[...]))
    active = active.astype(BF)
    dh = (mm(b, v_ref[...], NT) * slope).astype(BF)
    du_acc[...] += mm(dh, w_ref[...], NT)
    if weights_too:
        dw_ref[...] = mainw_ref[...].astype(F32) + mm(u, dh, TN)
        dv_ref[...] = mainv_ref[...].astype(F32) + mm(active, b, TN)
    else:
        out_acc[...] += mm(active, v_ref[...])

    @pl.when(j == pl.num_programs(0) - 1)
    def _():
        values = h_ref[...].astype(F32)
        grad = b.astype(F32)
        back, gain = norm_back(values, du_acc[...], vec_ref)
        if weights_too:
            small_ref[...] = jnp.zeros_like(small_ref)
            small_ref[0:1, :] = column_sum(gain)
            small_ref[1:2, :] = column_sum(du_acc[...])
            small_ref[2:3, :] = column_sum(grad)
        else:
            out_ref[...] = (values + out_acc[...] + vec_ref[2:3, :]).astype(BF)
            grad_ref[...] = (grad + back).astype(BF)


def lifted_rows(h_ref, pos_ref, vec_ref):
    values = h_ref[...].astype(F32)
    pos = pos_ref[...]
    for p in range(SEGS):
        values = values + jnp.where(pos == p, vec_ref[3 + p : 4 + p, :], 0.0)
    return values


def cls_att_forward(values, col_ref, row_ref, w_ref, vec_ref):
    features = values.shape[1]
    u = norm_rows(values, vec_ref).astype(BF)
    triple = mm(u, w_ref[:, : 3 * features]).astype(BF)
    column = jnp.concatenate([col_ref[...], col_ref[...]], 0)
    mask = column == row_ref[...]
    probs, mixed = [], []
    for pair in range(features // 128):
        lanes = slice(pair * 128, (pair + 1) * 128)
        q2 = two_heads(triple[:, lanes])
        k = triple[:, features + pair * 128 : features + (pair + 1) * 128]
        v = triple[:, 2 * features + pair * 128 : 2 * features + (pair + 1) * 128]
        scores = jnp.where(mask, mm(q2, k, NT) * SCORE_SCALE, MASKED)
        probs.append(softmax_rows(scores))
        mixed.append(join_heads(mm(probs[-1].astype(BF), v)).astype(BF))
    return u, triple, probs, jnp.concatenate(mixed, 1)


def cls_att_fwd_kernel(h_ref, pos_ref, col_ref, row_ref, w_ref, vec_ref, out_ref):
    values = lifted_rows(h_ref, pos_ref, vec_ref)
    features = values.shape[1]
    _, _, _, mixed = cls_att_forward(values, col_ref, row_ref, w_ref, vec_ref)
    out_ref[...] = (values + mm(mixed, w_ref[:, 3 * features :]) + vec_ref[2:3, :]).astype(BF)


def cls_att_bwd_kernel(weights_too, h_ref, g_ref, pos_ref, col_ref, row_ref, w_ref, vec_ref, *refs):
    values = lifted_rows(h_ref, pos_ref, vec_ref)
    features = values.shape[1]
    u, triple, probs, mixed = cls_att_forward(values, col_ref, row_ref, w_ref, vec_ref)
    b = g_ref[...]
    da = mm(b, w_ref[:, 3 * features :], NT).astype(BF)
    dqs, dks, dvs = [], [], []
    for pair in range(features // 128):
        lanes = slice(pair * 128, (pair + 1) * 128)
        q2 = two_heads(triple[:, lanes])
        k = triple[:, features + pair * 128 : features + (pair + 1) * 128]
        v = triple[:, 2 * features + pair * 128 : 2 * features + (pair + 1) * 128]
        da2 = two_heads(da[:, lanes])
        y = probs[pair]
        dy = mm(da2, v, NT)
        ds = (y * (dy - jnp.sum(dy * y, -1, keepdims=True))).astype(BF)
        dvs.append(mm(y.astype(BF), da2, TN).astype(BF))
        dqs.append((join_heads(mm(ds, k)) * SCORE_SCALE).astype(BF))
        dks.append((mm(ds, q2, TN) * SCORE_SCALE).astype(BF))
    dtriple = jnp.concatenate(dqs + dks + dvs, 1)
    du = mm(dtriple, w_ref[:, : 3 * features], NT)
    back, gain = norm_back(values, du, vec_ref)
    grad = b.astype(F32)
    total = grad + back
    if weights_too:
        small_ref, dw_ref = refs

        @pl.when(pl.program_id(0) == 0)
        def _():
            small_ref[...] = jnp.zeros_like(small_ref)
            dw_ref[...] = jnp.zeros_like(dw_ref)

        small_ref[0:1, :] += column_sum(gain)
        small_ref[1:2, :] += column_sum(du)
        small_ref[2:3, :] += column_sum(grad)
        pos = pos_ref[...]
        for p in range(SEGS):
            small_ref[3 + p : 4 + p, :] += column_sum(jnp.where(pos == p, total, 0.0))
        for part in range(3):
            span = slice(part * features, (part + 1) * features)
            dw_ref[:, span] += mm(u, dtriple[:, span], TN)
        dw_ref[:, 3 * features :] += mm(mixed, b, TN)
    else:
        (out_ref,) = refs
        out_ref[...] = total.astype(BF)


def att_place_kernel(first_ref, second_ref, out_ref):
    half = first_ref.shape[2] // 2
    part = half // 4
    for core, ref in enumerate((first_ref, second_ref)):
        for quarter in range(4):
            rows = slice(quarter * 2 * part, (quarter + 1) * 2 * part)
            for kind in range(2):
                out_ref[rows, kind * 2 * half + core * half : kind * 2 * half + (core + 1) * half] = ref[
                    quarter, : 2 * part, kind * half : (kind + 1) * half
                ].astype(F32)
            for side in range(2):
                out_ref[
                    side * half + quarter * part : side * half + (quarter + 1) * part,
                    4 * half + core * half : 4 * half + (core + 1) * half,
                ] = ref[quarter, 2 * part : 3 * part, side * half : (side + 1) * half].astype(F32)
            out_ref[core * half + quarter * part : core * half + (quarter + 1) * part, 6 * half :] = ref[
                quarter, 3 * part :, :
            ].astype(F32)


VMEM = pl.BlockSpec(memory_space=pltpu.VMEM)
LIMIT = 50 * 2**20


def call(kernel, out_shapes, args, scratch=(), flops=0, moved=0, alias=None):
    return pl.pallas_call(
        kernel,
        out_shape=[jax.ShapeDtypeStruct(*shape) for shape in out_shapes],
        in_specs=[VMEM] * len(args),
        out_specs=[VMEM] * len(out_shapes),
        scratch_shapes=list(scratch),
        compiler_params=pltpu.CompilerParams(vmem_limit_bytes=LIMIT),
        cost_estimate=pl.CostEstimate(flops=int(flops), bytes_accessed=int(moved), transcendentals=0),
        input_output_aliases=alias or {},
    )(*args)


def cls_mlp(rows, grads, wide_w, down_w, vector, main=None):
    count, features = rows.shape
    hidden = wide_w.shape[1]
    tile = features
    whole = lambda shape: pl.BlockSpec(shape, lambda j: (0,) * len(shape))
    wide_block = pl.BlockSpec((features, tile), lambda j: (0, j))
    down_block = pl.BlockSpec((tile, features), lambda j: (j, 0))
    in_specs = [whole(rows.shape), whole(grads.shape), wide_block, down_block, whole(vector.shape)]
    args = [rows, grads, wide_w, down_w, vector]
    if main is None:
        out_shape = [jax.ShapeDtypeStruct(rows.shape, BF)] * 2
        out_specs = [whole(rows.shape)] * 2
    else:
        in_specs += [wide_block, down_block]
        args += list(main)
        out_shape = [
            jax.ShapeDtypeStruct(vector.shape, F32),
            jax.ShapeDtypeStruct(wide_w.shape, F32),
            jax.ShapeDtypeStruct(down_w.shape, F32),
        ]
        out_specs = [whole(vector.shape), wide_block, down_block]
    return pl.pallas_call(
        partial(cls_mlp_kernel, main is not None),
        grid=(hidden // tile,),
        in_specs=in_specs,
        out_specs=out_specs,
        out_shape=out_shape,
        scratch_shapes=[
            pltpu.VMEM((count, features), BF),
            pltpu.VMEM((count, features), F32),
            pltpu.VMEM((count, features), F32),
        ],
        compiler_params=pltpu.CompilerParams(vmem_limit_bytes=LIMIT),
    )(*args)


def cls_att_weights(rows, grads, layout, wide_w, vector):
    count, features = rows.shape
    block = min(count, 128)
    by_row = lambda width: pl.BlockSpec((block, width), lambda i: (i, 0))
    whole = lambda shape: pl.BlockSpec(shape, lambda i: (0,) * len(shape))
    return pl.pallas_call(
        partial(cls_att_bwd_kernel, True),
        grid=(count // block,),
        in_specs=[
            by_row(features), by_row(features), by_row(1), by_row(1),
            pl.BlockSpec((1, block), lambda i: (0, i)), whole(wide_w.shape), whole(vector.shape),
        ],
        out_specs=[whole(vector.shape), whole(wide_w.shape)],
        out_shape=[jax.ShapeDtypeStruct(vector.shape, F32), jax.ShapeDtypeStruct(wide_w.shape, F32)],
        compiler_params=pltpu.CompilerParams(vmem_limit_bytes=LIMIT),
    )(rows, grads, *layout, wide_w, vector)


def documents(counts):
    ends = jnp.cumsum(counts, -1)
    places = jnp.arange(SEGS, dtype=jnp.int32)
    doc = jnp.sum((places[:, None] >= ends[..., None, :]).astype(jnp.int32), -1)
    slots = jnp.arange(counts.shape[-1], dtype=jnp.int32)
    first = jnp.sum(jnp.where(doc[..., None] == slots, (ends - counts)[..., None, :], 0), -1)
    return doc, places - first


def row_layout(counts):
    doc, pos = documents(counts)
    packs = counts.shape[0]
    label = doc + jnp.arange(packs, dtype=jnp.int32)[:, None] * (counts.shape[1] + 1)
    return pos.reshape(-1, 1), label.reshape(-1, 1), label.reshape(1, -1)


def local(inputs, cotangent, wide, down, vectors, seg_counts):
    sections = lax.axis_size("section")
    section = lax.axis_index("section")
    core = lax.axis_index("dp") % 2
    rows, features = inputs.shape[1:]
    hidden = wide.shape[2]
    half, span = features // 2, hidden // 2
    wide_w, down_w, vector = wide[0], down[0], vectors[0]
    x, cot = inputs[0], cotangent[0]

    x_sib = swap_core(x)
    att_place = ring_position(ATT_RINGS, section, core)
    mlp_place = ring_position(MLP_RINGS, section, core)
    att_parts = [
        lax.dynamic_slice(wide_w, (0, k * features + core * half), (features, half)) for k in range(3)
    ] + [lax.dynamic_slice(wide_w, (core * half, 3 * features), (half, features))]
    wq, wk, wv, wo = broadcast(att_parts, ATT_RINGS, att_place)
    near = [swap_section(vector, bits) for bits in (1, 2, 3)]
    every_vector = jnp.stack([vector] + near)
    avec, mvec = pick(every_vector, section), pick(every_vector, section ^ 1)
    chunk = features
    mlp_parts = []
    for c in range(span // chunk):
        mlp_parts.append(lax.dynamic_slice(wide_w, (0, core * span + c * chunk), (features, chunk)))
        mlp_parts.append(lax.dynamic_slice(down_w, (core * span + c * chunk, 0), (chunk, features)))
    mlp_weights = broadcast(mlp_parts, MLP_RINGS, mlp_place)

    is_cls = (jnp.arange(rows) % SEG == 0)[:, None]
    plain_cot = jnp.where(is_cls, jnp.zeros_like(cot), cot)
    plain_sib = swap_core(plain_cot)
    plain_both = jnp.concatenate([plain_cot, plain_sib], 0)

    flops = 2 * 2 * rows * features * half * 4
    q, k, v, a, partial_out = call(
        att_fwd_kernel,
        [((2 * rows, half), BF)] * 4 + [((2 * rows, features), BF)],
        [x, x_sib, wq, wk, wv, wo, avec],
        [pltpu.VMEM((2 * rows, features), BF)],
        flops * 1.3,
        8 * 2**20,
    )
    partial_sib = swap_core(partial_out)
    h1, u1 = call(
        att_join_kernel,
        [((2 * rows, features), BF)] * 2,
        [x, x_sib, partial_out, partial_sib, avec, mvec],
        moved=8 * 2**20,
    )

    grid = lambda values: values.reshape(rows // SEG, SEG, features)
    count = sections * (rows // SEG)

    def collect(mine, owner):
        arrived = [
            permute(mine, lambda s, r: (owner, r), lambda s, r: s == owner ^ bits) for bits in (1, 2, 3)
        ]
        ordered = [None] * 4
        ordered[owner] = mine
        for bits, value in zip((1, 2, 3), arrived):
            ordered[owner ^ bits] = value
        return jnp.concatenate(ordered, 0)

    def spread(all_rows, owner):
        split = all_rows.reshape(sections, rows // SEG, features)
        arrived = [
            permute(split[owner ^ bits], lambda s, r: (owner ^ bits, r), lambda s, r: s == owner) for bits in (1, 2, 3)
        ]
        return jnp.where(section == owner, split[owner], arrived[0] + arrived[1] + arrived[2])

    def hop(all_rows, start, end):
        return permute(all_rows, lambda s, r: (end, r), lambda s, r: s == start)

    def on(column, run, outs):
        return lax.cond(section == column, lambda: list(run()), lambda: [jnp.zeros((count, features), BF)] * outs)

    counts_here = seg_counts[0]
    layout = row_layout(counts_here)
    cot_cls = collect(grid(cot)[:, 0], 3)
    cls1 = collect(grid(h1[:rows])[:, 0], 1)
    cls2, _ = on(1, lambda: cls_mlp(cls1, jnp.zeros_like(cls1), wide_w, down_w, vector), 2)
    cls2_at2 = hop(cls2, 1, 2)
    cls3 = on(2, lambda: call(cls_att_fwd_kernel, [((count, features), BF)], [cls2_at2, *layout, wide_w, vector]), 1)[0]
    cls3_at3 = hop(cls3, 2, 3)
    cls4, dcls3 = on(3, lambda: cls_mlp(cls3_at3, cot_cls, wide_w, down_w, vector), 2)
    dcls3_at2 = hop(dcls3, 3, 2)
    dcls2 = on(
        2,
        lambda: call(
            partial(cls_att_bwd_kernel, False), [((count, features), BF)], [cls2_at2, dcls3_at2, *layout, wide_w, vector]
        ),
        1,
    )[0]
    dcls2_at1 = hop(dcls2, 2, 1)
    _, dcls1 = on(1, lambda: cls_mlp(cls1, dcls2_at1, wide_w, down_w, vector), 2)
    dcls1_own = spread(dcls1, 1)
    cls4_own = spread(cls4, 3)

    flops = 2 * 2 * rows * features * chunk * 6
    mlp_grads = []
    out_acc = du_acc = None
    shapes = [((2 * rows, features), F32)] * 2 + [((4, 2 * features // 4, features), BF)]
    for c in range(span // chunk):
        args = [u1, plain_both, mlp_weights[2 * c], mlp_weights[2 * c + 1]]
        if c:
            args += [out_acc, du_acc]
        out_acc, du_acc, grad = call(
            partial(mlp_kernel, c == 0, 256),
            shapes,
            args,
            flops=flops,
            moved=12 * 2**20,
        )
        mlp_grads.append(grad)
    out_sib = swap_core(out_acc[rows:].astype(BF))
    du_sib = swap_core(du_acc[rows:].astype(BF))
    h2, dh1, mlp_small = call(
        mlp_done_kernel,
        [((rows, features), BF)] * 2 + [((8, features), F32)],
        [h1[:rows], plain_cot, out_acc[:rows], out_sib, du_acc[:rows], du_sib, mvec],
        moved=8 * 2**20,
    )
    place = lambda values, heads: lax.dynamic_update_slice(grid(values), heads[:, None], (0, 0, 0)).reshape(rows, features)
    layer_out = place(h2, cls4_own)
    dh1 = place(dh1, dcls1_own)

    dh1_sib = swap_core(dh1)
    att_grad, du0_own, du0_sib = call(
        att_bwd_kernel,
        [((4, features // 2, features), BF), ((rows, features), F32), ((rows, features), BF)],
        [x, x_sib, dh1, dh1_sib, q, k, v, a, wq, wk, wv, wo, avec],
        [pltpu.VMEM((2 * rows, features), BF)] + [pltpu.VMEM((2 * rows, half), BF)] * 4,
        2 * 2 * rows * features * half * 8 * 1.3,
        16 * 2**20,
    )
    input_grad, att_small = call(
        att_done_kernel,
        [((rows, features), BF), ((8, features), F32)],
        [x, dh1, du0_own, swap_core(du0_sib), avec],
        moved=6 * 2**20,
    )

    mlp_total = [reduce_pieces(grad, section, 1) for grad in mlp_grads]
    att_total = reduce_pieces(att_grad, section, 0)
    small = jnp.concatenate([att_small, mlp_small], 0)
    bits = 1
    while bits < lax.axis_size("dp"):
        small = small + swap_dp(small, bits)
        bits *= 2
    small = small + swap_section(small, 1)
    small = small + swap_section(small, 2)

    def both_cores(mine):
        other = swap_core(mine)
        return jnp.where(core == 0, mine, other), jnp.where(core == 0, other, mine)

    att_first, att_second = both_cores(att_total)
    mlp_halves = [both_cores(total) for total in mlp_total]

    mine_in = jnp.where(section == 1, cls1, jnp.where(section == 2, cls2_at2, cls3_at3))
    mine_grad = jnp.where(section == 1, dcls2_at1, jnp.where(section == 2, dcls3_at2, cot_cls))
    all_in = lax.all_gather(mine_in, "dp", axis=0, tiled=True)
    all_grad = lax.all_gather(mine_grad, "dp", axis=0, tiled=True)
    all_counts = lax.all_gather(counts_here, "dp", axis=0, tiled=True)
    all_layout = row_layout(all_counts)
    small_pad = jnp.zeros((vector.shape[0] - 3, features), F32)
    zero_down = lambda: jnp.zeros(down_w.shape, F32)

    def first_sums():
        (wide_sum,) = call(att_place_kernel, [(wide_w.shape, F32)], [att_first, att_second])
        return jnp.concatenate([small[0:3], small_pad], 0), wide_sum, zero_down()

    def second_sums():
        rows_w, rows_v = [], []
        for c in range(2):
            for halves in mlp_halves:
                piece = halves[c]
                rows_w.append(piece[:, : features // 4].reshape(features, chunk))
                rows_v.append(piece[:, features // 4 :].reshape(chunk, features))
        main = (jnp.concatenate(rows_w, 1), jnp.concatenate(rows_v, 0))
        cls_small, wide_sum, down_sum = cls_mlp(all_in, all_grad, wide_w, down_w, vector, main)
        return cls_small + jnp.concatenate([small[8:11], small_pad], 0), wide_sum, down_sum

    def third_sums():
        cls_small, wide_sum = cls_att_weights(all_in, all_grad, all_layout, wide_w, vector)
        return cls_small, wide_sum, zero_down()

    def fourth_sums():
        main = (jnp.zeros(wide_w.shape, BF), jnp.zeros(down_w.shape, BF))
        return tuple(cls_mlp(all_in, all_grad, wide_w, down_w, vector, main))

    vector_sum, wide_sum, down_sum = lax.switch(section, [first_sums, second_sums, third_sums, fourth_sums])
    return layer_out[None], input_grad[None], wide_sum[None], down_sum[None], vector_sum[None]


def solution(mesh):
    return jax.shard_map(
        local,
        mesh=mesh,
        in_specs=(
            P("section", "dp", None),
            P("section", "dp", None),
            P("section", None, None),
            P("section", None, None),
            P("section", None, None),
            P("dp", None, None),
        ),
        out_specs=(
            P("section", "dp", None),
            P("section", "dp", None),
            P("section", None, None),
            P("section", None, None),
            P("section", None, None),
        ),
        check_vma=False,
    )
```

```python
from functools import partial

import jax
import jax.numpy as jnp
from jax import lax
from jax.experimental import pallas as pl
from jax.experimental.pallas import tpu as pltpu
from jax.sharding import PartitionSpec as P

HEADS = 12
SEG = 128
SEGS = 4
EPSILON = 1e-05
SCORE_SCALE = 0.125
MASKED = -1e30
AXES = ("section", "dp")
BF = jnp.bfloat16
F32 = jnp.float32

NN = (((1,), (0,)), ((), ()))
NT = (((1,), (1,)), ((), ()))
TN = (((0,), (0,)), ((), ()))

GELU_A = 0.7978845608028654
GELU_B = 0.044715

ATT_WAYS = ((0, 1, 2, 3), (0, 2, 1, 3))
MLP_WAYS = ((1, 0, 3, 2), (1, 3, 0, 2))


def mm(left, right, dims=NN):
    return lax.dot_general(left, right, dims, preferred_element_type=F32)


def permute(shard, move, keep=lambda s, r: True):
    sections, replicas = lax.axis_size("section"), lax.axis_size("dp")
    pairs = []
    for s in range(sections):
        for r in range(replicas):
            if keep(s, r):
                t, q = move(s, r)
                pairs.append((s * replicas + r, t * replicas + q))
    return lax.ppermute(shard, AXES, pairs)


def swap_core(shard):
    return permute(shard, lambda s, r: (s, r ^ 1))


def swap_section(shard, bits):
    return permute(shard, lambda s, r: (s ^ bits, r))


def swap_dp(shard, bits):
    return permute(shard, lambda s, r: (s, r ^ bits))


def send(values, ways, start, end):
    return permute(values, lambda s, r: (ways[r & 1][end], r), lambda s, r: ways[r & 1][start] == s)


def after(value, *marks):
    return lax.optimization_barrier((value, marks))[0]


def place_of(ways, section, core):
    position = jnp.int32(0)
    for c in range(2):
        for k, s in enumerate(ways[c]):
            position = jnp.where((section == s) & (core == c), k, position)
    return position


def pick(stack, index):
    return lax.dynamic_index_in_dim(stack, index, 0, keepdims=False)


def section_sum(grad, section, *marks):
    own = pick(grad, section).astype(F32)
    first, second, third = after([swap_section(pick(grad, section ^ bits), bits) for bits in (1, 2, 3)], *marks)
    return (own + first.astype(F32) + second.astype(F32) + third.astype(F32)).astype(BF)


def dp_sum(value, bits):
    while bits < lax.axis_size("dp"):
        value = pair_sum(value, swap_dp(value, bits))
        bits *= 2
    return value


def pair_sum(mine, other):
    return (mine.astype(F32) + other.astype(F32)).astype(BF)


def to_column(value, owner):
    arrived = [permute(value, lambda s, r: (owner, r), lambda s, r: s == owner ^ bits) for bits in (1, 2, 3)]
    ordered = [None] * 4
    ordered[owner] = value
    for bits, other in zip((1, 2, 3), arrived):
        ordered[owner ^ bits] = other
    return ordered


def fetch(sources, targets, sems):
    return [pltpu.make_async_copy(source, target, sems.at[i]) for i, (source, target) in enumerate(zip(sources, targets))]


def norm_parts(values):
    center = values - jnp.mean(values, -1, keepdims=True)
    spread = jnp.mean(center * center, -1, keepdims=True)
    scale = lax.rsqrt(spread + EPSILON)
    return center * scale, scale


def norm_rows(values, vec_ref):
    hat, _ = norm_parts(values)
    return hat * vec_ref[0:1, :] + vec_ref[1:2, :]


def norm_back(values, grad_normed, vec_ref):
    hat, scale = norm_parts(values)
    inner = grad_normed * vec_ref[0:1, :]
    first = jnp.mean(inner, -1, keepdims=True)
    second = jnp.mean(inner * hat, -1, keepdims=True)
    return scale * (inner - first - hat * second), grad_normed * hat


def column_sum(values):
    return jnp.sum(values, 0, keepdims=True)


def gelu_parts(hidden):
    square = hidden * hidden
    inner = GELU_A * hidden * (1.0 + GELU_B * square)
    t = jnp.tanh(inner)
    half = 0.5 * (1.0 + t)
    slope = half + 0.5 * hidden * (1.0 - t * t) * (GELU_A * (1.0 + 3.0 * GELU_B * square))
    return hidden * half, slope


def two_heads(pair):
    low = lax.broadcasted_iota(jnp.int32, pair.shape, 1) < 64
    zero = jnp.zeros_like(pair)
    return jnp.concatenate([jnp.where(low, pair, zero), jnp.where(low, zero, pair)], 0)


def join_heads(both):
    rows = both.shape[0] // 2
    low = lax.broadcasted_iota(jnp.int32, (rows, both.shape[1]), 1) < 64
    return jnp.where(low, both[:rows], both[rows:])


def softmax_rows(scores):
    powers = jnp.exp(scores - jnp.max(scores, -1, keepdims=True))
    return powers / jnp.sum(powers, -1, keepdims=True)


def softmax_columns(scores):
    powers = jnp.exp(scores - jnp.max(scores, 0, keepdims=True))
    return powers * (1.0 / jnp.sum(powers, 0, keepdims=True))


def head_pairs(q, k, v, out):
    for seg in range(q.shape[0] // SEG):
        at = slice(seg * SEG, (seg + 1) * SEG)
        mixed = []
        for pair in range(q.shape[1] // 128):
            lanes = slice(pair * 128, (pair + 1) * 128)
            probs = softmax_columns(mm(k[at, lanes], two_heads(q[at, lanes]), NT) * SCORE_SCALE)
            mixed.append(join_heads(mm(probs.astype(BF), v[at, lanes], TN)).astype(BF))
        out.append(jnp.concatenate(mixed, 1))


def att_fwd_kernel(place_ref, own_ref, sib_ref, vec_ref, *refs):
    choices, (triple_ref, a_ref, give_ref, keep_ref, wt, wo, sems) = refs[:4], refs[4:]
    rows, features = own_ref.shape
    half = a_ref.shape[1]
    top = pl.ds(0, features)

    def load(source):
        return fetch(
            [
                source.at[top, :],
                source.at[pl.ds(features, half), pl.ds(0, half)],
                source.at[pl.ds(features, half), pl.ds(half, half)],
                source.at[pl.ds(features + half, half), :],
            ],
            [
                wt.at[:, pl.ds(0, features)],
                wt.at[pl.ds(0, half), pl.ds(features, half)],
                wt.at[pl.ds(half, half), pl.ds(features, half)],
                wo,
            ],
            sems,
        )

    for k, choice in enumerate(choices):

        @pl.when(place_ref[0] == k)
        def _():
            for copy in load(choice):
                copy.start()

    waits = load(choices[0])
    for pack, (ref, out) in enumerate(((sib_ref, give_ref), (own_ref, keep_ref))):
        span = slice((1 - pack) * rows, (2 - pack) * rows)
        u = norm_rows(ref[...].astype(F32), vec_ref).astype(BF)
        if pack == 0:
            for wait in waits:
                wait.wait()
        triple = mm(u, wt[...]).astype(BF)
        triple_ref[span, :] = triple
        mixed = []
        head_pairs(triple[:, :half], triple[:, half : 2 * half], triple[:, 2 * half :], mixed)
        a = jnp.concatenate(mixed, 0)
        a_ref[span, :] = a
        out[...] = mm(a, wo[...]).astype(BF)


def att_bwd_kernel(
    own_ref, sib_ref, gown_ref, gsib_ref, triple_ref, a_ref, wt, wo, vec_ref, small_ref,
    grad_ref, duown_ref, dusib_ref, u_ref, dt_ref,
):
    rows = own_ref.shape[0]
    half = a_ref.shape[1]
    part = half // 4
    gain = shift = 0.0
    for pack, (x_ref, g_ref, out) in enumerate(((own_ref, gown_ref, duown_ref), (sib_ref, gsib_ref, dusib_ref))):
        span = slice(pack * rows, (pack + 1) * rows)
        hat, _ = norm_parts(x_ref[...].astype(F32))
        u_ref[span, :] = (hat * vec_ref[0:1, :] + vec_ref[1:2, :]).astype(BF)
        da = mm(g_ref[...], wo[...], NT).astype(BF)
        for seg in range(rows // SEG):
            at = slice(seg * SEG, (seg + 1) * SEG)
            to = slice(pack * rows + seg * SEG, pack * rows + (seg + 1) * SEG)
            for pair in range(half // 128):
                lanes = [slice(kind * half + pair * 128, kind * half + (pair + 1) * 128) for kind in range(3)]
                q2, k, v = two_heads(triple_ref[to, lanes[0]]), triple_ref[to, lanes[1]], triple_ref[to, lanes[2]]
                da2 = two_heads(da[at, lanes[0]])
                probs = softmax_columns(mm(k, q2, NT) * SCORE_SCALE)
                dy = mm(v, da2, NT)
                ds = (probs * (dy - jnp.sum(dy * probs, 0, keepdims=True))).astype(BF)
                dt_ref[to, lanes[2]] = mm(probs.astype(BF), da2).astype(BF)
                dt_ref[to, lanes[0]] = (join_heads(mm(ds, k, TN)) * SCORE_SCALE).astype(BF)
                dt_ref[to, lanes[1]] = (mm(ds, q2) * SCORE_SCALE).astype(BF)
        du = mm(dt_ref[span, :], wt[...], NT)
        out[...] = du.astype(BF)
        gain = gain + column_sum(du * hat)
        shift = shift + column_sum(du)

    grad_ref[:, 4 * part :, :] = jnp.zeros((4, 16, grad_ref.shape[2]), BF)
    rest = jnp.zeros((13, grad_ref.shape[2]), F32)
    sums = [gain, shift, column_sum(gown_ref[...].astype(F32)), rest]
    grad_ref[0, 4 * part :, :] = jnp.concatenate(sums, 0).astype(BF)
    grad_ref[1, 4 * part :, :] = jnp.concatenate([small_ref[...], small_ref[...]], 0).astype(BF)
    dwo = mm(a_ref[:rows, :], gown_ref[...], TN) + mm(a_ref[rows:, :], gsib_ref[...], TN)
    dw = mm(u_ref[...], dt_ref[:, : 2 * half], TN)
    dwv = mm(u_ref[...], dt_ref[:, 2 * half :], TN)
    for quarter in range(4):
        grad_ref[quarter, : 2 * part, :] = dw[quarter * 2 * part : (quarter + 1) * 2 * part, :].astype(BF)
        for side in range(2):
            grad_ref[quarter, 2 * part : 3 * part, side * half : (side + 1) * half] = dwv[
                side * half + quarter * part : side * half + (quarter + 1) * part, :
            ].astype(BF)
        grad_ref[quarter, 3 * part : 4 * part, :] = dwo[quarter * part : (quarter + 1) * part, :].astype(BF)


def att_done_kernel(x_ref, g_ref, duown_ref, dusib_ref, vec_ref, out_ref):
    du = duown_ref[...].astype(F32) + dusib_ref[...].astype(F32)
    back, _ = norm_back(x_ref[...].astype(F32), du, vec_ref)
    out_ref[...] = (g_ref[...].astype(F32) + back).astype(BF)


def att_join_kernel(x_ref, keep_ref, core_ref, avec_ref, mvec_ref, h_ref, u_ref):
    branch = keep_ref[...].astype(F32) + core_ref[...].astype(F32)
    out = (x_ref[...].astype(F32) + branch + avec_ref[2:3, :]).astype(BF)
    h_ref[...] = out
    u_ref[...] = norm_rows(out.astype(F32), mvec_ref).astype(BF)


def mlp_kernel(last, *refs):
    if last:
        uown_ref, usib_ref, bown_ref, bsib_ref, w_ref, v_ref, dwin_ref, dvin_ref, keep_ref, give_ref, grad_ref = refs[:11]
    else:
        place_ref, uown_ref, usib_ref, bown_ref, bsib_ref, *choices = refs[:9]
        keep_ref, give_ref, dw_ref, dv_ref, w_ref, v_ref = refs[9:15]
        size = w_ref.shape[0]
        load = lambda choice: fetch(
            [choice.at[pl.ds(0, size), :], choice.at[pl.ds(size, size), :]], [w_ref, v_ref], refs[19]
        )
        for k, choice in enumerate(choices):

            @pl.when(place_ref[0] == k)
            def _():
                for copy in load(choice):
                    copy.start()

        waits = load(choices[0])
    u, b, act, dhs = refs[11:15] if last else refs[15:19]
    rows = uown_ref.shape[0]
    for pack, (ur, br, to) in enumerate(((usib_ref, bsib_ref, give_ref), (uown_ref, bown_ref, keep_ref))):
        at = slice(pack * rows, (pack + 1) * rows)
        u[at, :], b[at, :] = ur[...], br[...]
        if not last and pack == 0:
            for wait in waits:
                wait.wait()
        active, slope = gelu_parts(mm(ur[...], w_ref[...]))
        act[at, :] = active.astype(BF)
        dhs[at, :] = (mm(br[...], v_ref[...], NT) * slope).astype(BF)
        to[:rows, :] = mm(dhs[at, :], w_ref[...], NT).astype(BF)
        to[rows:, :] = mm(act[at, :], v_ref[...]).astype(BF)
    dw = mm(u[...], dhs[...], TN)
    dv = mm(act[...], b[...], TN)
    if last:
        part = dw.shape[0] // 4
        for quarter in range(4):
            at = slice(quarter * part, (quarter + 1) * part)
            grad_ref[quarter, :part, :] = (dwin_ref[at, :] + dw[at, :]).astype(BF)
            grad_ref[quarter, part:, :] = (dvin_ref[at, :] + dv[at, :]).astype(BF)
    else:
        dw_ref[...] = dw
        dv_ref[...] = dv


def mlp_done_kernel(h_ref, b_ref, keep_ref, core_ref, z_ref, vec_ref, grad_ref, small_ref):
    rows = h_ref.shape[0]
    du = keep_ref[:rows, :].astype(F32) + core_ref[:rows, :].astype(F32) + z_ref[:rows, :].astype(F32)
    grad = b_ref[...].astype(F32)
    back, gain = norm_back(h_ref[...].astype(F32), du, vec_ref)
    grad_ref[...] = (grad + back).astype(BF)
    small_ref[...] = jnp.zeros_like(small_ref)
    small_ref[0:1, :] = column_sum(gain)
    small_ref[1:2, :] = column_sum(du)
    small_ref[2:3, :] = column_sum(grad)


def cls_mlp_kernel(mode, h_ref, b_ref, w_ref, v_ref, vec_ref, *refs):
    features = w_ref.shape[0]
    forward, backward = mode in ("out", "both"), mode in ("back", "both")
    weights, factors = mode == "weights", mode == "factors"
    j = pl.program_id(0)
    if weights:
        small_ref, dw_ref, dv_ref, u_ref, out_acc, du_acc = refs
    elif factors:
        small_ref, u_ref, dh_ref, act_ref, out_acc, du_acc = refs
    else:
        out_ref, u_ref, out_acc, du_acc = refs

    @pl.when(j == 0)
    def _():
        u_ref[...] = norm_rows(h_ref[:, :features].astype(F32), vec_ref).astype(BF)
        out_acc[...] = jnp.zeros_like(out_acc)
        du_acc[...] = jnp.zeros_like(du_acc)

    u = u_ref[...]
    active, slope = gelu_parts(mm(u, w_ref[...]))
    active = active.astype(BF)
    if forward:
        out_acc[...] += mm(active, v_ref[...])
    if not forward or backward:
        b = b_ref[:, -features:] if mode == "both" else b_ref[:, :features]
        dh = (mm(b, v_ref[...], NT) * slope).astype(BF)
        du_acc[...] += mm(dh, w_ref[...], NT)
    if weights:
        dw_ref[...] = mm(u, dh, TN)
        dv_ref[...] = mm(active, b, TN)
    if factors:
        dh_ref[...] = dh
        act_ref[...] = active

    @pl.when(j == pl.num_programs(0) - 1)
    def _():
        values = h_ref[:, :features].astype(F32)
        if forward:
            out = (values + out_acc[...] + vec_ref[2:3, :]).astype(BF)
        if not forward or backward:
            grad = b.astype(F32)
            back, gain = norm_back(values, du_acc[...], vec_ref)
            back = (grad + back).astype(BF)
        if mode == "out":
            out_ref[:, :features] = out
            out_ref[:, features:] = h_ref[:, features:]
        if mode == "both":
            out_ref[:, :features] = back
            out_ref[:, features:] = out
        if mode == "back":
            out_ref[:, :features] = back
            out_ref[:, features:] = b_ref[:, features:]
        if weights or factors:
            small_ref[...] = jnp.zeros_like(small_ref)
            small_ref[0:1, :] = column_sum(gain)
            small_ref[1:2, :] = column_sum(du_acc[...])
            small_ref[2:3, :] = column_sum(grad)


def lifted_rows(h_ref, pos_ref, vec_ref):
    values = h_ref[:, : vec_ref.shape[1]].astype(F32)
    pos = pos_ref[...]
    for p in range(SEGS):
        values = values + jnp.where(pos == p, vec_ref[3 + p : 4 + p, :], 0.0)
    return values


def cls_att_forward(values, col_ref, row_ref, w_ref, vec_ref):
    features = values.shape[1]
    u = norm_rows(values, vec_ref).astype(BF)
    triple = mm(u, w_ref[:, : 3 * features]).astype(BF)
    column = jnp.concatenate([col_ref[...], col_ref[...]], 0)
    mask = column == row_ref[...]
    probs, mixed = [], []
    for pair in range(features // 128):
        lanes = slice(pair * 128, (pair + 1) * 128)
        q2 = two_heads(triple[:, lanes])
        k = triple[:, features + pair * 128 : features + (pair + 1) * 128]
        v = triple[:, 2 * features + pair * 128 : 2 * features + (pair + 1) * 128]
        scores = jnp.where(mask, mm(q2, k, NT) * SCORE_SCALE, MASKED)
        probs.append(softmax_rows(scores))
        mixed.append(join_heads(mm(probs[-1].astype(BF), v)).astype(BF))
    return u, triple, probs, jnp.concatenate(mixed, 1)


def cls_att_fwd_kernel(h_ref, pos_ref, col_ref, row_ref, w_ref, vec_ref, out_ref):
    values = lifted_rows(h_ref, pos_ref, vec_ref)
    features = values.shape[1]
    _, _, _, mixed = cls_att_forward(values, col_ref, row_ref, w_ref, vec_ref)
    out_ref[:, :features] = (values + mm(mixed, w_ref[:, 3 * features :]) + vec_ref[2:3, :]).astype(BF)
    out_ref[:, features:] = h_ref[:, features:]


def cls_att_bwd_kernel(weights_too, h_ref, g_ref, pos_ref, col_ref, row_ref, w_ref, vec_ref, *refs):
    values = lifted_rows(h_ref, pos_ref, vec_ref)
    features = values.shape[1]
    u, triple, probs, mixed = cls_att_forward(values, col_ref, row_ref, w_ref, vec_ref)
    b = g_ref[:, :features]
    da = mm(b, w_ref[:, 3 * features :], NT).astype(BF)
    dqs, dks, dvs = [], [], []
    for pair in range(features // 128):
        lanes = slice(pair * 128, (pair + 1) * 128)
        q2 = two_heads(triple[:, lanes])
        k = triple[:, features + pair * 128 : features + (pair + 1) * 128]
        v = triple[:, 2 * features + pair * 128 : 2 * features + (pair + 1) * 128]
        da2 = two_heads(da[:, lanes])
        y = probs[pair]
        dy = mm(da2, v, NT)
        ds = (y * (dy - jnp.sum(dy * y, -1, keepdims=True))).astype(BF)
        dvs.append(mm(y.astype(BF), da2, TN).astype(BF))
        dqs.append((join_heads(mm(ds, k)) * SCORE_SCALE).astype(BF))
        dks.append((mm(ds, q2, TN) * SCORE_SCALE).astype(BF))
    dtriple = jnp.concatenate(dqs + dks + dvs, 1)
    du = mm(dtriple, w_ref[:, : 3 * features], NT)
    back, gain = norm_back(values, du, vec_ref)
    grad = b.astype(F32)
    total = grad + back
    if weights_too:
        small_ref, dw_ref = refs

        @pl.when(pl.program_id(0) == 0)
        def _():
            small_ref[...] = jnp.zeros_like(small_ref)
            dw_ref[...] = jnp.zeros_like(dw_ref)

        small_ref[0:1, :] += column_sum(gain)
        small_ref[1:2, :] += column_sum(du)
        small_ref[2:3, :] += column_sum(grad)
        pos = pos_ref[...]
        for p in range(SEGS):
            small_ref[3 + p : 4 + p, :] += column_sum(jnp.where(pos == p, total, 0.0))
        for part in range(3):
            span = slice(part * features, (part + 1) * features)
            dw_ref[:, span] += mm(u, dtriple[:, span], TN)
        dw_ref[:, 3 * features :] += mm(mixed, b, TN)
    else:
        (out_ref,) = refs
        out_ref[:, :features] = total.astype(BF)
        out_ref[:, features:] = g_ref[:, features:]


def parts_kernel(who_ref, wide_ref, down_ref, att_ref, mlp_ref, sems):
    features = down_ref.shape[1]
    half = features // 2
    lane = lambda kind: pl.ds(pl.multiple_of(kind * features + who_ref[1] * half, 128), half)
    quarter = pl.ds(pl.multiple_of(who_ref[2] * features, features), features)
    copies = fetch(
        [
            wide_ref.at[:, lane(0)],
            wide_ref.at[:, lane(1)],
            wide_ref.at[pl.ds(0, half), lane(2)],
            wide_ref.at[pl.ds(half, half), lane(2)],
            wide_ref.at[pl.ds(pl.multiple_of(who_ref[1] * half, half), half), pl.ds(3 * features, features)],
            wide_ref.at[:, quarter],
            down_ref.at[quarter, :],
        ],
        [
            att_ref.at[pl.ds(0, features), pl.ds(0, half)],
            att_ref.at[pl.ds(0, features), pl.ds(half, half)],
            att_ref.at[pl.ds(features, half), pl.ds(0, half)],
            att_ref.at[pl.ds(features, half), pl.ds(half, half)],
            att_ref.at[pl.ds(features + half, half), :],
            mlp_ref.at[pl.ds(0, features), :],
            mlp_ref.at[pl.ds(features, features), :],
        ],
        sems,
    )
    for copy in copies:
        copy.start()
    for copy in copies:
        copy.wait()


def att_place_kernel(who_ref, own_ref, other_ref, _, out_ref, held, block, sems, out_sems):
    half = held.shape[1]
    part = half // 4

    def fill(quarter, pieces):
        for core, ref in enumerate(pieces):
            for kind in range(2):
                lanes = slice((2 * kind + core) * half, (2 * kind + core + 1) * half)
                block[quarter, :, lanes] = ref[quarter, : 2 * part, kind * half : (kind + 1) * half].astype(F32)
            for low in range(2):
                row = quarter * 2 * part + low * part
                side, inside = row // half, row % half // part
                block[quarter, low * part : (low + 1) * part, (4 + core) * half : (5 + core) * half] = ref[
                    inside, 2 * part : 3 * part, side * half : (side + 1) * half
                ].astype(F32)
        for low in range(2):
            row = quarter * 2 * part + low * part
            block[quarter, low * part : (low + 1) * part, 6 * half :] = pieces[row // half][
                row % half // part, 3 * part :, :
            ].astype(F32)

    @pl.when(who_ref[0] == 0)
    def _():
        waits = fetch([own_ref, other_ref], [held.at[0:4], held.at[4:8]], sems)
        for copy in waits:
            copy.start()
        for copy in waits:
            copy.wait()
        copies = []
        for quarter in range(4):

            @pl.when(who_ref[1] == 0)
            def _():
                fill(quarter, (held.at[0:4], held.at[4:8]))

            @pl.when(who_ref[1] == 1)
            def _():
                fill(quarter, (held.at[4:8], held.at[0:4]))

            rows = pl.ds(quarter * 2 * part, 2 * part)
            copies.append(pltpu.make_async_copy(block.at[quarter], out_ref.at[rows, :], out_sems.at[quarter]))
            copies[-1].start()
        for copy in copies:
            copy.wait()


def mlp_place_kernel(
    who_ref, u_ref, b_ref, dh_ref, act_ref, own_ref, other_ref, _, __, wide_ref, down_ref, held, dws, dvs, sems, out_sems
):
    size = dws.shape[1]
    part = size // 4

    @pl.when(who_ref[0] == 1)
    def _():
        waits = fetch([own_ref, other_ref], [held.at[0], held.at[1]], sems)
        for copy in waits:
            copy.start()
        copies = []
        for relative in range(4):
            at = pl.ds(pl.multiple_of((who_ref[2] ^ relative) * size, size), size)
            dws[relative] = mm(u_ref[...], dh_ref[:, at], TN)
            dvs[relative] = mm(act_ref[:, at], b_ref[...], TN)
            if relative < 2:
                waits[relative].wait()
            for quarter in range(4):
                piece = held.at[relative % 2, quarter, relative // 2]
                rows = slice(quarter * part, (quarter + 1) * part)
                dws[relative, rows, :] += piece[:part, :].astype(F32)
                dvs[relative, rows, :] += piece[part:, :].astype(F32)
            for k, (source, target) in enumerate(
                ((dws.at[relative], wide_ref.at[:, at]), (dvs.at[relative], down_ref.at[at, :]))
            ):
                copies.append(pltpu.make_async_copy(source, target, out_sems.at[2 * relative + k]))
                copies[-1].start()
        for copy in copies:
            copy.wait()


VMEM = pl.BlockSpec(memory_space=pltpu.VMEM)
SMEM = pl.BlockSpec(memory_space=pltpu.SMEM)
ANY = pl.BlockSpec(memory_space=pl.ANY)
LIMIT = 58 * 2**20


def whole(shape):
    return pl.BlockSpec(shape, lambda i: (0,) * len(shape))


def estimate(microseconds):
    return pl.CostEstimate(flops=int(microseconds * 1.1e9), bytes_accessed=0, transcendentals=0)


def call(kernel, out_shapes, args, scratch=(), anywhere=0, scalars=0, cost=1):
    return pl.pallas_call(
        kernel,
        grid=(1,),
        out_shape=[jax.ShapeDtypeStruct(*shape) for shape in out_shapes],
        in_specs=[SMEM] * scalars
        + [whole(arg.shape) for arg in args[scalars : len(args) - anywhere]]
        + [ANY] * anywhere,
        out_specs=[whole(shape[0]) for shape in out_shapes],
        scratch_shapes=list(scratch),
        compiler_params=pltpu.CompilerParams(vmem_limit_bytes=LIMIT),
        cost_estimate=estimate(cost),
    )(*args)


def fence_kernel(in_ref, out_ref):
    out_ref[...] = in_ref[...]


def fence(microseconds, *marks):
    token = after(jnp.zeros((8, 128), F32), *marks)
    return call(fence_kernel, [(token.shape, F32)], [token], cost=microseconds)[0]


def blank(shape):
    return pl.pallas_call(lambda out_ref: None, out_shape=jax.ShapeDtypeStruct(shape, F32), out_specs=ANY)()


def cls_mlp(mode, rows, grads, wide_w, down_w, vector):
    count = rows.shape[0]
    features, hidden = wide_w.shape
    tile = features
    wide_block = pl.BlockSpec((features, tile), lambda j: (0, j))
    down_block = pl.BlockSpec((tile, features), lambda j: (j, 0))
    sums = jax.ShapeDtypeStruct(vector.shape, F32)
    scratch = [pltpu.VMEM((count, features), BF)] + [pltpu.VMEM((count, features), F32)] * 2
    if mode == "weights":
        out_shape = [sums, jax.ShapeDtypeStruct(wide_w.shape, F32), jax.ShapeDtypeStruct(down_w.shape, F32)]
        out_specs = [whole(vector.shape), wide_block, down_block]
    elif mode == "factors":
        out_shape = [sums, jax.ShapeDtypeStruct((count, features), BF)] + [jax.ShapeDtypeStruct((count, hidden), BF)] * 2
        out_specs = [whole(vector.shape), whole((count, features))] + [pl.BlockSpec((count, tile), lambda j: (0, j))] * 2
        scratch = scratch[1:]
    else:
        out_shape = [jax.ShapeDtypeStruct(rows.shape, BF)]
        out_specs = [whole(rows.shape)]
    return pl.pallas_call(
        partial(cls_mlp_kernel, mode),
        grid=(hidden // tile,),
        in_specs=[whole(rows.shape), whole(grads.shape), wide_block, down_block, whole(vector.shape)],
        out_specs=out_specs,
        out_shape=out_shape,
        scratch_shapes=scratch,
        compiler_params=pltpu.CompilerParams(vmem_limit_bytes=LIMIT),
    )(rows, grads, wide_w, down_w, vector)


def cls_att_weights(rows, grads, layout, wide_w, vector):
    count, features = rows.shape
    block = min(count, 128)
    by_row = lambda width: pl.BlockSpec((block, width), lambda i: (i, 0))
    return pl.pallas_call(
        partial(cls_att_bwd_kernel, True),
        grid=(count // block,),
        in_specs=[
            by_row(features), by_row(features), by_row(1), by_row(1),
            pl.BlockSpec((1, block), lambda i: (0, i)), whole(wide_w.shape), whole(vector.shape),
        ],
        out_specs=[whole(vector.shape), whole(wide_w.shape)],
        out_shape=[jax.ShapeDtypeStruct(vector.shape, F32), jax.ShapeDtypeStruct(wide_w.shape, F32)],
        compiler_params=pltpu.CompilerParams(vmem_limit_bytes=LIMIT),
    )(rows, grads, *layout, wide_w, vector)


def documents(counts):
    ends = jnp.cumsum(counts, -1)
    places = jnp.arange(SEGS, dtype=jnp.int32)
    doc = jnp.sum((places[:, None] >= ends[..., None, :]).astype(jnp.int32), -1)
    slots = jnp.arange(counts.shape[-1], dtype=jnp.int32)
    first = jnp.sum(jnp.where(doc[..., None] == slots, (ends - counts)[..., None, :], 0), -1)
    return doc, places - first


def row_layout(counts):
    doc, pos = documents(counts)
    packs = counts.shape[0]
    label = doc + jnp.arange(packs, dtype=jnp.int32)[:, None] * (counts.shape[1] + 1)
    return pos.reshape(-1, 1), label.reshape(-1, 1), label.reshape(1, -1)


def local(inputs, cotangent, wide, down, vectors, seg_counts):
    sections = lax.axis_size("section")
    replicas = lax.axis_size("dp")
    section = lax.axis_index("section")
    replica = lax.axis_index("dp")
    core, side = replica % 2, replica // 2 % 2
    rows, features = inputs.shape[1:]
    half = features // 2
    wide_w, down_w, vector = wide[0], down[0], vectors[0]
    x, cot = inputs[0], cotangent[0]

    fourth = 2 * side + core
    who = jnp.stack([section, core, fourth]).astype(jnp.int32)
    att_part, mlp_part = pl.pallas_call(
        parts_kernel,
        out_shape=[jax.ShapeDtypeStruct((2 * features, features), BF)] * 2,
        in_specs=[SMEM, ANY, ANY],
        out_specs=[VMEM, VMEM],
        scratch_shapes=[pltpu.SemaphoreType.DMA((7,))],
        compiler_params=pltpu.CompilerParams(vmem_limit_bytes=LIMIT),
    )(who, wide_w, down_w)
    att_first = send(att_part, ATT_WAYS, 0, 1)
    near = [swap_section(vector, bits) for bits in (1, 2, 3)]
    mlp_first = send(mlp_part, MLP_WAYS, 0, 1)
    x_sib = swap_core(x)
    every_vector = jnp.stack([vector] + near)
    avec, mvec = pick(every_vector, section), pick(every_vector, section ^ 1)
    att_second = send(after(att_part, every_vector, mlp_first), ATT_WAYS, 0, 2)
    att_last = send(att_first, ATT_WAYS, 1, 3)
    mlp_second = send(after(mlp_part, every_vector, att_first, x_sib), MLP_WAYS, 0, 2)
    mlp_last = send(after(mlp_first, att_first), MLP_WAYS, 1, 3)

    grid = lambda values: values.reshape(-1, SEG, features)
    heads = lambda values: grid(values)[:, 0]
    count = sections * (rows // SEG)
    is_cls = (jnp.arange(rows) % SEG == 0)[:, None]
    b_own = after(jnp.where(is_cls, jnp.zeros_like(cot), cot), every_vector)
    b_next = swap_dp(b_own, 2)
    b_sib, b_far = swap_core(b_own), swap_core(b_next)
    layout = row_layout(seg_counts[0])

    bf = lambda *shape: (shape, BF)
    triple, a, give0, keep0, wt, wo = call(
        att_fwd_kernel,
        [bf(2 * rows, 3 * half), bf(2 * rows, half)]
        + [bf(rows, features)] * 2
        + [bf(features, 3 * half), bf(half, features)],
        [place_of(ATT_WAYS, section, core).reshape(1), after(x, b_sib, b_far), x_sib, avec, att_part, att_first, att_second, att_last],
        [pltpu.SemaphoreType.DMA((4,))],
        scalars=1,
        anywhere=4,
        cost=1,
    )
    core0 = swap_core(give0)

    def hop(values, start, end):
        return permute(values, lambda s, r: (end, r), lambda s, r: s == start)

    def on(column, run):
        return lax.cond(section == column, lambda: run()[0], lambda: jnp.zeros((count, 2 * features), BF))

    branch = heads(keep0).astype(F32) + heads(core0).astype(F32)
    cls1_own = (heads(x).astype(F32) + branch + avec[2:3]).astype(BF)
    cls1 = jnp.concatenate(to_column(jnp.concatenate([cls1_own, heads(cot)], 1), 1), 0)
    h1, u_own = call(att_join_kernel, [bf(rows, features)] * 2, [x, keep0, after(core0, cls1_own), avec, mvec])
    u_next = swap_dp(u_own, 2)
    u_sib = swap_core(u_own)

    cls2 = on(1, lambda: cls_mlp("out", cls1, cls1, wide_w, down_w, vector))
    cls2_at2 = hop(cls2, 1, 2)

    scratch = [pltpu.VMEM((2 * rows, features), BF)] * 4
    square = ((features, features), F32)
    keep1, give1, dw, dv, w1, v1 = call(
        partial(mlp_kernel, False),
        [bf(2 * rows, features)] * 2 + [square] * 2 + [bf(features, features)] * 2,
        [
            place_of(MLP_WAYS, section, core).reshape(1), after(u_own, cls2_at2), u_sib, b_own, b_sib,
            mlp_part, mlp_first, mlp_second, mlp_last,
        ],
        scratch + [pltpu.SemaphoreType.DMA((2,))],
        scalars=1,
        anywhere=4,
        cost=13,
    )
    u_far = swap_core(after(u_next, dw))
    keep2, give2, mlp_grad = call(
        partial(mlp_kernel, True),
        [bf(2 * rows, features)] * 2 + [bf(4, half, features)],
        [u_next, u_far, b_next, b_far, w1, v1, dw, dv],
        scratch,
        cost=13,
    )
    cls2_at2 = after(cls2_at2, mlp_grad)
    core1, core2 = swap_core(give1), swap_core(give2)
    ybit, xbit = section // 2, section % 2
    near_row = swap_section(lax.dynamic_slice_in_dim(mlp_grad, 2 - 2 * ybit, 2, 0), 2)
    shape = [bf(count, 2 * features)]
    cls3 = on(2, lambda: call(cls_att_fwd_kernel, shape, [cls2_at2, *layout, wide_w, vector]))
    cls3_at3 = hop(cls3, 2, 3)
    pair_next = swap_dp(pair_sum(keep2, core2), 2)
    dcls3 = on(3, lambda: cls_mlp("both", cls3_at3, cls3_at3, wide_w, down_w, vector))
    dcls3_at2 = hop(dcls3, 3, 2)
    dcls2 = on(
        2, lambda: call(partial(cls_att_bwd_kernel, False), shape, [cls2_at2, dcls3_at2, *layout, wide_w, vector])
    )
    dcls2_at1 = after(hop(dcls2, 2, 1), near_row)
    dcls1 = on(1, lambda: cls_mlp("back", cls1, dcls2_at1, wide_w, down_w, vector))
    split = after(dcls1, pair_next).reshape(sections, rows // SEG, 2 * features)
    arrived = [hop(split[1 ^ bits], 1, 1 ^ bits) for bits in (1, 2, 3)]
    back_rows = jnp.where(section == 1, split[1], arrived[0] + arrived[1] + arrived[2])
    mlp_half = (lax.dynamic_slice_in_dim(mlp_grad, 2 * ybit, 2, 0).astype(F32) + near_row.astype(F32)).astype(BF)

    mine_in = jnp.where(section == 1, cls1, jnp.where(section == 2, cls2_at2, cls3_at3))
    mine_grad = jnp.where(section == 1, dcls2_at1[:, :features], dcls3_at2[:, :features])
    mine_grad = jnp.where(section == 3, cls3_at3[:, features:], mine_grad)
    marks = jnp.concatenate([layout[0], layout[1] % (SEGS + 1)], 1).astype(BF)
    everything = jnp.concatenate([mine_in[:, :features], mine_grad, jnp.pad(marks, ((0, 0), (0, 126)))], 1)
    bits = 1
    while bits < replicas:
        other = swap_dp(everything, bits)
        everything = jnp.where(
            replica & bits == 0, jnp.concatenate([everything, other], 0), jnp.concatenate([other, everything], 0)
        )
        bits *= 2

    dh1, mlp_small = call(
        mlp_done_kernel,
        [bf(rows, features), ((8, features), F32)],
        [after(h1, dcls1), b_own, keep1, core1, pair_next, mvec],
    )
    place = lambda values, cls: lax.dynamic_update_slice(grid(values), cls[:, None], (0, 0, 0)).reshape(rows, features)
    dh1 = place(dh1, back_rows[:, :features])
    dh1_sib = swap_core(dh1)

    near_block = swap_section(after(pick(mlp_half, 1 - xbit), back_rows), 1)
    mlp_block = (pick(mlp_half, xbit).astype(F32) + near_block.astype(F32)).astype(BF)
    mlp_block = after(mlp_block, everything)
    mlp_sum = dp_sum(mlp_block, 4)

    att_grad, du0_own, du0_sib = call(
        att_bwd_kernel,
        [bf(4, half + 16, features)] + [bf(rows, features)] * 2,
        [after(x, mlp_block), x_sib, dh1, dh1_sib, triple, a, wt, wo, avec, mlp_small],
        [pltpu.VMEM((2 * rows, features), BF), pltpu.VMEM((2 * rows, 3 * half), BF)],
        cost=19,
    )

    du0_core = swap_core(du0_sib)
    (input_grad,) = call(att_done_kernel, [bf(rows, features)], [x, dh1, du0_own, du0_core, avec])

    branch = keep1[rows:].astype(F32) + core1[rows:].astype(F32) + pair_next[rows:].astype(F32)
    h2 = (h1.astype(F32) + branch + mvec[2:3]).astype(BF)
    layer_out = place(h2, back_rows[:, features:])
    everything = after(everything, att_grad)
    all_in, all_grad = everything[:, :features], everything[:, features : 2 * features]
    all_pos = everything[:, 2 * features : 2 * features + 1].astype(jnp.int32)
    all_doc = everything[:, 2 * features + 1 : 2 * features + 2].astype(jnp.int32)
    all_doc += jnp.arange(all_doc.shape[0], dtype=jnp.int32)[:, None] // SEGS * (SEGS + 1)
    all_layout = (all_pos, all_doc, all_doc.reshape(1, -1))
    total = all_in.shape[0]
    none = lambda: [jnp.zeros((total, features), BF)] + [jnp.zeros((total, wide_w.shape[1]), BF)] * 2

    def first_column():
        return [jnp.zeros(vector.shape, F32), blank(wide_w.shape), jnp.zeros(down_w.shape, F32), *none()]

    def second_column():
        sums, *factors = cls_mlp("factors", all_in, all_grad, wide_w, down_w, vector)
        return [sums, blank(wide_w.shape), blank(down_w.shape), *factors]

    def third_column():
        sums, wide_sum = cls_att_weights(all_in, all_grad, all_layout, wide_w, vector)
        return [sums, wide_sum, jnp.zeros(down_w.shape, F32), *none()]

    def fourth_column():
        return [*cls_mlp("weights", all_in, all_grad, wide_w, down_w, vector), *none()]

    vector_sum, wide_sum, down_sum, u_cls, dh_cls, act_cls = lax.switch(
        section, [first_column, second_column, third_column, fourth_column]
    )
    mlp_next = swap_dp(after(mlp_sum, u_cls), 2)
    att_block = section_sum(att_grad, section, u_cls, input_grad, mlp_next)
    mlp_blocks = jnp.stack(after([mlp_sum, mlp_next], att_block))
    att_block = pair_sum(att_block, swap_dp(att_block, 2))
    wall = fence(60, att_block)
    att_block = pair_sum(att_block, after(swap_dp(att_block, 4), wall))
    att_block = dp_sum(att_block, 8)
    mlp_own = jnp.stack(after(to_column(mlp_blocks, 1), wall))
    small = att_block[half:]
    att_own = jnp.stack(to_column(att_block[:half], 0))
    att_other = swap_core(att_own)
    small = (small.astype(F32) + swap_core(small).astype(F32))[:3]
    mlp_other = swap_core(mlp_own)
    wide_like, down_like = jax.ShapeDtypeStruct(wide_w.shape, F32), jax.ShapeDtypeStruct(down_w.shape, F32)
    wide_sum, down_sum = pl.pallas_call(
        mlp_place_kernel,
        out_shape=[wide_like, down_like],
        in_specs=[SMEM] + [VMEM] * 4 + [ANY] * 4,
        out_specs=[ANY, ANY],
        scratch_shapes=[
            pltpu.VMEM((2, 4, 2, half, features), BF),
            pltpu.VMEM((4, features, features), F32),
            pltpu.VMEM((4, features, features), F32),
            pltpu.SemaphoreType.DMA((2,)),
            pltpu.SemaphoreType.DMA((8,)),
        ],
        input_output_aliases={7: 0, 8: 1},
        compiler_params=pltpu.CompilerParams(vmem_limit_bytes=LIMIT),
    )(who, u_cls, all_grad, dh_cls, act_cls, mlp_own, mlp_other, wide_sum, down_sum)
    wide_sum = pl.pallas_call(
        att_place_kernel,
        out_shape=wide_like,
        in_specs=[SMEM] + [ANY] * 3,
        out_specs=ANY,
        scratch_shapes=[
            pltpu.VMEM((8, half, features), BF),
            pltpu.VMEM((4, features // 4, 4 * features), F32),
            pltpu.SemaphoreType.DMA((2,)),
            pltpu.SemaphoreType.DMA((4,)),
        ],
        input_output_aliases={3: 0},
        compiler_params=pltpu.CompilerParams(vmem_limit_bytes=LIMIT),
    )(who, att_own, att_other, wide_sum)
    mine_small = jnp.where(section < 2, small, 0.0)
    vector_sum = vector_sum + jnp.pad(mine_small, ((0, vector.shape[0] - 3), (0, 0)))
    return layer_out[None], input_grad[None], wide_sum[None], down_sum[None], vector_sum[None]


def solution(mesh):
    return jax.shard_map(
        local,
        mesh=mesh,
        in_specs=(
            P("section", "dp", None),
            P("section", "dp", None),
            P("section", None, None),
            P("section", None, None),
            P("section", None, None),
            P("dp", None, None),
        ),
        out_specs=(
            P("section", "dp", None),
            P("section", "dp", None),
            P("section", None, None),
            P("section", None, None),
            P("section", None, None),
        ),
        check_vma=False,
    )
```

```python
from functools import partial

import jax
import jax.numpy as jnp
from jax import lax
from jax.experimental import pallas as pl
from jax.experimental.pallas import tpu as pltpu
from jax.sharding import PartitionSpec as P

HEADS = 12
SEG = 128
SEGS = 4
EPSILON = 1e-05
SCORE_SCALE = 0.125
MASKED = -1e30
AXES = ("section", "dp")
BF = jnp.bfloat16
F32 = jnp.float32

NN = (((1,), (0,)), ((), ()))
NT = (((1,), (1,)), ((), ()))
TN = (((0,), (0,)), ((), ()))

GELU_A = 0.7978845608028654
GELU_B = 0.044715

ATT_WAYS = ((0, 1, 2, 3), (0, 2, 1, 3))
MLP_WAYS = ((1, 0, 3, 2), (1, 3, 0, 2))


def mm(left, right, dims=NN):
    return lax.dot_general(left, right, dims, preferred_element_type=F32)


def permute(shard, move, keep=lambda s, r: True):
    sections, replicas = lax.axis_size("section"), lax.axis_size("dp")
    pairs = []
    for s in range(sections):
        for r in range(replicas):
            if keep(s, r):
                t, q = move(s, r)
                pairs.append((s * replicas + r, t * replicas + q))
    return lax.ppermute(shard, AXES, pairs)


def swap_core(shard):
    return permute(shard, lambda s, r: (s, r ^ 1))


def swap_section(shard, bits):
    return permute(shard, lambda s, r: (s ^ bits, r))


def swap_dp(shard, bits):
    return permute(shard, lambda s, r: (s, r ^ bits))


def send(values, ways, start, end):
    return permute(values, lambda s, r: (ways[r & 1][end], r), lambda s, r: ways[r & 1][start] == s)


def after(value, *marks):
    return lax.optimization_barrier((value, marks))[0]


def place_of(ways, section, core):
    position = jnp.int32(0)
    for c in range(2):
        for k, s in enumerate(ways[c]):
            position = jnp.where((section == s) & (core == c), k, position)
    return position


def pick(stack, index):
    return lax.dynamic_index_in_dim(stack, index, 0, keepdims=False)


def section_sum(grad, section, *marks):
    own = pick(grad, section).astype(F32)
    first, second, third = after([swap_section(pick(grad, section ^ bits), bits) for bits in (1, 2, 3)], *marks)
    return (own + first.astype(F32) + second.astype(F32) + third.astype(F32)).astype(BF)


def dp_sum(value, bits):
    while bits < lax.axis_size("dp"):
        value = pair_sum(value, swap_dp(value, bits))
        bits *= 2
    return value


def pair_sum(mine, other):
    return (mine.astype(F32) + other.astype(F32)).astype(BF)


def ordered(first, second, swapped):
    return jnp.where(swapped, jnp.concatenate([second, first], 0), jnp.concatenate([first, second], 0))


def gather_dp(value, replica):
    replicas = lax.axis_size("dp")
    if replicas == 8:
        one, two, three = [swap_dp(value, bits) for bits in (2, 4, 6)]
        odd, high = replica // 2 % 2 == 1, replica // 4 == 1
        value = ordered(ordered(value, one, odd), ordered(two, three, odd), high)
        return ordered(value, swap_core(value), replica % 2 == 1)
    bits = 1
    while bits < replicas:
        value = ordered(value, swap_dp(value, bits), replica & bits != 0)
        bits *= 2
    return value


def to_column(value, owner):
    arrived = [permute(value, lambda s, r: (owner, r), lambda s, r: s == owner ^ bits) for bits in (1, 2, 3)]
    columns = [None] * 4
    columns[owner] = value
    for bits, other in zip((1, 2, 3), arrived):
        columns[owner ^ bits] = other
    return columns


def fetch(sources, targets, sems):
    return [pltpu.make_async_copy(source, target, sems.at[i]) for i, (source, target) in enumerate(zip(sources, targets))]


def norm_parts(values):
    center = values - jnp.mean(values, -1, keepdims=True)
    spread = jnp.mean(center * center, -1, keepdims=True)
    scale = lax.rsqrt(spread + EPSILON)
    return center * scale, scale


def norm_rows(values, vec_ref):
    hat, _ = norm_parts(values)
    return hat * vec_ref[0:1, :] + vec_ref[1:2, :]


def norm_back(values, grad_normed, vec_ref):
    hat, scale = norm_parts(values)
    inner = grad_normed * vec_ref[0:1, :]
    first = jnp.mean(inner, -1, keepdims=True)
    second = jnp.mean(inner * hat, -1, keepdims=True)
    return scale * (inner - first - hat * second), grad_normed * hat


def column_sum(values):
    return jnp.sum(values, 0, keepdims=True)


def gelu_parts(hidden):
    square = hidden * hidden
    inner = GELU_A * hidden * (1.0 + GELU_B * square)
    t = jnp.tanh(inner)
    half = 0.5 * (1.0 + t)
    slope = half + 0.5 * hidden * (1.0 - t * t) * (GELU_A * (1.0 + 3.0 * GELU_B * square))
    return hidden * half, slope


def two_heads(pair):
    low = lax.broadcasted_iota(jnp.int32, pair.shape, 1) < 64
    zero = jnp.zeros_like(pair)
    return jnp.concatenate([jnp.where(low, pair, zero), jnp.where(low, zero, pair)], 0)


def join_heads(both):
    rows = both.shape[0] // 2
    low = lax.broadcasted_iota(jnp.int32, (rows, both.shape[1]), 1) < 64
    return jnp.where(low, both[:rows], both[rows:])


def softmax_rows(scores):
    powers = jnp.exp(scores - jnp.max(scores, -1, keepdims=True))
    return powers / jnp.sum(powers, -1, keepdims=True)


def softmax_columns(scores):
    powers = jnp.exp(scores - jnp.max(scores, 0, keepdims=True))
    return powers * (1.0 / jnp.sum(powers, 0, keepdims=True))


def head_pairs(q, k, v, out):
    for seg in range(q.shape[0] // SEG):
        at = slice(seg * SEG, (seg + 1) * SEG)
        mixed = []
        for pair in range(q.shape[1] // 128):
            lanes = slice(pair * 128, (pair + 1) * 128)
            probs = softmax_columns(mm(k[at, lanes], two_heads(q[at, lanes]), NT) * SCORE_SCALE)
            mixed.append(join_heads(mm(probs.astype(BF), v[at, lanes], TN)).astype(BF))
        out.append(jnp.concatenate(mixed, 1))


def att_fwd_kernel(place_ref, own_ref, sib_ref, vec_ref, *refs):
    choices, (triple_ref, a_ref, give_ref, keep_ref, wt, wo, sems) = refs[:4], refs[4:]
    rows, features = own_ref.shape
    half = a_ref.shape[1]
    top = pl.ds(0, features)

    def load(source):
        return fetch(
            [
                source.at[top, :],
                source.at[pl.ds(features, half), pl.ds(0, half)],
                source.at[pl.ds(features, half), pl.ds(half, half)],
                source.at[pl.ds(features + half, half), :],
            ],
            [
                wt.at[:, pl.ds(0, features)],
                wt.at[pl.ds(0, half), pl.ds(features, half)],
                wt.at[pl.ds(half, half), pl.ds(features, half)],
                wo,
            ],
            sems,
        )

    for k, choice in enumerate(choices):

        @pl.when(place_ref[0] == k)
        def _():
            for copy in load(choice):
                copy.start()

    waits = load(choices[0])
    for pack, (ref, out) in enumerate(((sib_ref, give_ref), (own_ref, keep_ref))):
        span = slice((1 - pack) * rows, (2 - pack) * rows)
        u = norm_rows(ref[...].astype(F32), vec_ref).astype(BF)
        if pack == 0:
            for wait in waits:
                wait.wait()
        triple = mm(u, wt[...]).astype(BF)
        triple_ref[span, :] = triple
        mixed = []
        head_pairs(triple[:, :half], triple[:, half : 2 * half], triple[:, 2 * half :], mixed)
        a = jnp.concatenate(mixed, 0)
        a_ref[span, :] = a
        out[...] = mm(a, wo[...]).astype(BF)


def att_bwd_kernel(
    own_ref, sib_ref, gown_ref, gsib_ref, triple_ref, a_ref, wt, wo, vec_ref, small_ref,
    grad_ref, duown_ref, dusib_ref, u_ref, dt_ref,
):
    rows = own_ref.shape[0]
    half = a_ref.shape[1]
    part = half // 4
    gain = shift = 0.0
    for pack, (x_ref, g_ref, out) in enumerate(((own_ref, gown_ref, duown_ref), (sib_ref, gsib_ref, dusib_ref))):
        span = slice(pack * rows, (pack + 1) * rows)
        hat, _ = norm_parts(x_ref[...].astype(F32))
        u_ref[span, :] = (hat * vec_ref[0:1, :] + vec_ref[1:2, :]).astype(BF)
        da = mm(g_ref[...], wo[...], NT).astype(BF)
        for seg in range(rows // SEG):
            at = slice(seg * SEG, (seg + 1) * SEG)
            to = slice(pack * rows + seg * SEG, pack * rows + (seg + 1) * SEG)
            for pair in range(half // 128):
                lanes = [slice(kind * half + pair * 128, kind * half + (pair + 1) * 128) for kind in range(3)]
                q2, k, v = two_heads(triple_ref[to, lanes[0]]), triple_ref[to, lanes[1]], triple_ref[to, lanes[2]]
                da2 = two_heads(da[at, lanes[0]])
                probs = softmax_columns(mm(k, q2, NT) * SCORE_SCALE)
                dy = mm(v, da2, NT)
                ds = (probs * (dy - jnp.sum(dy * probs, 0, keepdims=True))).astype(BF)
                dt_ref[to, lanes[2]] = mm(probs.astype(BF), da2).astype(BF)
                dt_ref[to, lanes[0]] = (join_heads(mm(ds, k, TN)) * SCORE_SCALE).astype(BF)
                dt_ref[to, lanes[1]] = (mm(ds, q2) * SCORE_SCALE).astype(BF)
        du = mm(dt_ref[span, :], wt[...], NT)
        out[...] = du.astype(BF)
        gain = gain + column_sum(du * hat)
        shift = shift + column_sum(du)

    grad_ref[:, 4 * part :, :] = jnp.zeros((4, 16, grad_ref.shape[2]), BF)
    rest = jnp.zeros((13, grad_ref.shape[2]), F32)
    sums = [gain, shift, column_sum(gown_ref[...].astype(F32)), rest]
    grad_ref[0, 4 * part :, :] = jnp.concatenate(sums, 0).astype(BF)
    grad_ref[1, 4 * part :, :] = jnp.concatenate([small_ref[...], small_ref[...]], 0).astype(BF)
    dwo = mm(a_ref[:rows, :], gown_ref[...], TN) + mm(a_ref[rows:, :], gsib_ref[...], TN)
    dw = mm(u_ref[...], dt_ref[:, : 2 * half], TN)
    dwv = mm(u_ref[...], dt_ref[:, 2 * half :], TN)
    for quarter in range(4):
        grad_ref[quarter, : 2 * part, :] = dw[quarter * 2 * part : (quarter + 1) * 2 * part, :].astype(BF)
        for side in range(2):
            grad_ref[quarter, 2 * part : 3 * part, side * half : (side + 1) * half] = dwv[
                side * half + quarter * part : side * half + (quarter + 1) * part, :
            ].astype(BF)
        grad_ref[quarter, 3 * part : 4 * part, :] = dwo[quarter * part : (quarter + 1) * part, :].astype(BF)


def att_done_kernel(x_ref, g_ref, duown_ref, dusib_ref, vec_ref, out_ref):
    du = duown_ref[...].astype(F32) + dusib_ref[...].astype(F32)
    back, _ = norm_back(x_ref[...].astype(F32), du, vec_ref)
    out_ref[...] = (g_ref[...].astype(F32) + back).astype(BF)


def att_join_kernel(x_ref, keep_ref, core_ref, avec_ref, mvec_ref, h_ref, u_ref):
    branch = keep_ref[...].astype(F32) + core_ref[...].astype(F32)
    out = (x_ref[...].astype(F32) + branch + avec_ref[2:3, :]).astype(BF)
    h_ref[...] = out
    u_ref[...] = norm_rows(out.astype(F32), mvec_ref).astype(BF)


def mlp_kernel(last, *refs):
    if last:
        uown_ref, usib_ref, bown_ref, bsib_ref, w_ref, v_ref, dwin_ref, dvin_ref, keep_ref, give_ref, grad_ref = refs[:11]
    else:
        place_ref, uown_ref, usib_ref, bown_ref, bsib_ref, *choices = refs[:9]
        keep_ref, give_ref, dw_ref, dv_ref, w_ref, v_ref = refs[9:15]
        size = w_ref.shape[0]
        load = lambda choice: fetch(
            [choice.at[pl.ds(0, size), :], choice.at[pl.ds(size, size), :]], [w_ref, v_ref], refs[19]
        )
        for k, choice in enumerate(choices):

            @pl.when(place_ref[0] == k)
            def _():
                for copy in load(choice):
                    copy.start()

        waits = load(choices[0])
    u, b, act, dhs = refs[11:15] if last else refs[15:19]
    rows = uown_ref.shape[0]
    for pack, (ur, br, to) in enumerate(((usib_ref, bsib_ref, give_ref), (uown_ref, bown_ref, keep_ref))):
        at = slice(pack * rows, (pack + 1) * rows)
        u[at, :], b[at, :] = ur[...], br[...]
        if not last and pack == 0:
            for wait in waits:
                wait.wait()
        active, slope = gelu_parts(mm(ur[...], w_ref[...]))
        act[at, :] = active.astype(BF)
        dhs[at, :] = (mm(br[...], v_ref[...], NT) * slope).astype(BF)
        to[:rows, :] = mm(dhs[at, :], w_ref[...], NT).astype(BF)
        to[rows:, :] = mm(act[at, :], v_ref[...]).astype(BF)
    dw = mm(u[...], dhs[...], TN)
    dv = mm(act[...], b[...], TN)
    if last:
        part = dw.shape[0] // 4
        for quarter in range(4):
            at = slice(quarter * part, (quarter + 1) * part)
            grad_ref[quarter, :part, :] = (dwin_ref[at, :] + dw[at, :]).astype(BF)
            grad_ref[quarter, part:, :] = (dvin_ref[at, :] + dv[at, :]).astype(BF)
    else:
        dw_ref[...] = dw
        dv_ref[...] = dv


def mlp_done_kernel(h_ref, b_ref, keep_ref, core_ref, z_ref, vec_ref, grad_ref, small_ref):
    rows = h_ref.shape[0]
    du = keep_ref[:rows, :].astype(F32) + core_ref[:rows, :].astype(F32) + z_ref[...].astype(F32)
    grad = b_ref[...].astype(F32)
    back, gain = norm_back(h_ref[...].astype(F32), du, vec_ref)
    grad_ref[...] = (grad + back).astype(BF)
    small_ref[...] = jnp.zeros_like(small_ref)
    small_ref[0:1, :] = column_sum(gain)
    small_ref[1:2, :] = column_sum(du)
    small_ref[2:3, :] = column_sum(grad)


def cls_mlp_kernel(mode, h_ref, b_ref, w_ref, v_ref, vec_ref, *refs):
    features = w_ref.shape[0]
    forward, backward = mode in ("out", "both"), mode in ("back", "both")
    weights, factors = mode == "weights", mode == "factors"
    j = pl.program_id(0)
    if weights:
        small_ref, dw_ref, dv_ref, u_ref, out_acc, du_acc = refs
    elif factors:
        small_ref, u_ref, dh_ref, act_ref, out_acc, du_acc = refs
    else:
        out_ref, u_ref, out_acc, du_acc = refs

    @pl.when(j == 0)
    def _():
        u_ref[...] = norm_rows(h_ref[:, :features].astype(F32), vec_ref).astype(BF)
        out_acc[...] = jnp.zeros_like(out_acc)
        du_acc[...] = jnp.zeros_like(du_acc)

    u = u_ref[...]
    active, slope = gelu_parts(mm(u, w_ref[...]))
    active = active.astype(BF)
    if forward:
        out_acc[...] += mm(active, v_ref[...])
    if not forward or backward:
        b = b_ref[:, -features:] if mode == "both" else b_ref[:, :features]
        dh = (mm(b, v_ref[...], NT) * slope).astype(BF)
        du_acc[...] += mm(dh, w_ref[...], NT)
    if weights:
        dw_ref[...] = mm(u, dh, TN)
        dv_ref[...] = mm(active, b, TN)
    if factors:
        dh_ref[...] = dh
        act_ref[...] = active

    @pl.when(j == pl.num_programs(0) - 1)
    def _():
        values = h_ref[:, :features].astype(F32)
        if forward:
            out = (values + out_acc[...] + vec_ref[2:3, :]).astype(BF)
        if not forward or backward:
            grad = b.astype(F32)
            back, gain = norm_back(values, du_acc[...], vec_ref)
            back = (grad + back).astype(BF)
        if mode == "out":
            out_ref[:, :features] = out
            out_ref[:, features:] = h_ref[:, features:]
        if mode == "both":
            out_ref[:, :features] = back
            out_ref[:, features:] = out
        if mode == "back":
            out_ref[:, :features] = back
            out_ref[:, features:] = b_ref[:, features:]
        if weights or factors:
            small_ref[...] = jnp.zeros_like(small_ref)
            small_ref[0:1, :] = column_sum(gain)
            small_ref[1:2, :] = column_sum(du_acc[...])
            small_ref[2:3, :] = column_sum(grad)


def lifted_rows(h_ref, pos_ref, vec_ref):
    values = h_ref[:, : vec_ref.shape[1]].astype(F32)
    pos = pos_ref[:, :1]
    for p in range(SEGS):
        values = values + jnp.where(pos == p, vec_ref[3 + p : 4 + p, :], 0.0)
    return values


def cls_att_forward(values, col_ref, row_ref, w_ref, vec_ref):
    features = values.shape[1]
    u = norm_rows(values, vec_ref).astype(BF)
    triple = mm(u, w_ref[:, : 3 * features]).astype(BF)
    column = jnp.concatenate([col_ref[:, :1], col_ref[:, :1]], 0)
    mask = column == row_ref[...]
    probs, mixed = [], []
    for pair in range(features // 128):
        lanes = slice(pair * 128, (pair + 1) * 128)
        q2 = two_heads(triple[:, lanes])
        k = triple[:, features + pair * 128 : features + (pair + 1) * 128]
        v = triple[:, 2 * features + pair * 128 : 2 * features + (pair + 1) * 128]
        scores = jnp.where(mask, mm(q2, k, NT) * SCORE_SCALE, MASKED)
        probs.append(softmax_rows(scores))
        mixed.append(join_heads(mm(probs[-1].astype(BF), v)).astype(BF))
    return u, triple, probs, jnp.concatenate(mixed, 1)


def cls_att_fwd_kernel(h_ref, pos_ref, col_ref, row_ref, w_ref, vec_ref, out_ref):
    values = lifted_rows(h_ref, pos_ref, vec_ref)
    features = values.shape[1]
    _, _, _, mixed = cls_att_forward(values, col_ref, row_ref, w_ref, vec_ref)
    out_ref[:, :features] = (values + mm(mixed, w_ref[:, 3 * features :]) + vec_ref[2:3, :]).astype(BF)
    out_ref[:, features:] = h_ref[:, features:]


def cls_att_bwd_kernel(weights_too, h_ref, g_ref, pos_ref, col_ref, row_ref, w_ref, vec_ref, *refs):
    values = lifted_rows(h_ref, pos_ref, vec_ref)
    features = values.shape[1]
    u, triple, probs, mixed = cls_att_forward(values, col_ref, row_ref, w_ref, vec_ref)
    b = g_ref[:, :features]
    da = mm(b, w_ref[:, 3 * features :], NT).astype(BF)
    dqs, dks, dvs = [], [], []
    for pair in range(features // 128):
        lanes = slice(pair * 128, (pair + 1) * 128)
        q2 = two_heads(triple[:, lanes])
        k = triple[:, features + pair * 128 : features + (pair + 1) * 128]
        v = triple[:, 2 * features + pair * 128 : 2 * features + (pair + 1) * 128]
        da2 = two_heads(da[:, lanes])
        y = probs[pair]
        dy = mm(da2, v, NT)
        ds = (y * (dy - jnp.sum(dy * y, -1, keepdims=True))).astype(BF)
        dvs.append(mm(y.astype(BF), da2, TN).astype(BF))
        dqs.append((join_heads(mm(ds, k)) * SCORE_SCALE).astype(BF))
        dks.append((mm(ds, q2, TN) * SCORE_SCALE).astype(BF))
    dtriple = jnp.concatenate(dqs + dks + dvs, 1)
    du = mm(dtriple, w_ref[:, : 3 * features], NT)
    back, gain = norm_back(values, du, vec_ref)
    grad = b.astype(F32)
    total = grad + back
    if weights_too:
        small_ref, dw_ref = refs

        @pl.when(pl.program_id(0) == 0)
        def _():
            small_ref[...] = jnp.zeros_like(small_ref)
            dw_ref[...] = jnp.zeros_like(dw_ref)

        small_ref[0:1, :] += column_sum(gain)
        small_ref[1:2, :] += column_sum(du)
        small_ref[2:3, :] += column_sum(grad)
        pos = pos_ref[:, :1]
        for p in range(SEGS):
            small_ref[3 + p : 4 + p, :] += column_sum(jnp.where(pos == p, total, 0.0))
        for part in range(3):
            span = slice(part * features, (part + 1) * features)
            dw_ref[:, span] += mm(u, dtriple[:, span], TN)
        dw_ref[:, 3 * features :] += mm(mixed, b, TN)
    else:
        (out_ref,) = refs
        out_ref[:, :features] = total.astype(BF)
        out_ref[:, features:] = g_ref[:, features:]


def parts_kernel(who_ref, wide_ref, down_ref, att_ref, mlp_ref, sems):
    features = down_ref.shape[1]
    half = features // 2
    lane = lambda kind: pl.ds(pl.multiple_of(kind * features + who_ref[1] * half, 128), half)
    quarter = pl.ds(pl.multiple_of(who_ref[2] * features, features), features)
    copies = fetch(
        [
            wide_ref.at[:, lane(0)],
            wide_ref.at[:, lane(1)],
            wide_ref.at[pl.ds(0, half), lane(2)],
            wide_ref.at[pl.ds(half, half), lane(2)],
            wide_ref.at[pl.ds(pl.multiple_of(who_ref[1] * half, half), half), pl.ds(3 * features, features)],
            wide_ref.at[:, quarter],
            down_ref.at[quarter, :],
        ],
        [
            att_ref.at[pl.ds(0, features), pl.ds(0, half)],
            att_ref.at[pl.ds(0, features), pl.ds(half, half)],
            att_ref.at[pl.ds(features, half), pl.ds(0, half)],
            att_ref.at[pl.ds(features, half), pl.ds(half, half)],
            att_ref.at[pl.ds(features + half, half), :],
            mlp_ref.at[pl.ds(0, features), :],
            mlp_ref.at[pl.ds(features, features), :],
        ],
        sems,
    )
    for copy in copies:
        copy.start()
    for copy in copies:
        copy.wait()


def att_place_kernel(who_ref, *refs):
    sources, (_, out_ref, held, block, sems, out_sems) = refs[:8], refs[8:]
    half = held.shape[1]
    part = half // 4

    def fill(quarter, pieces):
        for core, ref in enumerate(pieces):
            for kind in range(2):
                lanes = slice((2 * kind + core) * half, (2 * kind + core + 1) * half)
                block[quarter, :, lanes] = ref[quarter, : 2 * part, kind * half : (kind + 1) * half].astype(F32)
            for low in range(2):
                row = quarter * 2 * part + low * part
                side, inside = row // half, row % half // part
                block[quarter, low * part : (low + 1) * part, (4 + core) * half : (5 + core) * half] = ref[
                    inside, 2 * part : 3 * part, side * half : (side + 1) * half
                ].astype(F32)
        for low in range(2):
            row = quarter * 2 * part + low * part
            block[quarter, low * part : (low + 1) * part, 6 * half :] = pieces[row // half][
                row % half // part, 3 * part :, :
            ].astype(F32)

    @pl.when(who_ref[0] == 0)
    def _():
        waits = fetch(sources, [held.at[k] for k in range(8)], sems)
        for copy in waits:
            copy.start()
        for copy in waits:
            copy.wait()
        copies = []
        for quarter in range(4):

            @pl.when(who_ref[1] == 0)
            def _():
                fill(quarter, (held.at[0:4], held.at[4:8]))

            @pl.when(who_ref[1] == 1)
            def _():
                fill(quarter, (held.at[4:8], held.at[0:4]))

            rows = pl.ds(quarter * 2 * part, 2 * part)
            copies.append(pltpu.make_async_copy(block.at[quarter], out_ref.at[rows, :], out_sems.at[quarter]))
            copies[-1].start()
        for copy in copies:
            copy.wait()


def mlp_place_kernel(
    who_ref, u_ref, b_ref, dh_ref, act_ref, own_ref, other_ref, _, __, wide_ref, down_ref, held, dws, dvs, sems, out_sems
):
    size = dws.shape[1]
    part = size // 4

    @pl.when(who_ref[0] == 2)
    def _():
        dvs[0] = jnp.zeros_like(dvs[0])
        copies = fetch([dvs.at[0]] * 4, [down_ref.at[pl.ds(k * size, size), :] for k in range(4)], out_sems)
        for copy in copies:
            copy.start()
        for copy in copies:
            copy.wait()

    @pl.when(who_ref[0] == 1)
    def _():
        waits = fetch([own_ref, other_ref], [held.at[0], held.at[1]], sems)
        for copy in waits:
            copy.start()
        copies = []
        for relative in range(4):
            at = pl.ds(pl.multiple_of((who_ref[2] ^ relative) * size, size), size)
            dws[relative] = mm(u_ref[...], dh_ref[:, at], TN)
            dvs[relative] = mm(act_ref[:, at], b_ref[...], TN)
            if relative < 2:
                waits[relative].wait()
            for quarter in range(4):
                piece = held.at[relative % 2, quarter, relative // 2]
                rows = slice(quarter * part, (quarter + 1) * part)
                dws[relative, rows, :] += piece[:part, :].astype(F32)
                dvs[relative, rows, :] += piece[part:, :].astype(F32)
            for k, (source, target) in enumerate(
                ((dws.at[relative], wide_ref.at[:, at]), (dvs.at[relative], down_ref.at[at, :]))
            ):
                copies.append(pltpu.make_async_copy(source, target, out_sems.at[2 * relative + k]))
                copies[-1].start()
        for copy in copies:
            copy.wait()


VMEM = pl.BlockSpec(memory_space=pltpu.VMEM)
SMEM = pl.BlockSpec(memory_space=pltpu.SMEM)
ANY = pl.BlockSpec(memory_space=pl.ANY)
LIMIT = 58 * 2**20


def whole(shape):
    return pl.BlockSpec(shape, lambda i: (0,) * len(shape))


def estimate(microseconds):
    return pl.CostEstimate(flops=int(microseconds * 1.1e9), bytes_accessed=0, transcendentals=0)


def call(kernel, out_shapes, args, scratch=(), anywhere=0, scalars=0, cost=1):
    return pl.pallas_call(
        kernel,
        grid=(1,),
        out_shape=[jax.ShapeDtypeStruct(*shape) for shape in out_shapes],
        in_specs=[SMEM] * scalars
        + [whole(arg.shape) for arg in args[scalars : len(args) - anywhere]]
        + [ANY] * anywhere,
        out_specs=[whole(shape[0]) for shape in out_shapes],
        scratch_shapes=list(scratch),
        compiler_params=pltpu.CompilerParams(vmem_limit_bytes=LIMIT),
        cost_estimate=estimate(cost),
    )(*args)


def blank(shape, dtype=F32):
    return pl.pallas_call(lambda out_ref: None, out_shape=jax.ShapeDtypeStruct(shape, dtype), out_specs=ANY)()


def cls_mlp(mode, rows, grads, wide_w, down_w, vector):
    count = rows.shape[0]
    features, hidden = wide_w.shape
    tile = features
    wide_block = pl.BlockSpec((features, tile), lambda j: (0, j))
    down_block = pl.BlockSpec((tile, features), lambda j: (j, 0))
    sums = jax.ShapeDtypeStruct(vector.shape, F32)
    scratch = [pltpu.VMEM((count, features), BF)] + [pltpu.VMEM((count, features), F32)] * 2
    if mode == "weights":
        out_shape = [sums, jax.ShapeDtypeStruct(wide_w.shape, F32), jax.ShapeDtypeStruct(down_w.shape, F32)]
        out_specs = [whole(vector.shape), wide_block, down_block]
    elif mode == "factors":
        out_shape = [sums, jax.ShapeDtypeStruct((count, features), BF)] + [jax.ShapeDtypeStruct((count, hidden), BF)] * 2
        out_specs = [whole(vector.shape), whole((count, features))] + [pl.BlockSpec((count, tile), lambda j: (0, j))] * 2
        scratch = scratch[1:]
    else:
        out_shape = [jax.ShapeDtypeStruct(rows.shape, BF)]
        out_specs = [whole(rows.shape)]
    return pl.pallas_call(
        partial(cls_mlp_kernel, mode),
        grid=(hidden // tile,),
        in_specs=[whole(rows.shape), whole(grads.shape), wide_block, down_block, whole(vector.shape)],
        out_specs=out_specs,
        out_shape=out_shape,
        scratch_shapes=scratch,
        compiler_params=pltpu.CompilerParams(vmem_limit_bytes=LIMIT),
    )(rows, grads, wide_w, down_w, vector)


def cls_att_weights(rows, grads, layout, wide_w, vector):
    count, features = rows.shape
    block = min(count, 128)
    by_row = lambda width: pl.BlockSpec((block, width), lambda i: (i, 0))
    return pl.pallas_call(
        partial(cls_att_bwd_kernel, True),
        grid=(count // block,),
        in_specs=[
            by_row(features), by_row(features), by_row(128), by_row(128),
            pl.BlockSpec((1, block), lambda i: (0, i)), whole(wide_w.shape), whole(vector.shape),
        ],
        out_specs=[whole(vector.shape), whole(wide_w.shape)],
        out_shape=[jax.ShapeDtypeStruct(vector.shape, F32), jax.ShapeDtypeStruct(wide_w.shape, F32)],
        compiler_params=pltpu.CompilerParams(vmem_limit_bytes=LIMIT),
    )(rows, grads, *layout, wide_w, vector)


def documents(counts):
    ends = jnp.cumsum(counts, -1)
    places = jnp.arange(SEGS, dtype=jnp.int32)
    doc = jnp.sum((places[:, None] >= ends[..., None, :]).astype(jnp.int32), -1)
    slots = jnp.arange(counts.shape[-1], dtype=jnp.int32)
    first = jnp.sum(jnp.where(doc[..., None] == slots, (ends - counts)[..., None, :], 0), -1)
    return doc, places - first


def row_layout(counts):
    doc, pos = documents(counts)
    packs = counts.shape[0]
    label = doc + jnp.arange(packs, dtype=jnp.int32)[:, None] * (counts.shape[1] + 1)
    return wide_column(pos), wide_column(label), label.reshape(1, -1)


def wide_column(values):
    return jnp.broadcast_to(values.reshape(-1, 1), (values.size, 128))


def local(inputs, cotangent, wide, down, vectors, seg_counts):
    sections = lax.axis_size("section")
    replicas = lax.axis_size("dp")
    section = lax.axis_index("section")
    replica = lax.axis_index("dp")
    core, side = replica % 2, replica // 2 % 2
    rows, features = inputs.shape[1:]
    half = features // 2
    wide_w, down_w, vector = wide[0], down[0], vectors[0]
    x, cot = inputs[0], cotangent[0]

    fourth = 2 * side + core
    who = jnp.stack([section, core, fourth]).astype(jnp.int32)
    att_part, mlp_part = pl.pallas_call(
        parts_kernel,
        out_shape=[jax.ShapeDtypeStruct((2 * features, features), BF)] * 2,
        in_specs=[SMEM, ANY, ANY],
        out_specs=[VMEM, VMEM],
        scratch_shapes=[pltpu.SemaphoreType.DMA((7,))],
        compiler_params=pltpu.CompilerParams(vmem_limit_bytes=LIMIT),
    )(who, wide_w, down_w)
    att_first = send(att_part, ATT_WAYS, 0, 1)
    near = [swap_section(vector, bits) for bits in (1, 2, 3)]
    mlp_first = send(mlp_part, MLP_WAYS, 0, 1)
    x_sib = swap_core(x)
    every_vector = jnp.stack([vector] + near)
    avec, mvec = pick(every_vector, section), pick(every_vector, section ^ 1)
    att_second = send(after(att_part, every_vector, mlp_first), ATT_WAYS, 0, 2)
    att_last = send(att_first, ATT_WAYS, 1, 3)
    mlp_second = send(after(mlp_part, every_vector, att_first, x_sib), MLP_WAYS, 0, 2)
    mlp_last = send(after(mlp_first, att_first), MLP_WAYS, 1, 3)

    grid = lambda values: values.reshape(-1, SEG, features)
    heads = lambda values: grid(values)[:, 0]
    count = sections * (rows // SEG)
    is_cls = (jnp.arange(rows) % SEG == 0)[:, None]
    b_own = after(jnp.where(is_cls, jnp.zeros_like(cot), cot), every_vector)
    b_next = swap_dp(b_own, 2)
    b_sib, b_far = swap_core(b_own), swap_core(b_next)
    layout = row_layout(seg_counts[0])

    bf = lambda *shape: (shape, BF)
    triple, a, give0, keep0, wt, wo = call(
        att_fwd_kernel,
        [bf(2 * rows, 3 * half), bf(2 * rows, half)]
        + [bf(rows, features)] * 2
        + [bf(features, 3 * half), bf(half, features)],
        [place_of(ATT_WAYS, section, core).reshape(1), after(x, b_sib, b_far), x_sib, avec, att_part, att_first, att_second, att_last],
        [pltpu.SemaphoreType.DMA((4,))],
        scalars=1,
        anywhere=4,
        cost=1,
    )
    core0 = swap_core(give0)

    def hop(values, start, end):
        return permute(values, lambda s, r: (end, r), lambda s, r: s == start)

    def on(column, run):
        return lax.cond(section == column, lambda: run()[0], lambda: jnp.zeros((count, 2 * features), BF))

    branch = heads(keep0).astype(F32) + heads(core0).astype(F32)
    cls1_own = (heads(x).astype(F32) + branch + avec[2:3]).astype(BF)
    cls1 = jnp.concatenate(to_column(jnp.concatenate([cls1_own, heads(cot)], 1), 1), 0)
    h1, u_own = call(att_join_kernel, [bf(rows, features)] * 2, [x, keep0, after(core0, cls1_own), avec, mvec])
    u_own = after(u_own, cls1)
    u_next, u_sib = swap_dp(u_own, 2), swap_core(u_own)
    cls2 = on(1, lambda: cls_mlp("out", cls1, cls1, wide_w, down_w, vector))
    cls2_at2 = hop(cls2, 1, 2)

    scratch = [pltpu.VMEM((2 * rows, features), BF)] * 4
    square = ((features, features), F32)
    keep1, give1, dw, dv, w1, v1 = call(
        partial(mlp_kernel, False),
        [bf(2 * rows, features)] * 2 + [square] * 2 + [bf(features, features)] * 2,
        [
            place_of(MLP_WAYS, section, core).reshape(1), after(u_own, cls2), u_sib, b_own, b_sib,
            mlp_part, mlp_first, mlp_second, mlp_last,
        ],
        scratch + [pltpu.SemaphoreType.DMA((2,))],
        scalars=1,
        anywhere=4,
    )
    u_far = swap_core(after(u_next, dw))
    keep2, give2, mlp_grad = call(
        partial(mlp_kernel, True),
        [bf(2 * rows, features)] * 2 + [bf(4, half, features)],
        [after(u_next, cls2_at2), u_far, b_next, b_far, w1, v1, dw, dv],
        scratch,
    )
    core1, core2 = swap_core(give1), swap_core(give2)
    pair = pair_sum(keep2, core2)
    du_next = swap_dp(pair[:rows], 2)

    shape = [bf(count, 2 * features)]
    ybit, xbit = section // 2, section % 2
    near_row = swap_section(lax.dynamic_slice_in_dim(mlp_grad, 2 - 2 * ybit, 2, 0), 2)
    cls2_at2 = after(cls2_at2, mlp_grad)
    cls3 = on(2, lambda: call(cls_att_fwd_kernel, shape, [cls2_at2, *layout, wide_w, vector]))
    cls3_at3 = hop(cls3, 2, 3)
    dcls3 = on(3, lambda: cls_mlp("both", cls3_at3, cls3_at3, wide_w, down_w, vector))
    dcls3_at2 = hop(dcls3, 3, 2)
    dcls2 = on(
        2, lambda: call(partial(cls_att_bwd_kernel, False), shape, [cls2_at2, dcls3_at2, *layout, wide_w, vector])
    )
    dh1, mlp_small = call(
        mlp_done_kernel,
        [bf(rows, features), ((8, features), F32)],
        [h1, b_own, keep1, core1, du_next, mvec],
    )
    dcls2_at1 = after(hop(dcls2, 2, 1), dh1, near_row)
    out_next = swap_dp(after(pair[rows:], du_next), 2)
    dcls1 = on(1, lambda: cls_mlp("back", cls1, dcls2_at1, wide_w, down_w, vector))

    mine_in = jnp.where(section == 1, cls1, jnp.where(section == 2, cls2_at2, cls3_at3))
    mine_grad = jnp.where(section == 1, dcls2_at1[:, :features], dcls3_at2[:, :features])
    mine_grad = jnp.where(section == 3, cls3_at3[:, features:], mine_grad)
    marks = jnp.concatenate([layout[0][:, :1], layout[1][:, :1] % (SEGS + 1)], 1).astype(BF)
    everything = jnp.concatenate([mine_in[:, :features], mine_grad, jnp.pad(marks, ((0, 0), (0, 126)))], 1)
    split = dcls1.reshape(sections, rows // SEG, 2 * features)
    arrived = [hop(split[1 ^ bits], 1, 1 ^ bits) for bits in (1, 2, 3)]
    back_rows = jnp.where(section == 1, split[1], arrived[0] + arrived[1] + arrived[2])

    place = lambda values, cls: lax.dynamic_update_slice(grid(values), cls[:, None], (0, 0, 0)).reshape(rows, features)
    dh1 = place(dh1, back_rows[:, :features])
    dh1_sib = swap_core(dh1)


    everything = gather_dp(after(everything, back_rows), replica)

    mlp_half = pair_sum(lax.dynamic_slice_in_dim(mlp_grad, 2 * ybit, 2, 0), near_row)
    near_block = swap_section(after(pick(mlp_half, 1 - xbit), back_rows), 1)
    mlp_block = pair_sum(pick(mlp_half, xbit), near_block)
    mlp_sum = dp_sum(after(mlp_block, everything), 4)

    att_grad, du0_own, du0_sib = call(
        att_bwd_kernel,
        [bf(4, half + 16, features)] + [bf(rows, features)] * 2,
        [after(x, out_next, mlp_block), x_sib, dh1, dh1_sib, triple, a, wt, wo, avec, mlp_small],
        [pltpu.VMEM((2 * rows, features), BF), pltpu.VMEM((2 * rows, 3 * half), BF)],
        cost=19,
    )

    du0_core = swap_core(du0_sib)
    (input_grad,) = call(att_done_kernel, [bf(rows, features)], [x, dh1, du0_own, du0_core, avec])

    branch = keep1[rows:].astype(F32) + core1[rows:].astype(F32) + out_next.astype(F32)
    h2 = (h1.astype(F32) + branch + mvec[2:3]).astype(BF)
    layer_out = place(h2, back_rows[:, features:])
    all_in, all_grad = everything[:, :features], everything[:, features : 2 * features]
    all_pos = everything[:, 2 * features : 2 * features + 1].astype(jnp.int32)
    all_doc = everything[:, 2 * features + 1 : 2 * features + 2].astype(jnp.int32)
    all_doc += jnp.arange(all_doc.shape[0], dtype=jnp.int32)[:, None] // SEGS * (SEGS + 1)
    all_layout = (wide_column(all_pos), wide_column(all_doc), all_doc.reshape(1, -1))
    total = all_in.shape[0]
    none = lambda: [blank((total, features), BF)] + [blank((total, wide_w.shape[1]), BF) for _ in range(2)]

    def first_column():
        return [jnp.zeros(vector.shape, F32), blank(wide_w.shape), jnp.zeros(down_w.shape, F32), *none()]

    def second_column():
        sums, *factors = cls_mlp("factors", all_in, all_grad, wide_w, down_w, vector)
        return [sums, blank(wide_w.shape), blank(down_w.shape), *factors]

    def third_column():
        sums, wide_sum = cls_att_weights(all_in, all_grad, all_layout, wide_w, vector)
        return [sums, wide_sum, blank(down_w.shape), *none()]

    def fourth_column():
        return [*cls_mlp("weights", all_in, all_grad, wide_w, down_w, vector), *none()]

    vector_sum, wide_sum, down_sum, u_cls, dh_cls, act_cls = lax.switch(
        section, [first_column, second_column, third_column, fourth_column]
    )
    mlp_next = swap_dp(mlp_sum, 2)
    att_block = section_sum(att_grad, section, input_grad, layer_out, u_cls)
    mlp_blocks = jnp.stack(after([mlp_sum, mlp_next], att_block))
    att_block = pair_sum(att_block, swap_dp(att_block, 2))
    att_block = dp_sum(att_block, 4)
    mlp_own = jnp.stack(after(to_column(mlp_blocks, 1), att_block))
    small = att_block[half:]
    small = (small.astype(F32) + swap_core(small).astype(F32))[:3]
    mlp_other = swap_core(mlp_own)
    wide_like, down_like = jax.ShapeDtypeStruct(wide_w.shape, F32), jax.ShapeDtypeStruct(down_w.shape, F32)
    wide_sum, down_sum = pl.pallas_call(
        mlp_place_kernel,
        out_shape=[wide_like, down_like],
        in_specs=[SMEM] + [VMEM] * 4 + [ANY] * 4,
        out_specs=[ANY, ANY],
        scratch_shapes=[
            pltpu.VMEM((2, 4, 2, half, features), BF),
            pltpu.VMEM((4, features, features), F32),
            pltpu.VMEM((4, features, features), F32),
            pltpu.SemaphoreType.DMA((2,)),
            pltpu.SemaphoreType.DMA((8,)),
        ],
        input_output_aliases={7: 0, 8: 1},
        compiler_params=pltpu.CompilerParams(vmem_limit_bytes=LIMIT),
    )(who, u_cls, all_grad, dh_cls, act_cls, mlp_own, mlp_other, wide_sum, down_sum)
    att_own = after(to_column(att_block[:half], 0), down_sum)
    att_other = [swap_core(piece) for piece in att_own]
    wide_sum = pl.pallas_call(
        att_place_kernel,
        out_shape=wide_like,
        in_specs=[SMEM] + [ANY] * 9,
        out_specs=ANY,
        scratch_shapes=[
            pltpu.VMEM((8, half, features), BF),
            pltpu.VMEM((4, features // 4, 4 * features), F32),
            pltpu.SemaphoreType.DMA((8,)),
            pltpu.SemaphoreType.DMA((4,)),
        ],
        input_output_aliases={9: 0},
        compiler_params=pltpu.CompilerParams(vmem_limit_bytes=LIMIT),
    )(who, *att_own, *att_other, wide_sum)
    mine_small = jnp.where(section < 2, small, 0.0)
    vector_sum = vector_sum + jnp.pad(mine_small, ((0, vector.shape[0] - 3), (0, 0)))
    return layer_out[None], input_grad[None], wide_sum[None], down_sum[None], vector_sum[None]


def solution(mesh):
    return jax.shard_map(
        local,
        mesh=mesh,
        in_specs=(
            P("section", "dp", None),
            P("section", "dp", None),
            P("section", None, None),
            P("section", None, None),
            P("section", None, None),
            P("dp", None, None),
        ),
        out_specs=(
            P("section", "dp", None),
            P("section", "dp", None),
            P("section", None, None),
            P("section", None, None),
            P("section", None, None),
        ),
        check_vma=False,
    )
```

```python
from functools import partial

import jax
import jax.numpy as jnp
from jax import lax
from jax.experimental import pallas as pl
from jax.experimental.pallas import tpu as pltpu
from jax.sharding import PartitionSpec as P

HEADS = 12
SEG = 128
SEGS = 4
EPSILON = 1e-05
SCORE_SCALE = 0.125
MASKED = -1e30
AXES = ("section", "dp")
BF = jnp.bfloat16
F32 = jnp.float32

NN = (((1,), (0,)), ((), ()))
NT = (((1,), (1,)), ((), ()))
TN = (((0,), (0,)), ((), ()))

GELU_A = 0.7978845608028654
GELU_B = 0.044715

ATT_WAYS = ((0, 1, 2, 3), (0, 2, 1, 3))
MLP_WAYS = ((1, 0, 3, 2), (1, 3, 0, 2))


def mm(left, right, dims=NN):
    return lax.dot_general(left, right, dims, preferred_element_type=F32)


def permute(shard, move, keep=lambda s, r: True):
    sections, replicas = lax.axis_size("section"), lax.axis_size("dp")
    pairs = []
    for s in range(sections):
        for r in range(replicas):
            if keep(s, r):
                t, q = move(s, r)
                pairs.append((s * replicas + r, t * replicas + q))
    return lax.ppermute(shard, AXES, pairs)


def swap_core(shard):
    return permute(shard, lambda s, r: (s, r ^ 1))


def swap_section(shard, bits):
    return permute(shard, lambda s, r: (s ^ bits, r))


def swap_dp(shard, bits):
    return permute(shard, lambda s, r: (s, r ^ bits))


def send(values, ways, start, end):
    return permute(values, lambda s, r: (ways[r & 1][end], r), lambda s, r: ways[r & 1][start] == s)


def after(value, *marks):
    return lax.optimization_barrier((value, marks))[0]


def place_of(ways, section, core):
    position = jnp.int32(0)
    for c in range(2):
        for k, s in enumerate(ways[c]):
            position = jnp.where((section == s) & (core == c), k, position)
    return position


def pick(stack, index):
    return lax.dynamic_index_in_dim(stack, index, 0, keepdims=False)


def section_parts(parts):
    return [swap_section(parts[bits], bits) for bits in (1, 2, 3)]


def section_sum(parts, others=None):
    others = others or section_parts(parts)
    return sum([other.astype(F32) for other in others], parts[0].astype(F32)).astype(BF)


def dp_sum(value, bits):
    while bits < lax.axis_size("dp"):
        value = pair_sum(value, swap_dp(value, bits))
        bits *= 2
    return value


def pair_sum(mine, other):
    return (mine.astype(F32) + other.astype(F32)).astype(BF)


def ordered(first, second, swapped):
    return jnp.where(swapped, jnp.concatenate([second, first], 0), jnp.concatenate([first, second], 0))


def to_column(value, owner):
    arrived = [permute(value, lambda s, r: (owner, r), lambda s, r: s == owner ^ bits) for bits in (1, 2, 3)]
    columns = [None] * 4
    columns[owner] = value
    for bits, other in zip((1, 2, 3), arrived):
        columns[owner ^ bits] = other
    return columns


def fetch(sources, targets, sems):
    return [pltpu.make_async_copy(source, target, sems.at[i]) for i, (source, target) in enumerate(zip(sources, targets))]


def norm_parts(values):
    center = values - jnp.mean(values, -1, keepdims=True)
    spread = jnp.mean(center * center, -1, keepdims=True)
    scale = lax.rsqrt(spread + EPSILON)
    return center * scale, scale


def norm_rows(values, vec_ref):
    hat, _ = norm_parts(values)
    return hat * vec_ref[0:1, :] + vec_ref[1:2, :]


def norm_back(values, grad_normed, vec_ref):
    hat, scale = norm_parts(values)
    inner = grad_normed * vec_ref[0:1, :]
    first = jnp.mean(inner, -1, keepdims=True)
    second = jnp.mean(inner * hat, -1, keepdims=True)
    return scale * (inner - first - hat * second), grad_normed * hat


def column_sum(values):
    return jnp.sum(values, 0, keepdims=True)


def gelu_parts(hidden):
    square = hidden * hidden
    inner = GELU_A * hidden * (1.0 + GELU_B * square)
    t = jnp.tanh(inner)
    half = 0.5 * (1.0 + t)
    slope = half + 0.5 * hidden * (1.0 - t * t) * (GELU_A * (1.0 + 3.0 * GELU_B * square))
    return hidden * half, slope


def two_heads(pair):
    low = lax.broadcasted_iota(jnp.int32, pair.shape, 1) < 64
    zero = jnp.zeros_like(pair)
    return jnp.concatenate([jnp.where(low, pair, zero), jnp.where(low, zero, pair)], 0)


def join_heads(both):
    rows = both.shape[0] // 2
    low = lax.broadcasted_iota(jnp.int32, (rows, both.shape[1]), 1) < 64
    return jnp.where(low, both[:rows], both[rows:])


def softmax_rows(scores):
    powers = jnp.exp(scores - jnp.max(scores, -1, keepdims=True))
    return powers / jnp.sum(powers, -1, keepdims=True)


def softmax_columns(scores):
    powers = jnp.exp(scores - jnp.max(scores, 0, keepdims=True))
    return powers * (1.0 / jnp.sum(powers, 0, keepdims=True))


def head_pairs(q, k, v, out):
    for seg in range(q.shape[0] // SEG):
        at = slice(seg * SEG, (seg + 1) * SEG)
        mixed = []
        for pair in range(q.shape[1] // 128):
            lanes = slice(pair * 128, (pair + 1) * 128)
            probs = softmax_columns(mm(k[at, lanes], two_heads(q[at, lanes]), NT) * SCORE_SCALE)
            mixed.append(join_heads(mm(probs.astype(BF), v[at, lanes], TN)).astype(BF))
        out.append(jnp.concatenate(mixed, 1))


class Copies:
    def __init__(self, sems):
        self.sems, self.used = sems, 0

    def start(self, source, target):
        copy = pltpu.make_async_copy(source, target, self.sems.at[self.used])
        self.used += 1
        copy.start()
        return copy

    def choose(self, which, sources, target):
        sem = self.sems.at[self.used]
        self.used += 1
        for k, source in enumerate(sources):

            @pl.when(which == k)
            def _():
                pltpu.make_async_copy(source, target, sem).start()

        return pltpu.make_async_copy(sources[0], target, sem)


def wait(*copies):
    for copy in copies:
        copy.wait()


def load_triple(copies, place, choices, wt, half):
    features, left, right = wt.shape[0], pl.ds(0, half), pl.ds(half, half)
    return [
        copies.choose(place, [c.at[pl.ds(0, features), :] for c in choices], wt.at[:, pl.ds(0, features)]),
        copies.choose(place, [c.at[pl.ds(features, half), left] for c in choices], wt.at[left, pl.ds(features, half)]),
        copies.choose(place, [c.at[pl.ds(features, half), right] for c in choices], wt.at[right, pl.ds(features, half)]),
    ]


def att_fwd_kernel(place_ref, own_ref, sib_ref, vec_ref, *refs):
    choices, (triple_ref, a_ref, give_ref, keep_ref, wt, wo, triples, mixes, outs, sems) = refs[:4], refs[4:]
    rows, features = own_ref.shape
    half = a_ref.shape[1]
    copies = Copies(sems)
    wt_in = load_triple(copies, place_ref[0], choices, wt, half)
    wo_in = [copies.choose(place_ref[0], [c.at[pl.ds(features + half, half), :] for c in choices], wo)]
    done = []
    for pack, (ref, out) in enumerate(((sib_ref, give_ref), (own_ref, keep_ref))):
        span = pl.ds((1 - pack) * rows, rows)
        u = norm_rows(ref[...].astype(F32), vec_ref).astype(BF)
        if pack == 0:
            wait(*wt_in)
        triple = mm(u, wt[...]).astype(BF)
        triples[pack] = triple
        done.append(copies.start(triples.at[pack], triple_ref.at[span, :]))
        mixed = []
        head_pairs(triple[:, :half], triple[:, half : 2 * half], triple[:, 2 * half :], mixed)
        a = jnp.concatenate(mixed, 0)
        mixes[pack] = a
        done.append(copies.start(mixes.at[pack], a_ref.at[span, :]))
        if pack == 0:
            wait(*wo_in)
        outs[pack] = mm(a, wo[...]).astype(BF)
        done.append(copies.start(outs.at[pack], out))
    wait(*done)


def att_bwd_kernel(place_ref, vec_ref, small_ref, *refs):
    own_ref, sib_ref, gown_ref, gsib_ref, triple_ref, a_ref, *choices = refs[:10]
    grad_refs, (duown_ref, dusib_ref, xs, gs, triple, mixes, wt, wo, u, dt, dus, piece, sems) = refs[10:14], refs[14:]
    rows = own_ref.shape[0]
    half = a_ref.shape[1]
    part = half // 4
    copies = Copies(sems)
    gs_in = [copies.start(gown_ref, gs.at[pl.ds(0, rows), :])]
    early = copies.choose(place_ref[0], [c.at[pl.ds(wt.shape[0] + half, half), :] for c in choices], wo)
    triple_in = [copies.start(triple_ref.at[pl.ds(k * rows, rows), :], triple.at[pl.ds(k * rows, rows), :]) for k in range(2)]
    xs_in = [copies.start(own_ref, xs.at[pl.ds(0, rows), :])]
    wt_in = load_triple(copies, place_ref[0], choices, wt, half)
    gs_in.append(copies.start(gsib_ref, gs.at[pl.ds(rows, rows), :]))
    xs_in.append(copies.start(sib_ref, xs.at[pl.ds(rows, rows), :]))
    a_in = copies.start(a_ref, mixes)
    done = []
    gain = shift = 0.0
    for pack, out in enumerate((duown_ref, dusib_ref)):
        span = slice(pack * rows, (pack + 1) * rows)
        wait(gs_in[pack])
        if pack == 0:
            wait(early)
        da = mm(gs[span, :], wo[...], NT).astype(BF)
        wait(triple_in[pack])
        for seg in range(rows // SEG):
            at = slice(seg * SEG, (seg + 1) * SEG)
            to = slice(pack * rows + seg * SEG, pack * rows + (seg + 1) * SEG)
            for pair in range(half // 128):
                lanes = [slice(kind * half + pair * 128, kind * half + (pair + 1) * 128) for kind in range(3)]
                q2, k, v = two_heads(triple[to, lanes[0]]), triple[to, lanes[1]], triple[to, lanes[2]]
                da2 = two_heads(da[at, lanes[0]])
                probs = softmax_columns(mm(k, q2, NT) * SCORE_SCALE)
                dy = mm(v, da2, NT)
                ds = (probs * (dy - jnp.sum(dy * probs, 0, keepdims=True))).astype(BF)
                dt[to, lanes[2]] = mm(probs.astype(BF), da2).astype(BF)
                dt[to, lanes[0]] = (join_heads(mm(ds, k, TN)) * SCORE_SCALE).astype(BF)
                dt[to, lanes[1]] = (mm(ds, q2) * SCORE_SCALE).astype(BF)
        wait(xs_in[pack])
        hat, _ = norm_parts(xs[span, :].astype(F32))
        u[span, :] = (hat * vec_ref[0:1, :] + vec_ref[1:2, :]).astype(BF)
        if pack == 0:
            wait(*wt_in)
        du = mm(dt[span, :], wt[...], NT)
        dus[pack] = du.astype(BF)
        done.append(copies.start(dus.at[pack], out))
        gain = gain + column_sum(du * hat)
        shift = shift + column_sum(du)

    def send(start, count):
        at = pl.ds(start, count)
        for bits, ref in enumerate(grad_refs):
            done.append(copies.start(piece.at[place_ref[1] ^ bits, at, :], ref.at[at, :]))

    dw = mm(u[...], dt[:, : 2 * half], TN)
    for quarter in range(4):
        piece[quarter, : 2 * part, :] = dw[quarter * 2 * part : (quarter + 1) * 2 * part, :].astype(BF)
    send(0, 2 * part)
    dw = mm(u[...], dt[:, 2 * half :], TN)
    for quarter in range(4):
        for side in range(2):
            piece[quarter, 2 * part : 3 * part, side * half : (side + 1) * half] = dw[
                side * half + quarter * part : side * half + (quarter + 1) * part, :
            ].astype(BF)
    send(2 * part, part)
    wait(a_in)
    dw = mm(mixes[...], gs[...], TN)
    piece[:, 4 * part :, :] = jnp.zeros((4, 16, piece.shape[2]), BF)
    rest = jnp.zeros((13, piece.shape[2]), F32)
    sums = [gain, shift, column_sum(gs[:rows, :].astype(F32)), rest]
    piece[0, 4 * part :, :] = jnp.concatenate(sums, 0).astype(BF)
    piece[1, 4 * part :, :] = jnp.concatenate([small_ref[...], small_ref[...]], 0).astype(BF)
    for quarter in range(4):
        piece[quarter, 3 * part : 4 * part, :] = dw[quarter * part : (quarter + 1) * part, :].astype(BF)
    send(3 * part, part + 16)
    wait(*done)


def att_done_kernel(x_ref, g_ref, duown_ref, dusib_ref, vec_ref, out_ref):
    du = duown_ref[...].astype(F32) + dusib_ref[...].astype(F32)
    back, _ = norm_back(x_ref[...].astype(F32), du, vec_ref)
    out_ref[...] = (g_ref[...].astype(F32) + back).astype(BF)


def att_join_kernel(x_ref, keep_ref, core_ref, avec_ref, mvec_ref, h_ref, u_ref):
    branch = keep_ref[...].astype(F32) + core_ref[...].astype(F32)
    out = (x_ref[...].astype(F32) + branch + avec_ref[2:3, :]).astype(BF)
    h_ref[...] = out
    u_ref[...] = norm_rows(out.astype(F32), mvec_ref).astype(BF)


def mlp_kernel(last, who_ref, *refs):
    uown_ref, usib_ref, bown_ref, bsib_ref, *choices = refs[:8]
    before, refs = refs[8 : 10 if last else 8], refs[10 if last else 8 :]
    keep_ref, give_ref, first_ref, second_ref, u, b, act, dhs, w, v, outs, dws, held, sems = refs
    rows = uown_ref.shape[0]
    size = w.shape[0]
    copies = Copies(sems)
    us_in, bs_in, done = [None, None], [None, None], []
    us_in[1] = copies.start(usib_ref, u.at[pl.ds(rows, rows), :])
    w_in = copies.choose(who_ref[0], [c.at[pl.ds(0, size), :] for c in choices], w)
    bs_in[1] = copies.start(bsib_ref, b.at[pl.ds(rows, rows), :])
    v_in = copies.choose(who_ref[0], [c.at[pl.ds(size, size), :] for c in choices], v)
    for pack, out in ((1, give_ref), (0, keep_ref)):
        at = slice(pack * rows, (pack + 1) * rows)
        wait(us_in[pack])
        if pack == 1:
            wait(w_in)
            us_in[0] = copies.start(uown_ref, u.at[pl.ds(0, rows), :])
            bs_in[0] = copies.start(bown_ref, b.at[pl.ds(0, rows), :])
        active, slope = gelu_parts(mm(u[at, :], w[...]))
        act[at, :] = active.astype(BF)
        wait(bs_in[pack])
        if pack == 1:
            wait(v_in)
            before_in = [copies.start(ref, held.at[k]) for k, ref in enumerate(before)]
        dhs[at, :] = (mm(b[at, :], v[...], NT) * slope).astype(BF)
        outs[pack, :rows, :] = mm(dhs[at, :], w[...], NT).astype(BF)
        outs[pack, rows:, :] = mm(act[at, :], v[...]).astype(BF)
        done.append(copies.start(outs.at[pack], out))
    quarter = size // 4
    for kind, (left, right) in enumerate(((u, dhs), (act, b))):
        dw = mm(left[...], right[...], TN)
        if not last:
            dws[kind] = dw.astype(BF)
            done.append(copies.start(dws.at[kind], (first_ref, second_ref)[kind]))
            continue
        wait(before_in[kind])
        dws[kind] = (dw + held[kind].astype(F32)).astype(BF)
        for k in range(2):
            sem = sems.at[copies.used]
            copies.used += 1
            target = (first_ref, second_ref)[k].at[:, pl.ds(kind * quarter, quarter), :]
            for y in range(2):
                source = dws.at[kind, pl.ds((y ^ k) * 2 * quarter, 2 * quarter), :].reshape(2, quarter, size)

                @pl.when(who_ref[1] == y)
                def _():
                    pltpu.make_async_copy(source, target, sem).start()

            done.append(pltpu.make_async_copy(source, target, sem))
    wait(*done)


def mlp_done_kernel(h_ref, b_ref, keep_ref, core_ref, z_ref, vec_ref, grad_ref, small_ref):
    rows = h_ref.shape[0]
    du = keep_ref[:rows, :].astype(F32) + core_ref[:rows, :].astype(F32) + z_ref[...].astype(F32)
    grad = b_ref[...].astype(F32)
    back, gain = norm_back(h_ref[...].astype(F32), du, vec_ref)
    grad_ref[...] = (grad + back).astype(BF)
    small_ref[...] = jnp.zeros_like(small_ref)
    small_ref[0:1, :] = column_sum(gain)
    small_ref[1:2, :] = column_sum(du)
    small_ref[2:3, :] = column_sum(grad)


def cls_mlp_kernel(mode, h_ref, b_ref, w_ref, v_ref, vec_ref, *refs):
    features = w_ref.shape[0]
    forward, backward = mode in ("out", "both"), mode in ("back", "both")
    weights, factors = mode == "weights", mode == "factors"
    j = pl.program_id(0)
    if weights:
        small_ref, dw_ref, dv_ref, u_ref, out_acc, du_acc = refs
    elif factors:
        small_ref, u_ref, dh_ref, act_ref, out_acc, du_acc = refs
    else:
        out_ref, u_ref, out_acc, du_acc = refs

    @pl.when(j == 0)
    def _():
        u_ref[...] = norm_rows(h_ref[:, :features].astype(F32), vec_ref).astype(BF)
        out_acc[...] = jnp.zeros_like(out_acc)
        du_acc[...] = jnp.zeros_like(du_acc)

    u = u_ref[...]
    active, slope = gelu_parts(mm(u, w_ref[...]))
    active = active.astype(BF)
    if forward:
        out_acc[...] += mm(active, v_ref[...])
    if not forward or backward:
        b = b_ref[:, -features:] if mode == "both" else b_ref[:, :features]
        dh = (mm(b, v_ref[...], NT) * slope).astype(BF)
        du_acc[...] += mm(dh, w_ref[...], NT)
    if weights:
        dw_ref[...] = mm(u, dh, TN)
        dv_ref[...] = mm(active, b, TN)
    if factors:
        dh_ref[...] = dh
        act_ref[...] = active

    @pl.when(j == pl.num_programs(0) - 1)
    def _():
        values = h_ref[:, :features].astype(F32)
        if forward:
            out = (values + out_acc[...] + vec_ref[2:3, :]).astype(BF)
        if not forward or backward:
            grad = b.astype(F32)
            back, gain = norm_back(values, du_acc[...], vec_ref)
            back = (grad + back).astype(BF)
        if mode == "out":
            out_ref[:, :features] = out
            out_ref[:, features:] = h_ref[:, features:]
        if mode == "both":
            out_ref[:, :features] = back
            out_ref[:, features:] = out
        if mode == "back":
            out_ref[:, :features] = back
            out_ref[:, features:] = b_ref[:, features:]
        if weights or factors:
            small_ref[...] = jnp.zeros_like(small_ref)
            small_ref[0:1, :] = column_sum(gain)
            small_ref[1:2, :] = column_sum(du_acc[...])
            small_ref[2:3, :] = column_sum(grad)


def lifted_rows(h_ref, pos_ref, vec_ref):
    values = h_ref[:, : vec_ref.shape[1]].astype(F32)
    pos = pos_ref[:, :1]
    for p in range(SEGS):
        values = values + jnp.where(pos == p, vec_ref[3 + p : 4 + p, :], 0.0)
    return values


def cls_att_forward(values, col_ref, row_ref, w_ref, vec_ref):
    features = values.shape[1]
    u = norm_rows(values, vec_ref).astype(BF)
    triple = mm(u, w_ref[:, : 3 * features]).astype(BF)
    column = jnp.concatenate([col_ref[:, :1], col_ref[:, :1]], 0)
    mask = column == row_ref[...]
    probs, mixed = [], []
    for pair in range(features // 128):
        lanes = slice(pair * 128, (pair + 1) * 128)
        q2 = two_heads(triple[:, lanes])
        k = triple[:, features + pair * 128 : features + (pair + 1) * 128]
        v = triple[:, 2 * features + pair * 128 : 2 * features + (pair + 1) * 128]
        scores = jnp.where(mask, mm(q2, k, NT) * SCORE_SCALE, MASKED)
        probs.append(softmax_rows(scores))
        mixed.append(join_heads(mm(probs[-1].astype(BF), v)).astype(BF))
    return u, triple, probs, jnp.concatenate(mixed, 1)


def cls_att_fwd_kernel(h_ref, pos_ref, col_ref, row_ref, w_ref, vec_ref, out_ref):
    values = lifted_rows(h_ref, pos_ref, vec_ref)
    features = values.shape[1]
    _, _, _, mixed = cls_att_forward(values, col_ref, row_ref, w_ref, vec_ref)
    out_ref[:, :features] = (values + mm(mixed, w_ref[:, 3 * features :]) + vec_ref[2:3, :]).astype(BF)
    out_ref[:, features:] = h_ref[:, features:]


def cls_att_bwd_kernel(weights_too, h_ref, g_ref, pos_ref, col_ref, row_ref, w_ref, vec_ref, *refs):
    values = lifted_rows(h_ref, pos_ref, vec_ref)
    features = values.shape[1]
    u, triple, probs, mixed = cls_att_forward(values, col_ref, row_ref, w_ref, vec_ref)
    b = g_ref[:, :features]
    da = mm(b, w_ref[:, 3 * features :], NT).astype(BF)
    dqs, dks, dvs = [], [], []
    for pair in range(features // 128):
        lanes = slice(pair * 128, (pair + 1) * 128)
        q2 = two_heads(triple[:, lanes])
        k = triple[:, features + pair * 128 : features + (pair + 1) * 128]
        v = triple[:, 2 * features + pair * 128 : 2 * features + (pair + 1) * 128]
        da2 = two_heads(da[:, lanes])
        y = probs[pair]
        dy = mm(da2, v, NT)
        ds = (y * (dy - jnp.sum(dy * y, -1, keepdims=True))).astype(BF)
        dvs.append(mm(y.astype(BF), da2, TN).astype(BF))
        dqs.append((join_heads(mm(ds, k)) * SCORE_SCALE).astype(BF))
        dks.append((mm(ds, q2, TN) * SCORE_SCALE).astype(BF))
    dtriple = jnp.concatenate(dqs + dks + dvs, 1)
    du = mm(dtriple, w_ref[:, : 3 * features], NT)
    back, gain = norm_back(values, du, vec_ref)
    grad = b.astype(F32)
    total = grad + back
    if weights_too:
        small_ref, dw_ref = refs

        @pl.when(pl.program_id(0) == 0)
        def _():
            small_ref[...] = jnp.zeros_like(small_ref)
            dw_ref[...] = jnp.zeros_like(dw_ref)

        small_ref[0:1, :] += column_sum(gain)
        small_ref[1:2, :] += column_sum(du)
        small_ref[2:3, :] += column_sum(grad)
        pos = pos_ref[:, :1]
        for p in range(SEGS):
            small_ref[3 + p : 4 + p, :] += column_sum(jnp.where(pos == p, total, 0.0))
        for part in range(3):
            span = slice(part * features, (part + 1) * features)
            dw_ref[:, span] += mm(u, dtriple[:, span], TN)
        dw_ref[:, 3 * features :] += mm(mixed, b, TN)
    else:
        (out_ref,) = refs
        out_ref[:, :features] = total.astype(BF)
        out_ref[:, features:] = g_ref[:, features:]


def parts_kernel(who_ref, wide_ref, down_ref, att_ref, mlp_ref, sems):
    features = down_ref.shape[1]
    half = features // 2
    lane = lambda kind: pl.ds(pl.multiple_of(kind * features + who_ref[1] * half, 128), half)
    quarter = pl.ds(pl.multiple_of(who_ref[2] * features, features), features)
    copies = fetch(
        [
            wide_ref.at[:, lane(0)],
            wide_ref.at[:, lane(1)],
            wide_ref.at[pl.ds(0, half), lane(2)],
            wide_ref.at[pl.ds(half, half), lane(2)],
            wide_ref.at[pl.ds(pl.multiple_of(who_ref[1] * half, half), half), pl.ds(3 * features, features)],
            wide_ref.at[:, quarter],
            down_ref.at[quarter, :],
        ],
        [
            att_ref.at[pl.ds(0, features), pl.ds(0, half)],
            att_ref.at[pl.ds(0, features), pl.ds(half, half)],
            att_ref.at[pl.ds(features, half), pl.ds(0, half)],
            att_ref.at[pl.ds(features, half), pl.ds(half, half)],
            att_ref.at[pl.ds(features + half, half), :],
            mlp_ref.at[pl.ds(0, features), :],
            mlp_ref.at[pl.ds(features, features), :],
        ],
        sems,
    )
    for copy in copies:
        copy.start()
    for copy in copies:
        copy.wait()


def att_place_kernel(who_ref, *refs):
    sources, (_, out_ref, held, block, sems, out_sems) = refs[:8], refs[8:]
    half = held.shape[1]
    part = half // 4

    def fill(quarter, pieces):
        for core, ref in enumerate(pieces):
            for kind in range(2):
                lanes = slice((2 * kind + core) * half, (2 * kind + core + 1) * half)
                block[quarter, :, lanes] = ref[quarter, : 2 * part, kind * half : (kind + 1) * half].astype(F32)
            for low in range(2):
                row = quarter * 2 * part + low * part
                side, inside = row // half, row % half // part
                block[quarter, low * part : (low + 1) * part, (4 + core) * half : (5 + core) * half] = ref[
                    inside, 2 * part : 3 * part, side * half : (side + 1) * half
                ].astype(F32)
        for low in range(2):
            row = quarter * 2 * part + low * part
            block[quarter, low * part : (low + 1) * part, 6 * half :] = pieces[row // half][
                row % half // part, 3 * part :, :
            ].astype(F32)

    @pl.when(who_ref[0] == 0)
    def _():
        waits = fetch(sources, [held.at[k] for k in range(8)], sems)
        for copy in waits:
            copy.start()
        for copy in waits:
            copy.wait()
        copies = []
        for quarter in range(4):

            @pl.when(who_ref[1] == 0)
            def _():
                fill(quarter, (held.at[0:4], held.at[4:8]))

            @pl.when(who_ref[1] == 1)
            def _():
                fill(quarter, (held.at[4:8], held.at[0:4]))

            rows = pl.ds(quarter * 2 * part, 2 * part)
            copies.append(pltpu.make_async_copy(block.at[quarter], out_ref.at[rows, :], out_sems.at[quarter]))
            copies[-1].start()
        for copy in copies:
            copy.wait()


def mlp_place_kernel(
    who_ref, u_ref, b_ref, dh_ref, act_ref, *refs
):
    sources, (_, _, wide_ref, down_ref, held, dws, dvs, sems, out_sems) = refs[:8], refs[8:]
    size = dws.shape[1]
    part = size // 4

    @pl.when(who_ref[0] == 2)
    def _():
        dvs[0] = jnp.zeros_like(dvs[0])
        copies = fetch([dvs.at[0]] * 4, [down_ref.at[pl.ds(k * size, size), :] for k in range(4)], out_sems)
        for copy in copies:
            copy.start()
        for copy in copies:
            copy.wait()

    @pl.when(who_ref[0] == 1)
    def _():
        waits = fetch(sources, [held.at[k // 4, k % 4] for k in range(8)], sems)
        for copy in waits:
            copy.start()
        copies = []
        for relative in range(4):
            at = pl.ds(pl.multiple_of((who_ref[2] ^ relative) * size, size), size)
            dws[relative] = mm(u_ref[...], dh_ref[:, at], TN)
            dvs[relative] = mm(act_ref[:, at], b_ref[...], TN)
            if relative < 2:
                wait(*waits[4 * relative : 4 * relative + 4])
            for quarter in range(4):
                piece = held.at[relative % 2, quarter, relative // 2]
                rows = slice(quarter * part, (quarter + 1) * part)
                dws[relative, rows, :] += piece[:part, :].astype(F32)
                dvs[relative, rows, :] += piece[part:, :].astype(F32)
            for k, (source, target) in enumerate(
                ((dws.at[relative], wide_ref.at[:, at]), (dvs.at[relative], down_ref.at[at, :]))
            ):
                copies.append(pltpu.make_async_copy(source, target, out_sems.at[2 * relative + k]))
                copies[-1].start()
        for copy in copies:
            copy.wait()


VMEM = pl.BlockSpec(memory_space=pltpu.VMEM)
SMEM = pl.BlockSpec(memory_space=pltpu.SMEM)
ANY = pl.BlockSpec(memory_space=pl.ANY)
LIMIT = 58 * 2**20


def whole(shape):
    return pl.BlockSpec(shape, lambda i: (0,) * len(shape))


def estimate(microseconds):
    return pl.CostEstimate(flops=int(microseconds * 1.1e9), bytes_accessed=0, transcendentals=0)


def call(kernel, out_shapes, args, scratch=(), anywhere=0, scalars=0, outside=False, cost=1):
    return pl.pallas_call(
        kernel,
        grid=(1,),
        out_shape=[jax.ShapeDtypeStruct(*shape) for shape in out_shapes],
        in_specs=[SMEM] * scalars
        + [whole(arg.shape) for arg in args[scalars : len(args) - anywhere]]
        + [ANY] * anywhere,
        out_specs=[ANY if outside else whole(shape[0]) for shape in out_shapes],
        scratch_shapes=list(scratch),
        compiler_params=pltpu.CompilerParams(vmem_limit_bytes=LIMIT),
        cost_estimate=estimate(cost),
    )(*args)


def blank(shape, dtype=F32):
    return pl.pallas_call(lambda out_ref: None, out_shape=jax.ShapeDtypeStruct(shape, dtype), out_specs=ANY)()


def cls_mlp(mode, rows, grads, wide_w, down_w, vector):
    count = rows.shape[0]
    features, hidden = wide_w.shape
    tile = features
    wide_block = pl.BlockSpec((features, tile), lambda j: (0, j))
    down_block = pl.BlockSpec((tile, features), lambda j: (j, 0))
    sums = jax.ShapeDtypeStruct(vector.shape, F32)
    scratch = [pltpu.VMEM((count, features), BF)] + [pltpu.VMEM((count, features), F32)] * 2
    if mode == "weights":
        out_shape = [sums, jax.ShapeDtypeStruct(wide_w.shape, F32), jax.ShapeDtypeStruct(down_w.shape, F32)]
        out_specs = [whole(vector.shape), wide_block, down_block]
    elif mode == "factors":
        out_shape = [sums, jax.ShapeDtypeStruct((count, features), BF)] + [jax.ShapeDtypeStruct((count, hidden), BF)] * 2
        out_specs = [whole(vector.shape), whole((count, features))] + [pl.BlockSpec((count, tile), lambda j: (0, j))] * 2
        scratch = scratch[1:]
    else:
        out_shape = [jax.ShapeDtypeStruct(rows.shape, BF)]
        out_specs = [whole(rows.shape)]
    return pl.pallas_call(
        partial(cls_mlp_kernel, mode),
        grid=(hidden // tile,),
        in_specs=[whole(rows.shape), whole(grads.shape), wide_block, down_block, whole(vector.shape)],
        out_specs=out_specs,
        out_shape=out_shape,
        scratch_shapes=scratch,
        compiler_params=pltpu.CompilerParams(vmem_limit_bytes=LIMIT),
    )(rows, grads, wide_w, down_w, vector)


def cls_att_weights(rows, grads, layout, wide_w, vector):
    count, features = rows.shape
    block = min(count, 128)
    by_row = lambda width: pl.BlockSpec((block, width), lambda i: (i, 0))
    return pl.pallas_call(
        partial(cls_att_bwd_kernel, True),
        grid=(count // block,),
        in_specs=[
            by_row(features), by_row(features), by_row(128), by_row(128),
            pl.BlockSpec((1, block), lambda i: (0, i)), whole(wide_w.shape), whole(vector.shape),
        ],
        out_specs=[whole(vector.shape), whole(wide_w.shape)],
        out_shape=[jax.ShapeDtypeStruct(vector.shape, F32), jax.ShapeDtypeStruct(wide_w.shape, F32)],
        compiler_params=pltpu.CompilerParams(vmem_limit_bytes=LIMIT),
    )(rows, grads, *layout, wide_w, vector)


def documents(counts):
    ends = jnp.cumsum(counts, -1)
    places = jnp.arange(SEGS, dtype=jnp.int32)
    doc = jnp.sum((places[:, None] >= ends[..., None, :]).astype(jnp.int32), -1)
    slots = jnp.arange(counts.shape[-1], dtype=jnp.int32)
    first = jnp.sum(jnp.where(doc[..., None] == slots, (ends - counts)[..., None, :], 0), -1)
    return doc, places - first


def row_layout(counts):
    doc, pos = documents(counts)
    packs = counts.shape[0]
    label = doc + jnp.arange(packs, dtype=jnp.int32)[:, None] * (counts.shape[1] + 1)
    return wide_column(pos), wide_column(label), label.reshape(1, -1)


def wide_column(values):
    return jnp.broadcast_to(values.reshape(-1, 1), (values.size, 128))


def local(inputs, cotangent, wide, down, vectors, seg_counts):
    sections = lax.axis_size("section")
    replicas = lax.axis_size("dp")
    section = lax.axis_index("section")
    replica = lax.axis_index("dp")
    core, side = replica % 2, replica // 2 % 2
    rows, features = inputs.shape[1:]
    half = features // 2
    wide_w, down_w, vector = wide[0], down[0], vectors[0]
    x, cot = inputs[0], cotangent[0]

    fourth = 2 * side + core
    who = jnp.stack([section, core, fourth]).astype(jnp.int32)
    att_part, mlp_part = pl.pallas_call(
        parts_kernel,
        out_shape=[jax.ShapeDtypeStruct((2 * features, features), BF)] * 2,
        in_specs=[SMEM, ANY, ANY],
        out_specs=[VMEM, VMEM],
        scratch_shapes=[pltpu.SemaphoreType.DMA((7,))],
        compiler_params=pltpu.CompilerParams(vmem_limit_bytes=LIMIT),
    )(who, wide_w, down_w)
    att_first = send(att_part, ATT_WAYS, 0, 1)
    near = [swap_section(vector, bits) for bits in (1, 2, 3)]
    mlp_first = send(mlp_part, MLP_WAYS, 0, 1)
    x_sib = swap_core(x)
    every_vector = jnp.stack([vector] + near)
    avec, mvec = pick(every_vector, section), pick(every_vector, section ^ 1)
    att_second = send(after(att_part, every_vector, mlp_first), ATT_WAYS, 0, 2)
    att_last = send(att_first, ATT_WAYS, 1, 3)
    mlp_second = send(after(mlp_part, every_vector, att_first, x_sib), MLP_WAYS, 0, 2)
    mlp_last = send(after(mlp_first, att_first), MLP_WAYS, 1, 3)

    grid = lambda values: values.reshape(-1, SEG, features)
    heads = lambda values: grid(values)[:, 0]
    count = sections * (rows // SEG)
    is_cls = (jnp.arange(rows) % SEG == 0)[:, None]
    b_own = after(jnp.where(is_cls, jnp.zeros_like(cot), cot), every_vector)
    b_next = swap_dp(b_own, 2)
    b_sib, b_far = swap_core(b_own), swap_core(b_next)
    layout = row_layout(seg_counts[0])

    bf = lambda *shape: (shape, BF)
    att_who = jnp.stack([place_of(ATT_WAYS, section, core), section]).astype(jnp.int32)
    att_choices = [att_part, att_first, att_second, att_last]
    att_weights = [pltpu.VMEM((features, 3 * half), BF), pltpu.VMEM((half, features), BF)]
    triple, a, give0, keep0 = call(
        att_fwd_kernel,
        [bf(2 * rows, 3 * half), bf(2 * rows, half), bf(rows, features), bf(rows, features)],
        [att_who, after(x, b_sib, b_far), x_sib, avec, *att_choices],
        att_weights
        + [pltpu.VMEM((2, rows, 3 * half), BF), pltpu.VMEM((2, rows, half), BF), pltpu.VMEM((2, rows, features), BF)]
        + [pltpu.SemaphoreType.DMA((10,))],
        scalars=1,
        anywhere=4,
        outside=True,
    )
    core0 = swap_core(give0)

    def hop(values, start, end):
        return permute(values, lambda s, r: (end, r), lambda s, r: s == start)

    def on(column, run):
        return lax.cond(section == column, lambda: run()[0], lambda: jnp.zeros((count, 2 * features), BF))

    branch = heads(keep0).astype(F32) + heads(core0).astype(F32)
    cls1_own = (heads(x).astype(F32) + branch + avec[2:3]).astype(BF)
    cls1 = jnp.concatenate(to_column(jnp.concatenate([cls1_own, heads(cot)], 1), 1), 0)
    h1, u_own = call(att_join_kernel, [bf(rows, features)] * 2, [x, keep0, after(core0, cls1_own), avec, mvec])
    u_own = after(u_own, cls1)
    u_next, u_sib = swap_dp(u_own, 2), swap_core(u_own)
    cls2 = on(1, lambda: cls_mlp("out", cls1, cls1, wide_w, down_w, vector))
    cls2_at2 = hop(cls2, 1, 2)

    square = bf(features, features)
    scratch = [pltpu.VMEM((2 * rows, features), BF)] * 4 + [pltpu.VMEM(*square)] * 2
    scratch += [pltpu.VMEM((2, 2 * rows, features), BF)] + [pltpu.VMEM((2, features, features), BF)] * 2
    scratch += [pltpu.SemaphoreType.DMA((18,))]
    mlp_who = jnp.stack([place_of(MLP_WAYS, section, core), section // 2]).astype(jnp.int32)
    mlp_choices = [mlp_part, mlp_first, mlp_second, mlp_last]
    keep1, give1, dw, dv = call(
        partial(mlp_kernel, False),
        [bf(2 * rows, features)] * 2 + [square] * 2,
        [mlp_who, after(u_own, cls2), u_sib, b_own, b_sib, *mlp_choices],
        scratch,
        scalars=1,
        anywhere=8,
        outside=True,
    )
    u_far = swap_core(after(u_next, dw))
    keep2, give2, near_half, far_half = call(
        partial(mlp_kernel, True),
        [bf(2 * rows, features)] * 2 + [bf(2, half, features)] * 2,
        [mlp_who, after(u_next, cls2_at2), u_far, b_next, b_far, *mlp_choices, dw, dv],
        scratch,
        scalars=1,
        anywhere=10,
        outside=True,
    )
    core1, core2 = swap_core(give1), swap_core(give2)

    shape = [bf(count, 2 * features)]
    near_row = swap_section(far_half, 2)
    cls2_at2 = after(cls2_at2, far_half)
    cls3 = on(2, lambda: call(cls_att_fwd_kernel, shape, [cls2_at2, *layout, wide_w, vector]))
    cls3_at3 = hop(cls3, 2, 3)
    dcls3 = on(3, lambda: cls_mlp("both", cls3_at3, cls3_at3, wide_w, down_w, vector))
    dcls3_at2 = hop(dcls3, 3, 2)
    pair = pair_sum(keep2, after(core2, cls3))
    du_next = swap_dp(pair[:rows], 2)
    dcls2 = on(
        2, lambda: call(partial(cls_att_bwd_kernel, False), shape, [cls2_at2, dcls3_at2, *layout, wide_w, vector])
    )
    dh1, mlp_small = call(
        mlp_done_kernel,
        [bf(rows, features), ((8, features), F32)],
        [h1, b_own, keep1, core1, du_next, mvec],
    )
    dcls2_at1 = after(hop(dcls2, 2, 1), dh1, near_row)
    out_next = swap_dp(after(pair[rows:], du_next), 2)
    dcls1 = on(1, lambda: cls_mlp("back", cls1, dcls2_at1, wide_w, down_w, vector))

    mine_in = jnp.where(section == 1, cls1, jnp.where(section == 2, cls2_at2, cls3_at3))
    mine_grad = jnp.where(section == 1, dcls2_at1[:, :features], dcls3_at2[:, :features])
    mine_grad = jnp.where(section == 3, cls3_at3[:, features:], mine_grad)
    marks = jnp.pad(jnp.concatenate([layout[0][:, :1], layout[1][:, :1] % (SEGS + 1)], 1), ((0, 0), (0, features - 2)))
    everything = jnp.concatenate([mine_in[:, :features], mine_grad, marks.astype(BF)], 0)
    split = dcls1.reshape(sections, rows // SEG, 2 * features)
    arrived = [hop(split[1 ^ bits], 1, 1 ^ bits) for bits in (1, 2, 3)]
    back_rows = jnp.where(section == 1, split[1], arrived[0] + arrived[1] + arrived[2])

    place = lambda values, cls: lax.dynamic_update_slice(grid(values), cls[:, None], (0, 0, 0)).reshape(rows, features)
    dh1 = place(dh1, back_rows[:, :features])
    dh1_sib = swap_core(dh1)


    xbit = section % 2
    mlp_half = pair_sum(near_half, near_row)
    near_block = swap_section(after(pick(mlp_half, 1 - xbit), back_rows), 1)
    mlp_block = pair_sum(pick(mlp_half, xbit), near_block)
    mlp_sum, bits = mlp_block, 4
    while bits < replicas:
        other = swap_dp(jnp.concatenate([mlp_sum, everything], 0), bits)
        mlp_sum = pair_sum(mlp_sum, other[:half])
        everything = ordered(everything, other[half:], replica & bits != 0)
        bits *= 2

    *att_grads, du0_own, du0_sib = call(
        att_bwd_kernel,
        [bf(half + 16, features)] * 4 + [bf(rows, features)] * 2,
        [att_who, avec, mlp_small, after(x, out_next, mlp_block), x_sib, dh1, dh1_sib, triple, a, *att_choices],
        [pltpu.VMEM((2 * rows, features), BF)] * 2
        + [pltpu.VMEM((2 * rows, 3 * half), BF), pltpu.VMEM((2 * rows, half), BF), *att_weights]
        + [pltpu.VMEM((2 * rows, features), BF), pltpu.VMEM((2 * rows, 3 * half), BF)]
        + [pltpu.VMEM((2, rows, features), BF), pltpu.VMEM((4, half + 16, features), BF)]
        + [pltpu.SemaphoreType.DMA((26,))],
        scalars=1,
        anywhere=10,
        outside=True,
        cost=17,
    )
    du0_core = swap_core(du0_sib)
    (input_grad,) = call(att_done_kernel, [bf(rows, features)], [x, dh1, du0_own, du0_core, avec])

    branch = keep1[rows:].astype(F32) + core1[rows:].astype(F32) + out_next.astype(F32)
    h2 = (h1.astype(F32) + branch + mvec[2:3]).astype(BF)
    layer_out = place(h2, back_rows[:, features:])
    other = swap_dp(jnp.concatenate([mlp_sum, everything], 0), 2)
    mlp_next, everything = other[:half], ordered(everything, other[half:], replica & 2 != 0)
    everything = ordered(everything, swap_core(everything), replica & 1 != 0).reshape(-1, 3, count, features)
    received, layer_out, input_grad = lax.optimization_barrier((section_parts(att_grads), layer_out, input_grad))
    att_block = section_sum(att_grads, received)
    mlp_blocks = jnp.stack(after([mlp_sum, mlp_next], att_block))
    att_block = pair_sum(att_block, swap_dp(att_block, 2))
    all_in, all_grad, marks = [everything[:, k].reshape(-1, features) for k in range(3)]
    all_pos, all_doc = marks[:, :1].astype(jnp.int32), marks[:, 1:2].astype(jnp.int32)
    all_doc += jnp.arange(all_doc.shape[0], dtype=jnp.int32)[:, None] // SEGS * (SEGS + 1)
    all_layout = (wide_column(all_pos), wide_column(all_doc), all_doc.reshape(1, -1))
    total = all_in.shape[0]
    none = lambda: [blank((total, features), BF)] + [blank((total, wide_w.shape[1]), BF) for _ in range(2)]

    def first_column():
        return [jnp.zeros(vector.shape, F32), blank(wide_w.shape), jnp.zeros(down_w.shape, F32), *none()]

    def second_column():
        sums, *factors = cls_mlp("factors", all_in, all_grad, wide_w, down_w, vector)
        return [sums, blank(wide_w.shape), blank(down_w.shape), *factors]

    def third_column():
        sums, wide_sum = cls_att_weights(all_in, all_grad, all_layout, wide_w, vector)
        return [sums, wide_sum, blank(down_w.shape), *none()]

    def fourth_column():
        return [*cls_mlp("weights", all_in, all_grad, wide_w, down_w, vector), *none()]

    vector_sum, wide_sum, down_sum, u_cls, dh_cls, act_cls = lax.switch(
        section, [first_column, second_column, third_column, fourth_column]
    )
    mlp_own = to_column(mlp_blocks, 1)
    att_block = pair_sum(att_block, after(swap_dp(att_block, 4), u_cls, mlp_own))
    att_block = dp_sum(att_block, 8)
    small = att_block[half:]
    small = (small.astype(F32) + swap_core(small).astype(F32))[:3]
    mine_small = jnp.where(section < 2, small, 0.0)
    vector_sum = vector_sum + jnp.pad(mine_small, ((0, vector.shape[0] - 3), (0, 0)))
    att_own, vector_sum = lax.optimization_barrier((to_column(att_block[:half], 0), vector_sum))
    att_other = [swap_core(piece) for piece in att_own]
    mlp_own = after(mlp_own, att_own)
    mlp_other = [swap_core(piece) for piece in mlp_own]
    wide_like, down_like = jax.ShapeDtypeStruct(wide_w.shape, F32), jax.ShapeDtypeStruct(down_w.shape, F32)
    wide_sum = pl.pallas_call(
        att_place_kernel,
        out_shape=wide_like,
        in_specs=[SMEM] + [ANY] * 9,
        out_specs=ANY,
        scratch_shapes=[
            pltpu.VMEM((8, half, features), BF),
            pltpu.VMEM((4, features // 4, 4 * features), F32),
            pltpu.SemaphoreType.DMA((8,)),
            pltpu.SemaphoreType.DMA((4,)),
        ],
        input_output_aliases={9: 0},
        compiler_params=pltpu.CompilerParams(vmem_limit_bytes=LIMIT),
    )(who, *att_own, *att_other, wide_sum)
    wide_sum, down_sum = pl.pallas_call(
        mlp_place_kernel,
        out_shape=[wide_like, down_like],
        in_specs=[SMEM] + [VMEM] * 4 + [ANY] * 10,
        out_specs=[ANY, ANY],
        scratch_shapes=[
            pltpu.VMEM((2, 4, 2, half, features), BF),
            pltpu.VMEM((4, features, features), F32),
            pltpu.VMEM((4, features, features), F32),
            pltpu.SemaphoreType.DMA((8,)),
            pltpu.SemaphoreType.DMA((8,)),
        ],
        input_output_aliases={13: 0, 14: 1},
        compiler_params=pltpu.CompilerParams(vmem_limit_bytes=LIMIT),
    )(who, u_cls, all_grad, dh_cls, act_cls, *mlp_own, *mlp_other, wide_sum, down_sum)
    return layer_out[None], input_grad[None], wide_sum[None], down_sum[None], vector_sum[None]


def solution(mesh):
    return jax.shard_map(
        local,
        mesh=mesh,
        in_specs=(
            P("section", "dp", None),
            P("section", "dp", None),
            P("section", None, None),
            P("section", None, None),
            P("section", None, None),
            P("dp", None, None),
        ),
        out_specs=(
            P("section", "dp", None),
            P("section", "dp", None),
            P("section", None, None),
            P("section", None, None),
            P("section", None, None),
        ),
        check_vma=False,
    )
```

```python
from functools import partial

import jax
import jax.numpy as jnp
from jax import lax
from jax.experimental import pallas as pl
from jax.experimental.pallas import tpu as pltpu
from jax.sharding import PartitionSpec as P

HEADS = 12
SEG = 128
SEGS = 4
EPSILON = 1e-05
SCORE_SCALE = 0.125
MASKED = -1e30
AXES = ("section", "dp")
BF = jnp.bfloat16
F32 = jnp.float32

NN = (((1,), (0,)), ((), ()))
NT = (((1,), (1,)), ((), ()))
TN = (((0,), (0,)), ((), ()))

GELU_A = 0.7978845608028654
GELU_B = 0.044715

ATT_WAYS = ((0, 1, 2, 3), (0, 2, 1, 3))
MLP_WAYS = ((1, 0, 3, 2), (1, 3, 0, 2))


def mm(left, right, dims=NN):
    return lax.dot_general(left, right, dims, preferred_element_type=F32)


def permute(shard, move, keep=lambda s, r: True):
    sections, replicas = lax.axis_size("section"), lax.axis_size("dp")
    pairs = []
    for s in range(sections):
        for r in range(replicas):
            if keep(s, r):
                t, q = move(s, r)
                pairs.append((s * replicas + r, t * replicas + q))
    return lax.ppermute(shard, AXES, pairs)


def swap_core(shard):
    return permute(shard, lambda s, r: (s, r ^ 1))


def swap_section(shard, bits):
    return permute(shard, lambda s, r: (s ^ bits, r))


def swap_dp(shard, bits):
    return permute(shard, lambda s, r: (s, r ^ bits))


def send(values, ways, start, end):
    return permute(values, lambda s, r: (ways[r & 1][end], r), lambda s, r: ways[r & 1][start] == s)


def after(value, *marks):
    return lax.optimization_barrier((value, marks))[0]


def place_of(ways, section, core):
    position = jnp.int32(0)
    for c in range(2):
        for k, s in enumerate(ways[c]):
            position = jnp.where((section == s) & (core == c), k, position)
    return position


def pick(stack, index):
    return lax.dynamic_index_in_dim(stack, index, 0, keepdims=False)


def section_parts(parts):
    return [swap_section(parts[bits], bits) for bits in (1, 2, 3)]


def section_sum(parts, others=None):
    others = others or section_parts(parts)
    return sum([other.astype(F32) for other in others], parts[0].astype(F32)).astype(BF)


def dp_sum(value, bits):
    while bits < lax.axis_size("dp"):
        value = pair_sum(value, swap_dp(value, bits))
        bits *= 2
    return value


def pair_sum(mine, other):
    return (mine.astype(F32) + other.astype(F32)).astype(BF)


def ordered(first, second, swapped):
    return jnp.where(swapped, jnp.concatenate([second, first], 0), jnp.concatenate([first, second], 0))


def to_column(value, owner):
    arrived = [permute(value, lambda s, r: (owner, r), lambda s, r: s == owner ^ bits) for bits in (1, 2, 3)]
    columns = [None] * 4
    columns[owner] = value
    for bits, other in zip((1, 2, 3), arrived):
        columns[owner ^ bits] = other
    return columns


def fetch(sources, targets, sems):
    return [pltpu.make_async_copy(source, target, sems.at[i]) for i, (source, target) in enumerate(zip(sources, targets))]


def norm_parts(values):
    center = values - jnp.mean(values, -1, keepdims=True)
    spread = jnp.mean(center * center, -1, keepdims=True)
    scale = lax.rsqrt(spread + EPSILON)
    return center * scale, scale


def norm_rows(values, vec_ref):
    hat, _ = norm_parts(values)
    return hat * vec_ref[0:1, :] + vec_ref[1:2, :]


def norm_back(values, grad_normed, vec_ref):
    hat, scale = norm_parts(values)
    inner = grad_normed * vec_ref[0:1, :]
    first = jnp.mean(inner, -1, keepdims=True)
    second = jnp.mean(inner * hat, -1, keepdims=True)
    return scale * (inner - first - hat * second), grad_normed * hat


def column_sum(values):
    return jnp.sum(values, 0, keepdims=True)


def gelu_parts(hidden):
    square = hidden * hidden
    inner = GELU_A * hidden * (1.0 + GELU_B * square)
    t = jnp.tanh(inner)
    half = 0.5 * (1.0 + t)
    slope = half + 0.5 * hidden * (1.0 - t * t) * (GELU_A * (1.0 + 3.0 * GELU_B * square))
    return hidden * half, slope


def two_heads(pair):
    low = lax.broadcasted_iota(jnp.int32, pair.shape, 1) < 64
    zero = jnp.zeros_like(pair)
    return jnp.concatenate([jnp.where(low, pair, zero), jnp.where(low, zero, pair)], 0)


def join_heads(both):
    rows = both.shape[0] // 2
    low = lax.broadcasted_iota(jnp.int32, (rows, both.shape[1]), 1) < 64
    return jnp.where(low, both[:rows], both[rows:])


def softmax_rows(scores):
    powers = jnp.exp(scores - jnp.max(scores, -1, keepdims=True))
    return powers / jnp.sum(powers, -1, keepdims=True)


def softmax_columns(scores):
    powers = jnp.exp(scores - jnp.max(scores, 0, keepdims=True))
    return powers * (1.0 / jnp.sum(powers, 0, keepdims=True))


def head_pairs(q, k, v, out):
    for seg in range(q.shape[0] // SEG):
        at = slice(seg * SEG, (seg + 1) * SEG)
        mixed = []
        for pair in range(q.shape[1] // 128):
            lanes = slice(pair * 128, (pair + 1) * 128)
            probs = softmax_columns(mm(k[at, lanes], two_heads(q[at, lanes]), NT) * SCORE_SCALE)
            mixed.append(join_heads(mm(probs.astype(BF), v[at, lanes], TN)).astype(BF))
        out.append(jnp.concatenate(mixed, 1))


class Copies:
    def __init__(self, sems):
        self.sems, self.used = sems, 0

    def next(self):
        self.used += 1
        return self.sems.at[self.used - 1]

    def start(self, source, target):
        sem = self.next()
        send_parts(source, target, sem)
        return pltpu.make_async_copy(source, target, sem)

    def choose(self, which, sources, target):
        sem = self.next()
        for k, source in enumerate(sources):

            @pl.when(which == k)
            def _():
                send_parts(source, target, sem)

        return pltpu.make_async_copy(sources[0], target, sem)


def send_parts(source, target, sem):
    rows = source.shape[0]
    step = rows // 4 if rows % 64 == 0 else rows
    for start in range(0, rows, step):
        part = pl.ds(start, step)
        pltpu.make_async_copy(source.at[part], target.at[part], sem).start()


def wait(*copies):
    for copy in copies:
        copy.wait()


def load_triple(copies, place, choices, wt, half):
    features, left, right = wt.shape[0], pl.ds(0, half), pl.ds(half, half)
    return [
        copies.choose(place, [c.at[pl.ds(0, features), :] for c in choices], wt.at[:, pl.ds(0, features)]),
        copies.choose(place, [c.at[pl.ds(features, half), left] for c in choices], wt.at[left, pl.ds(features, half)]),
        copies.choose(place, [c.at[pl.ds(features, half), right] for c in choices], wt.at[right, pl.ds(features, half)]),
    ]


def att_fwd_kernel(place_ref, own_ref, sib_ref, vec_ref, *refs):
    choices, (triple_ref, a_ref, give_ref, keep_ref, wt, wo, triples, mixes, outs, sems) = refs[:4], refs[4:]
    rows, features = own_ref.shape
    half = a_ref.shape[1]
    copies = Copies(sems)
    wt_in = load_triple(copies, place_ref[0], choices, wt, half)
    wo_in = [copies.choose(place_ref[0], [c.at[pl.ds(features + half, half), :] for c in choices], wo)]
    done = []
    for pack, (ref, out) in enumerate(((sib_ref, give_ref), (own_ref, keep_ref))):
        span = pl.ds((1 - pack) * rows, rows)
        u = norm_rows(ref[...].astype(F32), vec_ref).astype(BF)
        if pack == 0:
            wait(*wt_in)
        triple = mm(u, wt[...]).astype(BF)
        triples[pack] = triple
        done.append(copies.start(triples.at[pack], triple_ref.at[span, :]))
        mixed = []
        head_pairs(triple[:, :half], triple[:, half : 2 * half], triple[:, 2 * half :], mixed)
        a = jnp.concatenate(mixed, 0)
        mixes[pack] = a
        done.append(copies.start(mixes.at[pack], a_ref.at[span, :]))
        if pack == 0:
            wait(*wo_in)
        outs[pack] = mm(a, wo[...]).astype(BF)
        done.append(copies.start(outs.at[pack], out))
    wait(*done)


def att_bwd_kernel(place_ref, vec_ref, small_ref, *refs):
    own_ref, sib_ref, gown_ref, gsib_ref, triple_ref, a_ref, *choices = refs[:10]
    grad_refs, (duown_ref, dusib_ref, xs, gs, triple, mixes, wt, wo, u, dt, dus, piece, sems) = refs[10:14], refs[14:]
    rows = own_ref.shape[0]
    half = a_ref.shape[1]
    part = half // 4
    copies = Copies(sems)
    gs_in = [copies.start(gown_ref, gs.at[pl.ds(0, rows), :])]
    early = copies.choose(place_ref[0], [c.at[pl.ds(wt.shape[0] + half, half), :] for c in choices], wo)
    triple_in = [copies.start(triple_ref.at[pl.ds(k * rows, rows), :], triple.at[pl.ds(k * rows, rows), :]) for k in range(2)]
    xs_in = [copies.start(own_ref, xs.at[pl.ds(0, rows), :])]
    wt_in = load_triple(copies, place_ref[0], choices, wt, half)
    gs_in.append(copies.start(gsib_ref, gs.at[pl.ds(rows, rows), :]))
    xs_in.append(copies.start(sib_ref, xs.at[pl.ds(rows, rows), :]))
    a_in = copies.start(a_ref, mixes)
    done = []
    gain = shift = 0.0
    for pack, out in enumerate((duown_ref, dusib_ref)):
        span = slice(pack * rows, (pack + 1) * rows)
        wait(gs_in[pack])
        if pack == 0:
            wait(early)
        da = mm(gs[span, :], wo[...], NT).astype(BF)
        wait(triple_in[pack])
        for seg in range(rows // SEG):
            at = slice(seg * SEG, (seg + 1) * SEG)
            to = slice(pack * rows + seg * SEG, pack * rows + (seg + 1) * SEG)
            for pair in range(half // 128):
                lanes = [slice(kind * half + pair * 128, kind * half + (pair + 1) * 128) for kind in range(3)]
                q2, k, v = two_heads(triple[to, lanes[0]]), triple[to, lanes[1]], triple[to, lanes[2]]
                da2 = two_heads(da[at, lanes[0]])
                probs = softmax_columns(mm(k, q2, NT) * SCORE_SCALE)
                dy = mm(v, da2, NT)
                ds = (probs * (dy - jnp.sum(dy * probs, 0, keepdims=True))).astype(BF)
                dt[to, lanes[2]] = mm(probs.astype(BF), da2).astype(BF)
                dt[to, lanes[0]] = (join_heads(mm(ds, k, TN)) * SCORE_SCALE).astype(BF)
                dt[to, lanes[1]] = (mm(ds, q2) * SCORE_SCALE).astype(BF)
        wait(xs_in[pack])
        hat, _ = norm_parts(xs[span, :].astype(F32))
        u[span, :] = (hat * vec_ref[0:1, :] + vec_ref[1:2, :]).astype(BF)
        if pack == 0:
            wait(*wt_in)
        du = mm(dt[span, :], wt[...], NT)
        dus[pack] = du.astype(BF)
        done.append(copies.start(dus.at[pack], out))
        gain = gain + column_sum(du * hat)
        shift = shift + column_sum(du)

    def send(start, count):
        at = pl.ds(start, count)
        for bits, ref in enumerate(grad_refs):
            done.append(copies.start(piece.at[place_ref[1] ^ bits, at, :], ref.at[at, :]))

    dw = mm(u[...], dt[:, : 2 * half], TN)
    for quarter in range(4):
        piece[quarter, : 2 * part, :] = dw[quarter * 2 * part : (quarter + 1) * 2 * part, :].astype(BF)
    send(0, 2 * part)
    dw = mm(u[...], dt[:, 2 * half :], TN)
    for quarter in range(4):
        for side in range(2):
            piece[quarter, 2 * part : 3 * part, side * half : (side + 1) * half] = dw[
                side * half + quarter * part : side * half + (quarter + 1) * part, :
            ].astype(BF)
    send(2 * part, part)
    wait(a_in)
    dw = mm(mixes[...], gs[...], TN)
    piece[:, 4 * part :, :] = jnp.zeros((4, 16, piece.shape[2]), BF)
    rest = jnp.zeros((13, piece.shape[2]), F32)
    sums = [gain, shift, column_sum(gs[:rows, :].astype(F32)), rest]
    piece[0, 4 * part :, :] = jnp.concatenate(sums, 0).astype(BF)
    piece[1, 4 * part :, :] = jnp.concatenate([small_ref[...], small_ref[...]], 0).astype(BF)
    for quarter in range(4):
        piece[quarter, 3 * part : 4 * part, :] = dw[quarter * part : (quarter + 1) * part, :].astype(BF)
    send(3 * part, part + 16)
    wait(*done)


def att_done_kernel(x_ref, g_ref, duown_ref, dusib_ref, vec_ref, out_ref):
    du = duown_ref[...].astype(F32) + dusib_ref[...].astype(F32)
    back, _ = norm_back(x_ref[...].astype(F32), du, vec_ref)
    out_ref[...] = (g_ref[...].astype(F32) + back).astype(BF)


def att_join_kernel(x_ref, keep_ref, core_ref, avec_ref, mvec_ref, h_ref, u_ref):
    branch = keep_ref[...].astype(F32) + core_ref[...].astype(F32)
    out = (x_ref[...].astype(F32) + branch + avec_ref[2:3, :]).astype(BF)
    h_ref[...] = out
    u_ref[...] = norm_rows(out.astype(F32), mvec_ref).astype(BF)


def mlp_kernel(last, who_ref, *refs):
    uown_ref, usib_ref, bown_ref, bsib_ref, *choices = refs[:8]
    before, refs = refs[8 : 10 if last else 8], refs[10 if last else 8 :]
    keep_ref, give_ref, first_ref, second_ref, u, b, act, dhs, w, v, outs, dws, held, sems = refs
    rows = uown_ref.shape[0]
    size = w.shape[0]
    copies = Copies(sems)
    us_in, bs_in, done = [None, None], [None, None], []
    us_in[1] = copies.start(usib_ref, u.at[pl.ds(rows, rows), :])
    w_in = copies.choose(who_ref[0], [c.at[pl.ds(0, size), :] for c in choices], w)
    bs_in[1] = copies.start(bsib_ref, b.at[pl.ds(rows, rows), :])
    v_in = copies.choose(who_ref[0], [c.at[pl.ds(size, size), :] for c in choices], v)
    for pack, out in ((1, give_ref), (0, keep_ref)):
        at = slice(pack * rows, (pack + 1) * rows)
        wait(us_in[pack])
        if pack == 1:
            wait(w_in)
            us_in[0] = copies.start(uown_ref, u.at[pl.ds(0, rows), :])
            bs_in[0] = copies.start(bown_ref, b.at[pl.ds(0, rows), :])
        active, slope = gelu_parts(mm(u[at, :], w[...]))
        act[at, :] = active.astype(BF)
        wait(bs_in[pack])
        if pack == 1:
            wait(v_in)
            before_in = [copies.start(ref, held.at[k]) for k, ref in enumerate(before)]
        dhs[at, :] = (mm(b[at, :], v[...], NT) * slope).astype(BF)
        outs[pack, :rows, :] = mm(dhs[at, :], w[...], NT).astype(BF)
        outs[pack, rows:, :] = mm(act[at, :], v[...]).astype(BF)
        done.append(copies.start(outs.at[pack], out))
    quarter = size // 4
    for kind, (left, right) in enumerate(((u, dhs), (act, b))):
        dw = mm(left[...], right[...], TN)
        if not last:
            dws[kind] = dw.astype(BF)
            done.append(copies.start(dws.at[kind], (first_ref, second_ref)[kind]))
            continue
        wait(before_in[kind])
        dws[kind] = (dw + held[kind].astype(F32)).astype(BF)
        for k in range(2):
            sem = copies.next()
            target = (first_ref, second_ref)[k].at[:, pl.ds(kind * quarter, quarter), :]
            for y in range(2):
                source = dws.at[kind, pl.ds((y ^ k) * 2 * quarter, 2 * quarter), :].reshape(2, quarter, size)

                @pl.when(who_ref[1] == y)
                def _():
                    pltpu.make_async_copy(source, target, sem).start()

            done.append(pltpu.make_async_copy(source, target, sem))
    wait(*done)


def mlp_done_kernel(h_ref, b_ref, keep_ref, core_ref, z_ref, vec_ref, grad_ref, small_ref):
    rows = h_ref.shape[0]
    du = keep_ref[:rows, :].astype(F32) + core_ref[:rows, :].astype(F32) + z_ref[...].astype(F32)
    grad = b_ref[...].astype(F32)
    back, gain = norm_back(h_ref[...].astype(F32), du, vec_ref)
    grad_ref[...] = (grad + back).astype(BF)
    small_ref[...] = jnp.zeros_like(small_ref)
    small_ref[0:1, :] = column_sum(gain)
    small_ref[1:2, :] = column_sum(du)
    small_ref[2:3, :] = column_sum(grad)


def cls_step_kernel(mode, h_ref, b_ref, vec_ref, w_ref, v_ref, out_ref, w, v, sems):
    forward, backward = mode in ("out", "both"), mode in ("back", "both")
    features, hidden = w_ref.shape
    copies = Copies(sems)
    spans = [slice(start, start + features) for start in range(0, hidden, features)]
    loads = []
    for span in spans:
        at = pl.ds(span.start, features)
        loads.append((copies.start(w_ref.at[:, at], w.at[:, at]), copies.start(v_ref.at[at, :], v.at[at, :])))
    values = h_ref[:, :features].astype(F32)
    u = norm_rows(values, vec_ref).astype(BF)
    b = b_ref[:, -features:] if mode == "both" else b_ref[:, :features]
    out = du = 0.0
    for span, (w_in, v_in) in zip(spans, loads):
        w_in.wait()
        active, slope = gelu_parts(mm(u, w[:, span]))
        v_in.wait()
        if forward:
            out = out + mm(active.astype(BF), v[span, :])
        if backward:
            dh = (mm(b, v[span, :], NT) * slope).astype(BF)
            du = du + mm(dh, w[:, span], NT)
    if forward:
        out = (values + out + vec_ref[2:3, :]).astype(BF)
    if backward:
        back, _ = norm_back(values, du, vec_ref)
        back = (b.astype(F32) + back).astype(BF)
    out_ref[:, :features] = back if backward else out
    out_ref[:, features:] = {"out": h_ref, "back": b_ref}[mode][:, features:] if mode != "both" else out


def cls_mlp_kernel(mode, h_ref, b_ref, w_ref, v_ref, vec_ref, *refs):
    features = w_ref.shape[0]
    forward, backward = mode in ("out", "both"), mode in ("back", "both")
    weights, factors = mode == "weights", mode == "factors"
    j = pl.program_id(0)
    if weights:
        small_ref, dw_ref, dv_ref, u_ref, out_acc, du_acc = refs
    elif factors:
        small_ref, u_ref, dh_ref, act_ref, out_acc, du_acc = refs
    else:
        out_ref, u_ref, out_acc, du_acc = refs

    @pl.when(j == 0)
    def _():
        u_ref[...] = norm_rows(h_ref[:, :features].astype(F32), vec_ref).astype(BF)
        out_acc[...] = jnp.zeros_like(out_acc)
        du_acc[...] = jnp.zeros_like(du_acc)

    u = u_ref[...]
    active, slope = gelu_parts(mm(u, w_ref[...]))
    active = active.astype(BF)
    if forward:
        out_acc[...] += mm(active, v_ref[...])
    if not forward or backward:
        b = b_ref[:, -features:] if mode == "both" else b_ref[:, :features]
        dh = (mm(b, v_ref[...], NT) * slope).astype(BF)
        du_acc[...] += mm(dh, w_ref[...], NT)
    if weights:
        dw_ref[...] = mm(u, dh, TN)
        dv_ref[...] = mm(active, b, TN)
    if factors:
        dh_ref[...] = dh
        act_ref[...] = active

    @pl.when(j == pl.num_programs(0) - 1)
    def _():
        values = h_ref[:, :features].astype(F32)
        if forward:
            out = (values + out_acc[...] + vec_ref[2:3, :]).astype(BF)
        if not forward or backward:
            grad = b.astype(F32)
            back, gain = norm_back(values, du_acc[...], vec_ref)
            back = (grad + back).astype(BF)
        if mode == "out":
            out_ref[:, :features] = out
            out_ref[:, features:] = h_ref[:, features:]
        if mode == "both":
            out_ref[:, :features] = back
            out_ref[:, features:] = out
        if mode == "back":
            out_ref[:, :features] = back
            out_ref[:, features:] = b_ref[:, features:]
        if weights or factors:
            small_ref[...] = jnp.zeros_like(small_ref)
            small_ref[0:1, :] = column_sum(gain)
            small_ref[1:2, :] = column_sum(du_acc[...])
            small_ref[2:3, :] = column_sum(grad)


def lifted_rows(h_ref, pos_ref, vec_ref):
    values = h_ref[:, : vec_ref.shape[1]].astype(F32)
    pos = pos_ref[:, :1]
    for p in range(SEGS):
        values = values + jnp.where(pos == p, vec_ref[3 + p : 4 + p, :], 0.0)
    return values


def cls_att_heads(triple, col_ref, row_ref):
    features = triple.shape[1] // 3
    column = jnp.concatenate([col_ref[:, :1], col_ref[:, :1]], 0)
    mask = column == row_ref[...]
    probs, mixed = [], []
    for pair in range(features // 128):
        lanes = slice(pair * 128, (pair + 1) * 128)
        q2 = two_heads(triple[:, lanes])
        k = triple[:, features + pair * 128 : features + (pair + 1) * 128]
        v = triple[:, 2 * features + pair * 128 : 2 * features + (pair + 1) * 128]
        scores = jnp.where(mask, mm(q2, k, NT) * SCORE_SCALE, MASKED)
        probs.append(softmax_rows(scores))
        mixed.append(join_heads(mm(probs[-1].astype(BF), v)).astype(BF))
    return probs, jnp.concatenate(mixed, 1)


def cls_att_fwd_kernel(h_ref, pos_ref, col_ref, row_ref, w_ref, vec_ref, out_ref, triple_ref, w, sems):
    features = vec_ref.shape[1]
    copies = Copies(sems)
    parts = [pl.ds(k * features, features) for k in range(4)]
    loads = [copies.start(w_ref.at[:, part], w.at[:, part]) for part in parts]
    values = lifted_rows(h_ref, pos_ref, vec_ref)
    u = norm_rows(values, vec_ref).astype(BF)
    for part, load in zip(parts[:3], loads):
        load.wait()
        triple_ref[:, part] = mm(u, w[:, part]).astype(BF)
    _, mixed = cls_att_heads(triple_ref[...], col_ref, row_ref)
    loads[3].wait()
    out_ref[:, :features] = (values + mm(mixed, w[:, 3 * features :]) + vec_ref[2:3, :]).astype(BF)
    out_ref[:, features:] = h_ref[:, features:]


def cls_att_bwd_kernel(weights_too, h_ref, g_ref, *refs):
    if weights_too:
        pos_ref, col_ref, row_ref, w_ref, vec_ref, *refs = refs
    else:
        triple_ref, pos_ref, col_ref, row_ref, source_ref, vec_ref, out_ref, w_ref, sems = refs
        features = vec_ref.shape[1]
        copies = Copies(sems)
        parts = [pl.ds(k * features, features) for k in (3, 0, 1, 2)]
        loads = [copies.start(source_ref.at[:, part], w_ref.at[:, part]) for part in parts]
    values = lifted_rows(h_ref, pos_ref, vec_ref)
    features = values.shape[1]
    if weights_too:
        u = norm_rows(values, vec_ref).astype(BF)
        triple = mm(u, w_ref[:, : 3 * features]).astype(BF)
    else:
        triple = triple_ref[...]
    probs, mixed = cls_att_heads(triple, col_ref, row_ref)
    b = g_ref[:, :features]
    if not weights_too:
        wait(loads[0])
    da = mm(b, w_ref[:, 3 * features :], NT).astype(BF)
    dqs, dks, dvs = [], [], []
    for pair in range(features // 128):
        lanes = slice(pair * 128, (pair + 1) * 128)
        q2 = two_heads(triple[:, lanes])
        k = triple[:, features + pair * 128 : features + (pair + 1) * 128]
        v = triple[:, 2 * features + pair * 128 : 2 * features + (pair + 1) * 128]
        da2 = two_heads(da[:, lanes])
        y = probs[pair]
        dy = mm(da2, v, NT)
        ds = (y * (dy - jnp.sum(dy * y, -1, keepdims=True))).astype(BF)
        dvs.append(mm(y.astype(BF), da2, TN).astype(BF))
        dqs.append((join_heads(mm(ds, k)) * SCORE_SCALE).astype(BF))
        dks.append((mm(ds, q2, TN) * SCORE_SCALE).astype(BF))
    dtriple = jnp.concatenate(dqs + dks + dvs, 1)
    if not weights_too:
        wait(*loads[1:])
    du = mm(dtriple, w_ref[:, : 3 * features], NT)
    back, gain = norm_back(values, du, vec_ref)
    grad = b.astype(F32)
    total = grad + back
    if weights_too:
        small_ref, dw_ref = refs

        @pl.when(pl.program_id(0) == 0)
        def _():
            small_ref[...] = jnp.zeros_like(small_ref)
            dw_ref[...] = jnp.zeros_like(dw_ref)

        small_ref[0:1, :] += column_sum(gain)
        small_ref[1:2, :] += column_sum(du)
        small_ref[2:3, :] += column_sum(grad)
        pos = pos_ref[:, :1]
        for p in range(SEGS):
            small_ref[3 + p : 4 + p, :] += column_sum(jnp.where(pos == p, total, 0.0))
        for part in range(3):
            span = slice(part * features, (part + 1) * features)
            dw_ref[:, span] += mm(u, dtriple[:, span], TN)
        dw_ref[:, 3 * features :] += mm(mixed, b, TN)
    else:
        out_ref[:, :features] = total.astype(BF)
        out_ref[:, features:] = g_ref[:, features:]


def parts_kernel(who_ref, wide_ref, down_ref, att_ref, mlp_ref, att, mlp, sems):
    features = down_ref.shape[1]
    half = features // 2
    lane = lambda kind: pl.ds(pl.multiple_of(kind * features + who_ref[1] * half, 128), half)
    quarter = pl.ds(pl.multiple_of(who_ref[2] * features, features), features)
    left, right, low, high = pl.ds(0, half), pl.ds(half, half), pl.ds(0, features), pl.ds(features, features)
    copies = Copies(sems)
    att_in = [
        copies.start(wide_ref.at[:, lane(0)], att.at[low, left]),
        copies.start(wide_ref.at[:, lane(1)], att.at[low, right]),
        copies.start(wide_ref.at[left, lane(2)], att.at[pl.ds(features, half), left]),
        copies.start(wide_ref.at[right, lane(2)], att.at[pl.ds(features, half), right]),
        copies.start(
            wide_ref.at[pl.ds(pl.multiple_of(who_ref[1] * half, half), half), pl.ds(3 * features, features)],
            att.at[pl.ds(features + half, half), :],
        ),
    ]
    mlp_in = [copies.start(wide_ref.at[:, quarter], mlp.at[low, :]), copies.start(down_ref.at[quarter, :], mlp.at[high, :])]
    wait(*att_in)
    done = [copies.start(att, att_ref)]
    wait(*mlp_in)
    done.append(copies.start(mlp, mlp_ref))
    wait(*done)


def att_place_kernel(part, who_ref, *refs):
    sources, (_, out_ref, held, triple, rest, sems, out_sems) = refs[:4], refs[4:]
    half = held.shape[1]
    step = half // 4

    @pl.when(who_ref[0] == 0)
    def _():
        core = who_ref[1] if part == 0 else 1 - who_ref[1]
        inward, outward = Copies(sems), Copies(out_sems)
        waits = [inward.start(source, held.at[k]) for k, source in enumerate(sources)]
        done = []
        for quarter in range(4):
            waits[quarter].wait()
            rows = slice(quarter * 2 * step, (quarter + 1) * 2 * step)
            triple[rows, : 2 * half] = held[quarter, : 2 * step, :].astype(F32)
            for side in range(2):
                row = side * half + quarter * step
                triple[row : row + step, 2 * half :] = held[
                    quarter, 2 * step : 3 * step, side * half : (side + 1) * half
                ].astype(F32)
            rest[quarter * step : (quarter + 1) * step, :] = held[quarter, 3 * step :, :].astype(F32)
        for kind in range(3):
            lanes = pl.ds(pl.multiple_of((2 * kind + core) * half, 128), half)
            done.append(outward.start(triple.at[:, pl.ds(kind * half, half)], out_ref.at[:, lanes]))
        rows = pl.ds(pl.multiple_of(core * half, half), half)
        done.append(outward.start(rest, out_ref.at[rows, pl.ds(6 * half, 2 * half)]))
        wait(*done)


def mlp_place_kernel(part, who_ref, u_ref, b_ref, dh_ref, act_ref, *refs):
    sources, (_, _, wide_ref, down_ref, held, dws, dvs, sems, out_sems) = refs[:4], refs[4:]
    size = dws.shape[1]
    step = size // 4

    if part == 0:

        @pl.when(who_ref[0] == 2)
        def _():
            dvs[0] = jnp.zeros_like(dvs[0])
            copies = fetch([dvs.at[0]] * 4, [down_ref.at[pl.ds(k * size, size), :] for k in range(4)], out_sems)
            for copy in copies:
                copy.start()
            wait(*copies)

    @pl.when(who_ref[0] == 1)
    def _():
        inward, outward = Copies(sems), Copies(out_sems)
        waits = [inward.start(source, held.at[k]) for k, source in enumerate(sources)]
        done = []
        for k in range(2):
            at = pl.ds(pl.multiple_of((who_ref[2] ^ (part + 2 * k)) * size, size), size)
            dws[k] = mm(u_ref[...], dh_ref[:, at], TN)
            dvs[k] = mm(act_ref[:, at], b_ref[...], TN)
            for quarter in range(4):
                if k == 0:
                    waits[quarter].wait()
                rows = slice(quarter * step, (quarter + 1) * step)
                dws[k, rows, :] += held[quarter, k, :step, :].astype(F32)
                dvs[k, rows, :] += held[quarter, k, step:, :].astype(F32)
            done.append(outward.start(dws.at[k], wide_ref.at[:, at]))
            done.append(outward.start(dvs.at[k], down_ref.at[at, :]))
        wait(*done)


VMEM = pl.BlockSpec(memory_space=pltpu.VMEM)
SMEM = pl.BlockSpec(memory_space=pltpu.SMEM)
ANY = pl.BlockSpec(memory_space=pl.ANY)
LIMIT = 58 * 2**20


def whole(shape):
    return pl.BlockSpec(shape, lambda i: (0,) * len(shape))


def estimate(microseconds):
    return pl.CostEstimate(flops=int(microseconds * 1.1e9), bytes_accessed=0, transcendentals=0)


def call(kernel, out_shapes, args, scratch=(), anywhere=0, scalars=0, outside=False, inside=None, cost=1):
    return pl.pallas_call(
        kernel,
        grid=(1,),
        out_shape=[jax.ShapeDtypeStruct(*shape) for shape in out_shapes],
        in_specs=[
            SMEM if k < scalars else ANY if k >= len(args) - anywhere or k == inside else whole(arg.shape)
            for k, arg in enumerate(args)
        ],
        out_specs=[ANY if outside else whole(shape[0]) for shape in out_shapes],
        scratch_shapes=list(scratch),
        compiler_params=pltpu.CompilerParams(vmem_limit_bytes=LIMIT),
        cost_estimate=estimate(cost),
    )(*args)


def blank(shape, dtype=F32):
    return pl.pallas_call(lambda out_ref: None, out_shape=jax.ShapeDtypeStruct(shape, dtype), out_specs=ANY)()


def cls_mlp(mode, rows, grads, wide_w, down_w, vector):
    count = rows.shape[0]
    features, hidden = wide_w.shape
    tile = features
    wide_block = pl.BlockSpec((features, tile), lambda j: (0, j))
    down_block = pl.BlockSpec((tile, features), lambda j: (j, 0))
    sums = jax.ShapeDtypeStruct(vector.shape, F32)
    scratch = [pltpu.VMEM((count, features), BF)] + [pltpu.VMEM((count, features), F32)] * 2
    if mode == "weights":
        out_shape = [sums, jax.ShapeDtypeStruct(wide_w.shape, F32), jax.ShapeDtypeStruct(down_w.shape, F32)]
        out_specs = [whole(vector.shape), wide_block, down_block]
    elif mode == "factors":
        out_shape = [sums, jax.ShapeDtypeStruct((count, features), BF)] + [jax.ShapeDtypeStruct((count, hidden), BF)] * 2
        out_specs = [whole(vector.shape), whole((count, features))] + [pl.BlockSpec((count, tile), lambda j: (0, j))] * 2
        scratch = scratch[1:]
    else:
        out_shape = [jax.ShapeDtypeStruct(rows.shape, BF)]
        out_specs = [whole(rows.shape)]
    return pl.pallas_call(
        partial(cls_mlp_kernel, mode),
        grid=(hidden // tile,),
        in_specs=[whole(rows.shape), whole(grads.shape), wide_block, down_block, whole(vector.shape)],
        out_specs=out_specs,
        out_shape=out_shape,
        scratch_shapes=scratch,
        compiler_params=pltpu.CompilerParams(vmem_limit_bytes=LIMIT),
    )(rows, grads, wide_w, down_w, vector)


def cls_step(mode, rows, grads, wide_w, down_w, vector):
    weights = [pltpu.VMEM(wide_w.shape, BF), pltpu.VMEM(down_w.shape, BF)]
    sems = pltpu.SemaphoreType.DMA((2 * wide_w.shape[1] // wide_w.shape[0],))
    return call(
        partial(cls_step_kernel, mode),
        [(rows.shape, BF)],
        [rows, grads, vector, wide_w, down_w],
        weights + [sems],
        anywhere=2,
    )


def cls_att_weights(rows, grads, layout, wide_w, vector):
    count, features = rows.shape
    block = min(count, 128)
    by_row = lambda width: pl.BlockSpec((block, width), lambda i: (i, 0))
    return pl.pallas_call(
        partial(cls_att_bwd_kernel, True),
        grid=(count // block,),
        in_specs=[
            by_row(features), by_row(features), by_row(128), by_row(128),
            pl.BlockSpec((1, block), lambda i: (0, i)), whole(wide_w.shape), whole(vector.shape),
        ],
        out_specs=[whole(vector.shape), whole(wide_w.shape)],
        out_shape=[jax.ShapeDtypeStruct(vector.shape, F32), jax.ShapeDtypeStruct(wide_w.shape, F32)],
        compiler_params=pltpu.CompilerParams(vmem_limit_bytes=LIMIT),
    )(rows, grads, *layout, wide_w, vector)


def documents(counts):
    ends = jnp.cumsum(counts, -1)
    places = jnp.arange(SEGS, dtype=jnp.int32)
    doc = jnp.sum((places[:, None] >= ends[..., None, :]).astype(jnp.int32), -1)
    slots = jnp.arange(counts.shape[-1], dtype=jnp.int32)
    first = jnp.sum(jnp.where(doc[..., None] == slots, (ends - counts)[..., None, :], 0), -1)
    return doc, places - first


def row_layout(counts):
    doc, pos = documents(counts)
    packs = counts.shape[0]
    label = doc + jnp.arange(packs, dtype=jnp.int32)[:, None] * (counts.shape[1] + 1)
    return wide_column(pos), wide_column(label), label.reshape(1, -1)


def wide_column(values):
    return jnp.broadcast_to(values.reshape(-1, 1), (values.size, 128))


def local(inputs, cotangent, wide, down, vectors, seg_counts):
    sections = lax.axis_size("section")
    replicas = lax.axis_size("dp")
    section = lax.axis_index("section")
    replica = lax.axis_index("dp")
    core, side = replica % 2, replica // 2 % 2
    rows, features = inputs.shape[1:]
    half = features // 2
    wide_w, down_w, vector = wide[0], down[0], vectors[0]
    x, cot = inputs[0], cotangent[0]

    fourth = 2 * side + core
    who = jnp.stack([section, core, fourth]).astype(jnp.int32)
    att_part, mlp_part = pl.pallas_call(
        parts_kernel,
        out_shape=[jax.ShapeDtypeStruct((2 * features, features), BF)] * 2,
        in_specs=[SMEM, ANY, ANY],
        out_specs=[ANY, ANY],
        scratch_shapes=[pltpu.VMEM((2 * features, features), BF)] * 2 + [pltpu.SemaphoreType.DMA((9,))],
        compiler_params=pltpu.CompilerParams(vmem_limit_bytes=LIMIT),
    )(who, wide_w, down_w)
    att_first = send(att_part, ATT_WAYS, 0, 1)
    near = [swap_section(vector, bits) for bits in (1, 2, 3)]
    mlp_first = send(mlp_part, MLP_WAYS, 0, 1)
    x_sib = swap_core(x)
    every_vector = jnp.stack([vector] + near)
    avec, mvec = pick(every_vector, section), pick(every_vector, section ^ 1)
    att_second = send(after(att_part, every_vector, mlp_first), ATT_WAYS, 0, 2)
    att_last = send(att_first, ATT_WAYS, 1, 3)
    mlp_second = send(after(mlp_part, every_vector, att_first, x_sib), MLP_WAYS, 0, 2)
    mlp_last = send(after(mlp_first, att_first), MLP_WAYS, 1, 3)

    grid = lambda values: values.reshape(-1, SEG, features)
    heads = lambda values: grid(values)[:, 0]
    count = sections * (rows // SEG)
    is_cls = (jnp.arange(rows) % SEG == 0)[:, None]
    b_own = after(jnp.where(is_cls, jnp.zeros_like(cot), cot), every_vector)
    b_next = swap_dp(b_own, 2)
    b_sib, b_far = swap_core(b_own), swap_core(b_next)
    layout = row_layout(seg_counts[0])

    bf = lambda *shape: (shape, BF)
    att_who = jnp.stack([place_of(ATT_WAYS, section, core), section]).astype(jnp.int32)
    att_choices = [att_part, att_first, att_second, att_last]
    att_weights = [pltpu.VMEM((features, 3 * half), BF), pltpu.VMEM((half, features), BF)]
    triple, a, give0, keep0 = call(
        att_fwd_kernel,
        [bf(2 * rows, 3 * half), bf(2 * rows, half), bf(rows, features), bf(rows, features)],
        [att_who, after(x, b_sib, b_far), x_sib, avec, *att_choices],
        att_weights
        + [pltpu.VMEM((2, rows, 3 * half), BF), pltpu.VMEM((2, rows, half), BF), pltpu.VMEM((2, rows, features), BF)]
        + [pltpu.SemaphoreType.DMA((10,))],
        scalars=1,
        anywhere=4,
        outside=True,
    )
    core0 = swap_core(give0)

    def hop(values, start, end):
        return permute(values, lambda s, r: (end, r), lambda s, r: s == start)

    def on(column, run):
        return lax.cond(section == column, lambda: run()[0], lambda: jnp.zeros((count, 2 * features), BF))

    branch = heads(keep0).astype(F32) + heads(core0).astype(F32)
    cls1_own = (heads(x).astype(F32) + branch + avec[2:3]).astype(BF)
    cls1 = jnp.concatenate(to_column(jnp.concatenate([cls1_own, heads(cot)], 1), 1), 0)
    h1, u_own = call(att_join_kernel, [bf(rows, features)] * 2, [x, keep0, after(core0, cls1_own), avec, mvec])
    u_own = after(u_own, cls1)
    u_next, u_sib = swap_dp(u_own, 2), swap_core(u_own)
    cls2 = on(1, lambda: cls_step("out", cls1, cls1, wide_w, down_w, vector))
    cls2_at2 = hop(cls2, 1, 2)

    square = bf(features, features)
    scratch = [pltpu.VMEM((2 * rows, features), BF)] * 4 + [pltpu.VMEM(*square)] * 2
    scratch += [pltpu.VMEM((2, 2 * rows, features), BF)] + [pltpu.VMEM((2, features, features), BF)] * 2
    scratch += [pltpu.SemaphoreType.DMA((18,))]
    mlp_who = jnp.stack([place_of(MLP_WAYS, section, core), section // 2]).astype(jnp.int32)
    mlp_choices = [mlp_part, mlp_first, mlp_second, mlp_last]
    keep1, give1, dw, dv = call(
        partial(mlp_kernel, False),
        [bf(2 * rows, features)] * 2 + [square] * 2,
        [mlp_who, after(u_own, cls2), u_sib, b_own, b_sib, *mlp_choices],
        scratch,
        scalars=1,
        anywhere=8,
        outside=True,
    )
    u_far = swap_core(after(u_next, dw))
    keep2, give2, near_half, far_half = call(
        partial(mlp_kernel, True),
        [bf(2 * rows, features)] * 2 + [bf(2, half, features)] * 2,
        [mlp_who, after(u_next, cls2_at2), u_far, b_next, b_far, *mlp_choices, dw, dv],
        scratch,
        scalars=1,
        anywhere=10,
        outside=True,
    )
    core1, core2 = swap_core(give1), swap_core(give2)

    shape = [bf(count, 2 * features)]
    near_row = swap_section(far_half, 2)
    cls2_at2 = after(cls2_at2, far_half)
    blanks = lambda: [jnp.zeros((count, 2 * features), BF), jnp.zeros((count, 3 * features), BF)]
    cls3, cls_triple = lax.cond(
        section == 2,
        lambda: list(
            call(
                cls_att_fwd_kernel,
                shape + [bf(count, 3 * features)],
                [cls2_at2, *layout, wide_w, vector],
                [pltpu.VMEM((features, 4 * features), BF), pltpu.SemaphoreType.DMA((4,))],
                inside=4,
            )
        ),
        blanks,
    )
    cls3_at3 = hop(cls3, 2, 3)
    dcls3 = on(3, lambda: cls_step("both", cls3_at3, cls3_at3, wide_w, down_w, vector))
    dcls3_at2 = hop(dcls3, 3, 2)
    pair = pair_sum(keep2, after(core2, cls3))
    du_next = swap_dp(pair[:rows], 2)
    dcls2 = on(
        2, lambda: call(
            partial(cls_att_bwd_kernel, False),
            shape,
            [cls2_at2, dcls3_at2, cls_triple, *layout, wide_w, vector],
            [pltpu.VMEM((features, 4 * features), BF), pltpu.SemaphoreType.DMA((4,))],
            inside=6,
        )
    )
    dh1, mlp_small = call(
        mlp_done_kernel,
        [bf(rows, features), ((8, features), F32)],
        [h1, b_own, keep1, core1, du_next, mvec],
    )
    dcls2_at1 = after(hop(dcls2, 2, 1), dh1, near_row)
    out_next = swap_dp(after(pair[rows:], du_next), 2)
    dcls1 = on(1, lambda: cls_step("back", cls1, dcls2_at1, wide_w, down_w, vector))

    mine_in = jnp.where(section == 1, cls1, jnp.where(section == 2, cls2_at2, cls3_at3))
    mine_grad = jnp.where(section == 1, dcls2_at1[:, :features], dcls3_at2[:, :features])
    mine_grad = jnp.where(section == 3, cls3_at3[:, features:], mine_grad)
    marks = jnp.pad(jnp.concatenate([layout[0][:, :1], layout[1][:, :1] % (SEGS + 1)], 1), ((0, 0), (0, features - 2)))
    everything = jnp.concatenate([mine_in[:, :features], mine_grad, marks.astype(BF)], 0)
    split = dcls1.reshape(sections, rows // SEG, 2 * features)
    arrived = [hop(split[1 ^ bits], 1, 1 ^ bits) for bits in (1, 2, 3)]
    back_rows = jnp.where(section == 1, split[1], arrived[0] + arrived[1] + arrived[2])

    place = lambda values, cls: lax.dynamic_update_slice(grid(values), cls[:, None], (0, 0, 0)).reshape(rows, features)
    dh1 = place(dh1, back_rows[:, :features])
    dh1_sib = swap_core(dh1)


    xbit = section % 2
    mlp_half = pair_sum(near_half, near_row)
    near_block = swap_section(after(pick(mlp_half, 1 - xbit), dcls1), 1)
    mlp_block = pair_sum(pick(mlp_half, xbit), near_block)
    mlp_sum, bits = mlp_block, 4
    while bits < replicas:
        other = swap_dp(jnp.concatenate([mlp_sum, everything], 0), bits)
        mlp_sum = pair_sum(mlp_sum, other[:half])
        everything = ordered(everything, other[half:], replica & bits != 0)
        bits *= 2

    *att_grads, du0_own, du0_sib = call(
        att_bwd_kernel,
        [bf(half + 16, features)] * 4 + [bf(rows, features)] * 2,
        [att_who, avec, mlp_small, after(x, out_next, mlp_block), x_sib, dh1, dh1_sib, triple, a, *att_choices],
        [pltpu.VMEM((2 * rows, features), BF)] * 2
        + [pltpu.VMEM((2 * rows, 3 * half), BF), pltpu.VMEM((2 * rows, half), BF), *att_weights]
        + [pltpu.VMEM((2 * rows, features), BF), pltpu.VMEM((2 * rows, 3 * half), BF)]
        + [pltpu.VMEM((2, rows, features), BF), pltpu.VMEM((4, half + 16, features), BF)]
        + [pltpu.SemaphoreType.DMA((26,))],
        scalars=1,
        anywhere=10,
        outside=True,
        cost=17,
    )
    du0_core = swap_core(du0_sib)
    (input_grad,) = call(att_done_kernel, [bf(rows, features)], [x, dh1, du0_own, du0_core, avec])

    branch = keep1[rows:].astype(F32) + core1[rows:].astype(F32) + out_next.astype(F32)
    h2 = (h1.astype(F32) + branch + mvec[2:3]).astype(BF)
    layer_out = place(h2, back_rows[:, features:])
    other = swap_dp(jnp.concatenate([mlp_sum, everything], 0), 2)
    mlp_next, everything = other[:half], ordered(everything, other[half:], replica & 2 != 0)
    everything = ordered(everything, swap_core(everything), replica & 1 != 0).reshape(-1, 3, count, features)
    received, layer_out, input_grad = lax.optimization_barrier((section_parts(att_grads), layer_out, input_grad))
    att_block = section_sum(att_grads, received)
    mlp_blocks = jnp.stack(after([mlp_sum, mlp_next], att_block))
    att_block = pair_sum(att_block, swap_dp(att_block, 2))
    all_in, all_grad, marks = [everything[:, k].reshape(-1, features) for k in range(3)]
    all_pos, all_doc = marks[:, :1].astype(jnp.int32), marks[:, 1:2].astype(jnp.int32)
    all_doc += jnp.arange(all_doc.shape[0], dtype=jnp.int32)[:, None] // SEGS * (SEGS + 1)
    all_layout = (wide_column(all_pos), wide_column(all_doc), all_doc.reshape(1, -1))
    total = all_in.shape[0]
    none = lambda: [blank((total, features), BF)] + [blank((total, wide_w.shape[1]), BF) for _ in range(2)]

    def first_column():
        return [jnp.zeros(vector.shape, F32), blank(wide_w.shape), jnp.zeros(down_w.shape, F32), *none()]

    def second_column():
        sums, *factors = cls_mlp("factors", all_in, all_grad, wide_w, down_w, vector)
        return [sums, blank(wide_w.shape), blank(down_w.shape), *factors]

    def third_column():
        sums, wide_sum = cls_att_weights(all_in, all_grad, all_layout, wide_w, vector)
        return [sums, wide_sum, blank(down_w.shape), *none()]

    def fourth_column():
        return [*cls_mlp("weights", all_in, all_grad, wide_w, down_w, vector), *none()]

    vector_sum, wide_sum, down_sum, u_cls, dh_cls, act_cls = lax.switch(
        section, [first_column, second_column, third_column, fourth_column]
    )
    mlp_own = to_column(mlp_blocks, 1)
    att_block = pair_sum(att_block, after(swap_dp(att_block, 4), u_cls, mlp_own))
    att_block = dp_sum(att_block, 8)
    small = att_block[half:]
    small = (small.astype(F32) + swap_core(small).astype(F32))[:3]
    mine_small = jnp.where(section < 2, small, 0.0)
    vector_sum = vector_sum + jnp.pad(mine_small, ((0, vector.shape[0] - 3), (0, 0)))
    att_own, vector_sum = lax.optimization_barrier((to_column(att_block[:half], 0), vector_sum))
    att_other = [swap_core(piece) for piece in att_own]
    mlp_own = after(mlp_own, att_own)
    mlp_other = [swap_core(piece) for piece in mlp_own]
    wide_like, down_like = jax.ShapeDtypeStruct(wide_w.shape, F32), jax.ShapeDtypeStruct(down_w.shape, F32)
    for part, (att_pieces, mlp_pieces) in enumerate(((att_own, mlp_own), (att_other, mlp_other))):
        if part:
            att_pieces, mlp_pieces = after([att_pieces, mlp_pieces], wide_sum)
        wide_sum = pl.pallas_call(
            partial(att_place_kernel, part),
            out_shape=wide_like,
            in_specs=[SMEM] + [ANY] * 5,
            out_specs=ANY,
            scratch_shapes=[
                pltpu.VMEM((4, half, features), BF),
                pltpu.VMEM((features, 3 * half), F32),
                pltpu.VMEM((half, features), F32),
                pltpu.SemaphoreType.DMA((4,)),
                pltpu.SemaphoreType.DMA((4,)),
            ],
            input_output_aliases={5: 0},
            compiler_params=pltpu.CompilerParams(vmem_limit_bytes=LIMIT),
        )(who, *att_pieces, wide_sum)
        wide_sum, down_sum = pl.pallas_call(
            partial(mlp_place_kernel, part),
            out_shape=[wide_like, down_like],
            in_specs=[SMEM] + [VMEM] * 4 + [ANY] * 6,
            out_specs=[ANY, ANY],
            scratch_shapes=[
                pltpu.VMEM((4, 2, half, features), BF),
                pltpu.VMEM((2, features, features), F32),
                pltpu.VMEM((2, features, features), F32),
                pltpu.SemaphoreType.DMA((4,)),
                pltpu.SemaphoreType.DMA((4,)),
            ],
            input_output_aliases={9: 0, 10: 1},
            compiler_params=pltpu.CompilerParams(vmem_limit_bytes=LIMIT),
        )(who, u_cls, all_grad, dh_cls, act_cls, *mlp_pieces, wide_sum, down_sum)
    return layer_out[None], input_grad[None], wide_sum[None], down_sum[None], vector_sum[None]


def solution(mesh):
    return jax.shard_map(
        local,
        mesh=mesh,
        in_specs=(
            P("section", "dp", None),
            P("section", "dp", None),
            P("section", None, None),
            P("section", None, None),
            P("section", None, None),
            P("dp", None, None),
        ),
        out_specs=(
            P("section", "dp", None),
            P("section", "dp", None),
            P("section", None, None),
            P("section", None, None),
            P("section", None, None),
        ),
        check_vma=False,
    )
```

```python
from functools import partial

import jax
import jax.numpy as jnp
from jax import lax
from jax.experimental import pallas as pl
from jax.experimental.pallas import tpu as pltpu
from jax.sharding import PartitionSpec as P

HEADS = 12
SEG = 128
SEGS = 4
EPSILON = 1e-05
SCORE_SCALE = 0.125
MASKED = -1e30
AXES = ("section", "dp")
BF = jnp.bfloat16
F32 = jnp.float32

NN = (((1,), (0,)), ((), ()))
NT = (((1,), (1,)), ((), ()))
TN = (((0,), (0,)), ((), ()))

GELU_A = 0.7978845608028654
GELU_B = 0.044715

ATT_WAYS = ((0, 1, 2, 3), (0, 2, 1, 3))
MLP_WAYS = ((1, 0, 3, 2), (1, 3, 0, 2))


def mm(left, right, dims=NN):
    return lax.dot_general(left, right, dims, preferred_element_type=F32)


def permute(shard, move, keep=lambda s, r: True):
    sections, replicas = lax.axis_size("section"), lax.axis_size("dp")
    pairs = []
    for s in range(sections):
        for r in range(replicas):
            if keep(s, r):
                t, q = move(s, r)
                pairs.append((s * replicas + r, t * replicas + q))
    return lax.ppermute(shard, AXES, pairs)


def swap_core(shard):
    return permute(shard, lambda s, r: (s, r ^ 1))


def swap_section(shard, bits):
    return permute(shard, lambda s, r: (s ^ bits, r))


def swap_dp(shard, bits):
    return permute(shard, lambda s, r: (s, r ^ bits))


def send(values, ways, start, end):
    return permute(values, lambda s, r: (ways[r & 1][end], r), lambda s, r: ways[r & 1][start] == s)


def after(value, *marks):
    return lax.optimization_barrier((value, marks))[0]


def place_of(ways, section, core):
    position = jnp.int32(0)
    for c in range(2):
        for k, s in enumerate(ways[c]):
            position = jnp.where((section == s) & (core == c), k, position)
    return position


def pick(stack, index):
    return lax.dynamic_index_in_dim(stack, index, 0, keepdims=False)


def section_parts(parts):
    return [swap_section(parts[bits], bits) for bits in (1, 2, 3)]


def section_sum(parts, others=None):
    others = others or section_parts(parts)
    return sum([other.astype(F32) for other in others], parts[0].astype(F32)).astype(BF)


def dp_sum(value, bits):
    while bits < lax.axis_size("dp"):
        value = pair_sum(value, swap_dp(value, bits))
        bits *= 2
    return value


def pair_sum(mine, other):
    return (mine.astype(F32) + other.astype(F32)).astype(BF)


def ordered(first, second, swapped):
    return jnp.where(swapped, jnp.concatenate([second, first], 0), jnp.concatenate([first, second], 0))


def to_column(value, owner):
    arrived = [permute(value, lambda s, r: (owner, r), lambda s, r: s == owner ^ bits) for bits in (1, 2, 3)]
    columns = [None] * 4
    columns[owner] = value
    for bits, other in zip((1, 2, 3), arrived):
        columns[owner ^ bits] = other
    return columns


def fetch(sources, targets, sems):
    return [pltpu.make_async_copy(source, target, sems.at[i]) for i, (source, target) in enumerate(zip(sources, targets))]


def norm_parts(values):
    center = values - jnp.mean(values, -1, keepdims=True)
    spread = jnp.mean(center * center, -1, keepdims=True)
    scale = lax.rsqrt(spread + EPSILON)
    return center * scale, scale


def norm_rows(values, vec_ref):
    hat, _ = norm_parts(values)
    return hat * vec_ref[0:1, :] + vec_ref[1:2, :]


def norm_back(values, grad_normed, vec_ref):
    hat, scale = norm_parts(values)
    inner = grad_normed * vec_ref[0:1, :]
    first = jnp.mean(inner, -1, keepdims=True)
    second = jnp.mean(inner * hat, -1, keepdims=True)
    return scale * (inner - first - hat * second), grad_normed * hat


def column_sum(values):
    return jnp.sum(values, 0, keepdims=True)


def gelu_parts(hidden):
    square = hidden * hidden
    inner = GELU_A * hidden * (1.0 + GELU_B * square)
    t = jnp.tanh(inner)
    half = 0.5 * (1.0 + t)
    slope = half + 0.5 * hidden * (1.0 - t * t) * (GELU_A * (1.0 + 3.0 * GELU_B * square))
    return hidden * half, slope


def two_heads(pair):
    low = lax.broadcasted_iota(jnp.int32, pair.shape, 1) < 64
    zero = jnp.zeros_like(pair)
    return jnp.concatenate([jnp.where(low, pair, zero), jnp.where(low, zero, pair)], 0)


def join_heads(both):
    rows = both.shape[0] // 2
    low = lax.broadcasted_iota(jnp.int32, (rows, both.shape[1]), 1) < 64
    return jnp.where(low, both[:rows], both[rows:])


def softmax_rows(scores):
    powers = jnp.exp(scores - jnp.max(scores, -1, keepdims=True))
    return powers / jnp.sum(powers, -1, keepdims=True)


def softmax_columns(scores):
    powers = jnp.exp(scores - jnp.max(scores, 0, keepdims=True))
    return powers * (1.0 / jnp.sum(powers, 0, keepdims=True))


def head_pairs(q, k, v, out):
    for seg in range(q.shape[0] // SEG):
        at = slice(seg * SEG, (seg + 1) * SEG)
        mixed = []
        for pair in range(q.shape[1] // 128):
            lanes = slice(pair * 128, (pair + 1) * 128)
            probs = softmax_columns(mm(k[at, lanes], two_heads(q[at, lanes]), NT) * SCORE_SCALE)
            mixed.append(join_heads(mm(probs.astype(BF), v[at, lanes], TN)).astype(BF))
        out.append(jnp.concatenate(mixed, 1))


class Copies:
    def __init__(self, sems):
        self.sems, self.used = sems, 0

    def next(self):
        self.used += 1
        return self.sems.at[self.used - 1]

    def start(self, source, target):
        sem = self.next()
        send_parts(source, target, sem)
        return pltpu.make_async_copy(source, target, sem)

    def choose(self, which, sources, target):
        sem = self.next()
        for k, source in enumerate(sources):

            @pl.when(which == k)
            def _():
                send_parts(source, target, sem)

        return pltpu.make_async_copy(sources[0], target, sem)


def send_parts(source, target, sem):
    rows = source.shape[0]
    step = rows // 4 if rows % 64 == 0 else rows
    for start in range(0, rows, step):
        part = pl.ds(start, step)
        pltpu.make_async_copy(source.at[part], target.at[part], sem).start()


def wait(*copies):
    for copy in copies:
        copy.wait()


def load_triple(copies, place, choices, wt, half):
    features, left, right = wt.shape[0], pl.ds(0, half), pl.ds(half, half)
    return [
        copies.choose(place, [c.at[pl.ds(0, features), :] for c in choices], wt.at[:, pl.ds(0, features)]),
        copies.choose(place, [c.at[pl.ds(features, half), left] for c in choices], wt.at[left, pl.ds(features, half)]),
        copies.choose(place, [c.at[pl.ds(features, half), right] for c in choices], wt.at[right, pl.ds(features, half)]),
    ]


def att_fwd_kernel(place_ref, own_ref, sib_ref, vec_ref, *refs):
    choices, (triple_ref, a_ref, give_ref, keep_ref, wt, wo, triples, mixes, outs, sems) = refs[:4], refs[4:]
    rows, features = own_ref.shape
    half = a_ref.shape[1]
    copies = Copies(sems)
    wt_in = load_triple(copies, place_ref[0], choices, wt, half)
    wo_in = [copies.choose(place_ref[0], [c.at[pl.ds(features + half, half), :] for c in choices], wo)]
    done = []
    for pack, (ref, out) in enumerate(((sib_ref, give_ref), (own_ref, keep_ref))):
        span = pl.ds((1 - pack) * rows, rows)
        u = norm_rows(ref[...].astype(F32), vec_ref).astype(BF)
        if pack == 0:
            wait(*wt_in)
        triple = mm(u, wt[...]).astype(BF)
        triples[pack] = triple
        done.append(copies.start(triples.at[pack], triple_ref.at[span, :]))
        mixed = []
        head_pairs(triple[:, :half], triple[:, half : 2 * half], triple[:, 2 * half :], mixed)
        a = jnp.concatenate(mixed, 0)
        mixes[pack] = a
        done.append(copies.start(mixes.at[pack], a_ref.at[span, :]))
        if pack == 0:
            wait(*wo_in)
        outs[pack] = mm(a, wo[...]).astype(BF)
        done.append(copies.start(outs.at[pack], out))
    wait(*done)


def att_bwd_kernel(place_ref, vec_ref, small_ref, *refs):
    own_ref, sib_ref, gown_ref, gsib_ref, triple_ref, a_ref, *choices = refs[:10]
    grad_refs, (duown_ref, dusib_ref, xs, gs, triple, mixes, wt, wo, u, dt, dus, piece, sems) = refs[10:14], refs[14:]
    rows = own_ref.shape[0]
    half = a_ref.shape[1]
    part = half // 4
    copies = Copies(sems)
    gs_in = [copies.start(gown_ref, gs.at[pl.ds(0, rows), :])]
    early = copies.choose(place_ref[0], [c.at[pl.ds(wt.shape[0] + half, half), :] for c in choices], wo)
    triple_in = [copies.start(triple_ref.at[pl.ds(k * rows, rows), :], triple.at[pl.ds(k * rows, rows), :]) for k in range(2)]
    xs_in = [copies.start(own_ref, xs.at[pl.ds(0, rows), :])]
    wt_in = load_triple(copies, place_ref[0], choices, wt, half)
    gs_in.append(copies.start(gsib_ref, gs.at[pl.ds(rows, rows), :]))
    xs_in.append(copies.start(sib_ref, xs.at[pl.ds(rows, rows), :]))
    a_in = copies.start(a_ref, mixes)
    done = []
    gain = shift = 0.0
    for pack, out in enumerate((duown_ref, dusib_ref)):
        span = slice(pack * rows, (pack + 1) * rows)
        wait(gs_in[pack])
        if pack == 0:
            wait(early)
        da = mm(gs[span, :], wo[...], NT).astype(BF)
        wait(triple_in[pack])
        for seg in range(rows // SEG):
            at = slice(seg * SEG, (seg + 1) * SEG)
            to = slice(pack * rows + seg * SEG, pack * rows + (seg + 1) * SEG)
            for pair in range(half // 128):
                lanes = [slice(kind * half + pair * 128, kind * half + (pair + 1) * 128) for kind in range(3)]
                q2, k, v = two_heads(triple[to, lanes[0]]), triple[to, lanes[1]], triple[to, lanes[2]]
                da2 = two_heads(da[at, lanes[0]])
                probs = softmax_columns(mm(k, q2, NT) * SCORE_SCALE)
                dy = mm(v, da2, NT)
                ds = (probs * (dy - jnp.sum(dy * probs, 0, keepdims=True))).astype(BF)
                dt[to, lanes[2]] = mm(probs.astype(BF), da2).astype(BF)
                dt[to, lanes[0]] = (join_heads(mm(ds, k, TN)) * SCORE_SCALE).astype(BF)
                dt[to, lanes[1]] = (mm(ds, q2) * SCORE_SCALE).astype(BF)
        wait(xs_in[pack])
        hat, _ = norm_parts(xs[span, :].astype(F32))
        u[span, :] = (hat * vec_ref[0:1, :] + vec_ref[1:2, :]).astype(BF)
        if pack == 0:
            wait(*wt_in)
        du = mm(dt[span, :], wt[...], NT)
        dus[pack] = du.astype(BF)
        done.append(copies.start(dus.at[pack], out))
        gain = gain + column_sum(du * hat)
        shift = shift + column_sum(du)

    def send(start, count):
        at = pl.ds(start, count)
        for bits, ref in enumerate(grad_refs):
            done.append(copies.start(piece.at[place_ref[1] ^ bits, at, :], ref.at[at, :]))

    dw = mm(u[...], dt[:, : 2 * half], TN)
    for quarter in range(4):
        piece[quarter, : 2 * part, :] = dw[quarter * 2 * part : (quarter + 1) * 2 * part, :].astype(BF)
    send(0, 2 * part)
    dw = mm(u[...], dt[:, 2 * half :], TN)
    for quarter in range(4):
        for side in range(2):
            piece[quarter, 2 * part : 3 * part, side * half : (side + 1) * half] = dw[
                side * half + quarter * part : side * half + (quarter + 1) * part, :
            ].astype(BF)
    send(2 * part, part)
    wait(a_in)
    dw = mm(mixes[...], gs[...], TN)
    piece[:, 4 * part :, :] = jnp.zeros((4, 16, piece.shape[2]), BF)
    rest = jnp.zeros((13, piece.shape[2]), F32)
    sums = [gain, shift, column_sum(gs[:rows, :].astype(F32)), rest]
    piece[0, 4 * part :, :] = jnp.concatenate(sums, 0).astype(BF)
    piece[1, 4 * part :, :] = jnp.concatenate([small_ref[...], small_ref[...]], 0).astype(BF)
    for quarter in range(4):
        piece[quarter, 3 * part : 4 * part, :] = dw[quarter * part : (quarter + 1) * part, :].astype(BF)
    send(3 * part, part + 16)
    wait(*done)


def att_done_kernel(x_ref, g_ref, duown_ref, dusib_ref, vec_ref, out_ref):
    du = duown_ref[...].astype(F32) + dusib_ref[...].astype(F32)
    back, _ = norm_back(x_ref[...].astype(F32), du, vec_ref)
    out_ref[...] = (g_ref[...].astype(F32) + back).astype(BF)


def att_join_kernel(x_ref, keep_ref, core_ref, avec_ref, mvec_ref, h_ref, u_ref):
    branch = keep_ref[...].astype(F32) + core_ref[...].astype(F32)
    out = (x_ref[...].astype(F32) + branch + avec_ref[2:3, :]).astype(BF)
    h_ref[...] = out
    u_ref[...] = norm_rows(out.astype(F32), mvec_ref).astype(BF)


def mlp_kernel(last, who_ref, *refs):
    uown_ref, usib_ref, bown_ref, bsib_ref, *choices = refs[:8]
    before, refs = refs[8 : 10 if last else 8], refs[10 if last else 8 :]
    keep_ref, give_ref, first_ref, second_ref, u, b, act, dhs, w, v, outs, dws, held, sems = refs
    rows = uown_ref.shape[0]
    size = w.shape[0]
    copies = Copies(sems)
    us_in, bs_in, done = [None, None], [None, None], []
    us_in[1] = copies.start(usib_ref, u.at[pl.ds(rows, rows), :])
    w_in = copies.choose(who_ref[0], [c.at[pl.ds(0, size), :] for c in choices], w)
    bs_in[1] = copies.start(bsib_ref, b.at[pl.ds(rows, rows), :])
    v_in = copies.choose(who_ref[0], [c.at[pl.ds(size, size), :] for c in choices], v)
    for pack, out in ((1, give_ref), (0, keep_ref)):
        at = slice(pack * rows, (pack + 1) * rows)
        wait(us_in[pack])
        if pack == 1:
            wait(w_in)
            us_in[0] = copies.start(uown_ref, u.at[pl.ds(0, rows), :])
            bs_in[0] = copies.start(bown_ref, b.at[pl.ds(0, rows), :])
        active, slope = gelu_parts(mm(u[at, :], w[...]))
        act[at, :] = active.astype(BF)
        wait(bs_in[pack])
        if pack == 1:
            wait(v_in)
            before_in = [copies.start(ref, held.at[k]) for k, ref in enumerate(before)]
        dhs[at, :] = (mm(b[at, :], v[...], NT) * slope).astype(BF)
        outs[pack, :rows, :] = mm(dhs[at, :], w[...], NT).astype(BF)
        outs[pack, rows:, :] = mm(act[at, :], v[...]).astype(BF)
        done.append(copies.start(outs.at[pack], out))
    quarter = size // 4
    for kind, (left, right) in enumerate(((u, dhs), (act, b))):
        dw = mm(left[...], right[...], TN)
        if not last:
            dws[kind] = dw.astype(BF)
            done.append(copies.start(dws.at[kind], (first_ref, second_ref)[kind]))
            continue
        wait(before_in[kind])
        dws[kind] = (dw + held[kind].astype(F32)).astype(BF)
        for k in range(2):
            sem = copies.next()
            target = (first_ref, second_ref)[k].at[:, pl.ds(kind * quarter, quarter), :]
            for y in range(2):
                source = dws.at[kind, pl.ds((y ^ k) * 2 * quarter, 2 * quarter), :].reshape(2, quarter, size)

                @pl.when(who_ref[1] == y)
                def _():
                    pltpu.make_async_copy(source, target, sem).start()

            done.append(pltpu.make_async_copy(source, target, sem))
    wait(*done)


def mlp_done_kernel(h_ref, b_ref, keep_ref, core_ref, z_ref, vec_ref, grad_ref, small_ref):
    rows = h_ref.shape[0]
    du = keep_ref[:rows, :].astype(F32) + core_ref[:rows, :].astype(F32) + z_ref[...].astype(F32)
    grad = b_ref[...].astype(F32)
    back, gain = norm_back(h_ref[...].astype(F32), du, vec_ref)
    grad_ref[...] = (grad + back).astype(BF)
    small_ref[...] = jnp.zeros_like(small_ref)
    small_ref[0:1, :] = column_sum(gain)
    small_ref[1:2, :] = column_sum(du)
    small_ref[2:3, :] = column_sum(grad)


def cls_step_kernel(mode, h_ref, b_ref, vec_ref, w_ref, v_ref, out_ref, w, v, sems):
    forward, backward = mode in ("out", "both"), mode in ("back", "both")
    features, hidden = w_ref.shape
    copies = Copies(sems)
    spans = [slice(start, start + features) for start in range(0, hidden, features)]
    loads = []
    for span in spans:
        at = pl.ds(span.start, features)
        loads.append((copies.start(w_ref.at[:, at], w.at[:, at]), copies.start(v_ref.at[at, :], v.at[at, :])))
    values = h_ref[:, :features].astype(F32)
    u = norm_rows(values, vec_ref).astype(BF)
    b = b_ref[:, -features:] if mode == "both" else b_ref[:, :features]
    out = du = 0.0
    for span, (w_in, v_in) in zip(spans, loads):
        w_in.wait()
        active, slope = gelu_parts(mm(u, w[:, span]))
        v_in.wait()
        if forward:
            out = out + mm(active.astype(BF), v[span, :])
        if backward:
            dh = (mm(b, v[span, :], NT) * slope).astype(BF)
            du = du + mm(dh, w[:, span], NT)
    if forward:
        out = (values + out + vec_ref[2:3, :]).astype(BF)
    if backward:
        back, _ = norm_back(values, du, vec_ref)
        back = (b.astype(F32) + back).astype(BF)
    out_ref[:, :features] = back if backward else out
    out_ref[:, features:] = {"out": h_ref, "back": b_ref}[mode][:, features:] if mode != "both" else out


def cls_mlp_kernel(mode, h_ref, b_ref, w_ref, v_ref, vec_ref, *refs):
    features = w_ref.shape[0]
    forward, backward = mode in ("out", "both"), mode in ("back", "both")
    weights, factors = mode == "weights", mode == "factors"
    j = pl.program_id(0)
    if weights:
        small_ref, dw_ref, dv_ref, u_ref, out_acc, du_acc = refs
    elif factors:
        small_ref, u_ref, dh_ref, act_ref, out_acc, du_acc = refs
    else:
        out_ref, u_ref, out_acc, du_acc = refs

    @pl.when(j == 0)
    def _():
        u_ref[...] = norm_rows(h_ref[:, :features].astype(F32), vec_ref).astype(BF)
        out_acc[...] = jnp.zeros_like(out_acc)
        du_acc[...] = jnp.zeros_like(du_acc)

    u = u_ref[...]
    active, slope = gelu_parts(mm(u, w_ref[...]))
    active = active.astype(BF)
    if forward:
        out_acc[...] += mm(active, v_ref[...])
    if not forward or backward:
        b = b_ref[:, -features:] if mode == "both" else b_ref[:, :features]
        dh = (mm(b, v_ref[...], NT) * slope).astype(BF)
        du_acc[...] += mm(dh, w_ref[...], NT)
    if weights:
        dw_ref[...] = mm(u, dh, TN)
        dv_ref[...] = mm(active, b, TN)
    if factors:
        dh_ref[...] = dh
        act_ref[...] = active

    @pl.when(j == pl.num_programs(0) - 1)
    def _():
        values = h_ref[:, :features].astype(F32)
        if forward:
            out = (values + out_acc[...] + vec_ref[2:3, :]).astype(BF)
        if not forward or backward:
            grad = b.astype(F32)
            back, gain = norm_back(values, du_acc[...], vec_ref)
            back = (grad + back).astype(BF)
        if mode == "out":
            out_ref[:, :features] = out
            out_ref[:, features:] = h_ref[:, features:]
        if mode == "both":
            out_ref[:, :features] = back
            out_ref[:, features:] = out
        if mode == "back":
            out_ref[:, :features] = back
            out_ref[:, features:] = b_ref[:, features:]
        if weights or factors:
            small_ref[...] = jnp.zeros_like(small_ref)
            small_ref[0:1, :] = column_sum(gain)
            small_ref[1:2, :] = column_sum(du_acc[...])
            small_ref[2:3, :] = column_sum(grad)


def lifted_rows(h_ref, pos_ref, vec_ref):
    values = h_ref[:, : vec_ref.shape[1]].astype(F32)
    pos = pos_ref[:, :1]
    for p in range(SEGS):
        values = values + jnp.where(pos == p, vec_ref[3 + p : 4 + p, :], 0.0)
    return values


def cls_att_heads(triple, col_ref, row_ref):
    features = triple.shape[1] // 3
    column = jnp.concatenate([col_ref[:, :1], col_ref[:, :1]], 0)
    mask = column == row_ref[...]
    probs, mixed = [], []
    for pair in range(features // 128):
        lanes = slice(pair * 128, (pair + 1) * 128)
        q2 = two_heads(triple[:, lanes])
        k = triple[:, features + pair * 128 : features + (pair + 1) * 128]
        v = triple[:, 2 * features + pair * 128 : 2 * features + (pair + 1) * 128]
        scores = jnp.where(mask, mm(q2, k, NT) * SCORE_SCALE, MASKED)
        probs.append(softmax_rows(scores))
        mixed.append(join_heads(mm(probs[-1].astype(BF), v)).astype(BF))
    return probs, jnp.concatenate(mixed, 1)


def cls_att_fwd_kernel(h_ref, pos_ref, col_ref, row_ref, w_ref, vec_ref, out_ref, triple_ref, w, sems):
    features = vec_ref.shape[1]
    copies = Copies(sems)
    parts = [pl.ds(k * features, features) for k in range(4)]
    loads = [copies.start(w_ref.at[:, part], w.at[:, part]) for part in parts]
    values = lifted_rows(h_ref, pos_ref, vec_ref)
    u = norm_rows(values, vec_ref).astype(BF)
    for part, load in zip(parts[:3], loads):
        load.wait()
        triple_ref[:, part] = mm(u, w[:, part]).astype(BF)
    _, mixed = cls_att_heads(triple_ref[...], col_ref, row_ref)
    loads[3].wait()
    out_ref[:, :features] = (values + mm(mixed, w[:, 3 * features :]) + vec_ref[2:3, :]).astype(BF)
    out_ref[:, features:] = h_ref[:, features:]


def cls_att_bwd_kernel(weights_too, h_ref, g_ref, *refs):
    if weights_too:
        pos_ref, col_ref, row_ref, w_ref, vec_ref, *refs = refs
    else:
        triple_ref, pos_ref, col_ref, row_ref, source_ref, vec_ref, out_ref, w_ref, sems = refs
        features = vec_ref.shape[1]
        copies = Copies(sems)
        parts = [pl.ds(k * features, features) for k in (3, 0, 1, 2)]
        loads = [copies.start(source_ref.at[:, part], w_ref.at[:, part]) for part in parts]
    values = lifted_rows(h_ref, pos_ref, vec_ref)
    features = values.shape[1]
    if weights_too:
        u = norm_rows(values, vec_ref).astype(BF)
        triple = mm(u, w_ref[:, : 3 * features]).astype(BF)
    else:
        triple = triple_ref[...]
    probs, mixed = cls_att_heads(triple, col_ref, row_ref)
    b = g_ref[:, :features]
    if not weights_too:
        wait(loads[0])
    da = mm(b, w_ref[:, 3 * features :], NT).astype(BF)
    dqs, dks, dvs = [], [], []
    for pair in range(features // 128):
        lanes = slice(pair * 128, (pair + 1) * 128)
        q2 = two_heads(triple[:, lanes])
        k = triple[:, features + pair * 128 : features + (pair + 1) * 128]
        v = triple[:, 2 * features + pair * 128 : 2 * features + (pair + 1) * 128]
        da2 = two_heads(da[:, lanes])
        y = probs[pair]
        dy = mm(da2, v, NT)
        ds = (y * (dy - jnp.sum(dy * y, -1, keepdims=True))).astype(BF)
        dvs.append(mm(y.astype(BF), da2, TN).astype(BF))
        dqs.append((join_heads(mm(ds, k)) * SCORE_SCALE).astype(BF))
        dks.append((mm(ds, q2, TN) * SCORE_SCALE).astype(BF))
    dtriple = jnp.concatenate(dqs + dks + dvs, 1)
    if not weights_too:
        wait(*loads[1:])
    du = mm(dtriple, w_ref[:, : 3 * features], NT)
    back, gain = norm_back(values, du, vec_ref)
    grad = b.astype(F32)
    total = grad + back
    if weights_too:
        small_ref, dw_ref = refs

        @pl.when(pl.program_id(0) == 0)
        def _():
            small_ref[...] = jnp.zeros_like(small_ref)
            dw_ref[...] = jnp.zeros_like(dw_ref)

        small_ref[0:1, :] += column_sum(gain)
        small_ref[1:2, :] += column_sum(du)
        small_ref[2:3, :] += column_sum(grad)
        pos = pos_ref[:, :1]
        for p in range(SEGS):
            small_ref[3 + p : 4 + p, :] += column_sum(jnp.where(pos == p, total, 0.0))
        for part in range(3):
            span = slice(part * features, (part + 1) * features)
            dw_ref[:, span] += mm(u, dtriple[:, span], TN)
        dw_ref[:, 3 * features :] += mm(mixed, b, TN)
    else:
        out_ref[:, :features] = total.astype(BF)
        out_ref[:, features:] = g_ref[:, features:]


def parts_kernel(who_ref, wide_ref, down_ref, att_ref, mlp_ref, att, mlp, sems):
    features = down_ref.shape[1]
    half = features // 2
    lane = lambda kind: pl.ds(pl.multiple_of(kind * features + who_ref[1] * half, 128), half)
    quarter = pl.ds(pl.multiple_of(who_ref[2] * features, features), features)
    left, right, low, high = pl.ds(0, half), pl.ds(half, half), pl.ds(0, features), pl.ds(features, features)
    copies = Copies(sems)
    att_in = [
        copies.start(wide_ref.at[:, lane(0)], att.at[low, left]),
        copies.start(wide_ref.at[:, lane(1)], att.at[low, right]),
        copies.start(wide_ref.at[left, lane(2)], att.at[pl.ds(features, half), left]),
        copies.start(wide_ref.at[right, lane(2)], att.at[pl.ds(features, half), right]),
        copies.start(
            wide_ref.at[pl.ds(pl.multiple_of(who_ref[1] * half, half), half), pl.ds(3 * features, features)],
            att.at[pl.ds(features + half, half), :],
        ),
    ]
    mlp_in = [copies.start(wide_ref.at[:, quarter], mlp.at[low, :]), copies.start(down_ref.at[quarter, :], mlp.at[high, :])]
    wait(*att_in)
    done = [copies.start(att, att_ref)]
    wait(*mlp_in)
    done.append(copies.start(mlp, mlp_ref))
    wait(*done)


def att_place_kernel(part, who_ref, *refs):
    sources, (_, out_ref, held, triple, rest, sems, out_sems) = refs[:4], refs[4:]
    half = held.shape[1]
    step = half // 4

    @pl.when(who_ref[0] == 0)
    def _():
        core = who_ref[1] if part == 0 else 1 - who_ref[1]
        inward, outward = Copies(sems), Copies(out_sems)
        waits = [inward.start(source, held.at[k]) for k, source in enumerate(sources)]
        done = []
        for quarter in range(4):
            waits[quarter].wait()
            rows = slice(quarter * 2 * step, (quarter + 1) * 2 * step)
            triple[rows, : 2 * half] = held[quarter, : 2 * step, :].astype(F32)
            for side in range(2):
                row = side * half + quarter * step
                triple[row : row + step, 2 * half :] = held[
                    quarter, 2 * step : 3 * step, side * half : (side + 1) * half
                ].astype(F32)
            rest[quarter * step : (quarter + 1) * step, :] = held[quarter, 3 * step :, :].astype(F32)
        for kind in range(3):
            lanes = pl.ds(pl.multiple_of((2 * kind + core) * half, 128), half)
            done.append(outward.start(triple.at[:, pl.ds(kind * half, half)], out_ref.at[:, lanes]))
        rows = pl.ds(pl.multiple_of(core * half, half), half)
        done.append(outward.start(rest, out_ref.at[rows, pl.ds(6 * half, 2 * half)]))
        wait(*done)


def mlp_place_kernel(part, who_ref, u_ref, b_ref, dh_ref, act_ref, *refs):
    sources, (_, _, wide_ref, down_ref, held, dws, dvs, sems, out_sems) = refs[:4], refs[4:]
    size = dws.shape[1]
    step = size // 4

    if part == 0:

        @pl.when(who_ref[0] == 2)
        def _():
            dvs[0] = jnp.zeros_like(dvs[0])
            copies = fetch([dvs.at[0]] * 4, [down_ref.at[pl.ds(k * size, size), :] for k in range(4)], out_sems)
            for copy in copies:
                copy.start()
            wait(*copies)

    @pl.when(who_ref[0] == 1)
    def _():
        inward, outward = Copies(sems), Copies(out_sems)
        waits = [inward.start(source, held.at[k]) for k, source in enumerate(sources)]
        done = []
        for k in range(2):
            at = pl.ds(pl.multiple_of((who_ref[2] ^ (part + 2 * k)) * size, size), size)
            dws[k] = mm(u_ref[...], dh_ref[:, at], TN)
            dvs[k] = mm(act_ref[:, at], b_ref[...], TN)
            for quarter in range(4):
                if k == 0:
                    waits[quarter].wait()
                rows = slice(quarter * step, (quarter + 1) * step)
                dws[k, rows, :] += held[quarter, k, :step, :].astype(F32)
                dvs[k, rows, :] += held[quarter, k, step:, :].astype(F32)
            done.append(outward.start(dws.at[k], wide_ref.at[:, at]))
            done.append(outward.start(dvs.at[k], down_ref.at[at, :]))
        wait(*done)


VMEM = pl.BlockSpec(memory_space=pltpu.VMEM)
SMEM = pl.BlockSpec(memory_space=pltpu.SMEM)
ANY = pl.BlockSpec(memory_space=pl.ANY)
LIMIT = 58 * 2**20


def whole(shape):
    return pl.BlockSpec(shape, lambda i: (0,) * len(shape))


def estimate(microseconds):
    return pl.CostEstimate(flops=int(microseconds * 1.1e9), bytes_accessed=0, transcendentals=0)


def call(kernel, out_shapes, args, scratch=(), anywhere=0, scalars=0, outside=False, inside=None, cost=0):
    return pl.pallas_call(
        kernel,
        grid=(1,),
        out_shape=[jax.ShapeDtypeStruct(*shape) for shape in out_shapes],
        in_specs=[
            SMEM if k < scalars else ANY if k >= len(args) - anywhere or k == inside else whole(arg.shape)
            for k, arg in enumerate(args)
        ],
        out_specs=[ANY if outside else whole(shape[0]) for shape in out_shapes],
        scratch_shapes=list(scratch),
        compiler_params=pltpu.CompilerParams(vmem_limit_bytes=LIMIT),
        cost_estimate=estimate(cost),
    )(*args)


def blank(shape, dtype=F32):
    return pl.pallas_call(lambda out_ref: None, out_shape=jax.ShapeDtypeStruct(shape, dtype), out_specs=ANY)()


def cls_mlp(mode, rows, grads, wide_w, down_w, vector):
    count = rows.shape[0]
    features, hidden = wide_w.shape
    tile = features
    wide_block = pl.BlockSpec((features, tile), lambda j: (0, j))
    down_block = pl.BlockSpec((tile, features), lambda j: (j, 0))
    sums = jax.ShapeDtypeStruct(vector.shape, F32)
    scratch = [pltpu.VMEM((count, features), BF)] + [pltpu.VMEM((count, features), F32)] * 2
    if mode == "weights":
        out_shape = [sums, jax.ShapeDtypeStruct(wide_w.shape, F32), jax.ShapeDtypeStruct(down_w.shape, F32)]
        out_specs = [whole(vector.shape), wide_block, down_block]
    elif mode == "factors":
        out_shape = [sums, jax.ShapeDtypeStruct((count, features), BF)] + [jax.ShapeDtypeStruct((count, hidden), BF)] * 2
        out_specs = [whole(vector.shape), whole((count, features))] + [pl.BlockSpec((count, tile), lambda j: (0, j))] * 2
        scratch = scratch[1:]
    else:
        out_shape = [jax.ShapeDtypeStruct(rows.shape, BF)]
        out_specs = [whole(rows.shape)]
    return pl.pallas_call(
        partial(cls_mlp_kernel, mode),
        grid=(hidden // tile,),
        in_specs=[whole(rows.shape), whole(grads.shape), wide_block, down_block, whole(vector.shape)],
        out_specs=out_specs,
        out_shape=out_shape,
        scratch_shapes=scratch,
        compiler_params=pltpu.CompilerParams(vmem_limit_bytes=LIMIT),
    )(rows, grads, wide_w, down_w, vector)


def cls_step(mode, rows, grads, wide_w, down_w, vector):
    weights = [pltpu.VMEM(wide_w.shape, BF), pltpu.VMEM(down_w.shape, BF)]
    sems = pltpu.SemaphoreType.DMA((2 * wide_w.shape[1] // wide_w.shape[0],))
    return call(
        partial(cls_step_kernel, mode),
        [(rows.shape, BF)],
        [rows, grads, vector, wide_w, down_w],
        weights + [sems],
        anywhere=2,
    )


def cls_att_weights(rows, grads, layout, wide_w, vector):
    count, features = rows.shape
    block = min(count, 128)
    by_row = lambda width: pl.BlockSpec((block, width), lambda i: (i, 0))
    return pl.pallas_call(
        partial(cls_att_bwd_kernel, True),
        grid=(count // block,),
        in_specs=[
            by_row(features), by_row(features), by_row(128), by_row(128),
            pl.BlockSpec((1, block), lambda i: (0, i)), whole(wide_w.shape), whole(vector.shape),
        ],
        out_specs=[whole(vector.shape), whole(wide_w.shape)],
        out_shape=[jax.ShapeDtypeStruct(vector.shape, F32), jax.ShapeDtypeStruct(wide_w.shape, F32)],
        compiler_params=pltpu.CompilerParams(vmem_limit_bytes=LIMIT),
    )(rows, grads, *layout, wide_w, vector)


def documents(counts):
    ends = jnp.cumsum(counts, -1)
    places = jnp.arange(SEGS, dtype=jnp.int32)
    doc = jnp.sum((places[:, None] >= ends[..., None, :]).astype(jnp.int32), -1)
    slots = jnp.arange(counts.shape[-1], dtype=jnp.int32)
    first = jnp.sum(jnp.where(doc[..., None] == slots, (ends - counts)[..., None, :], 0), -1)
    return doc, places - first


def row_layout(counts):
    doc, pos = documents(counts)
    packs = counts.shape[0]
    label = doc + jnp.arange(packs, dtype=jnp.int32)[:, None] * (counts.shape[1] + 1)
    return wide_column(pos), wide_column(label), label.reshape(1, -1)


def wide_column(values):
    return jnp.broadcast_to(values.reshape(-1, 1), (values.size, 128))


def local(inputs, cotangent, wide, down, vectors, seg_counts):
    sections = lax.axis_size("section")
    replicas = lax.axis_size("dp")
    section = lax.axis_index("section")
    replica = lax.axis_index("dp")
    core, side = replica % 2, replica // 2 % 2
    rows, features = inputs.shape[1:]
    half = features // 2
    wide_w, down_w, vector = wide[0], down[0], vectors[0]
    x, cot = inputs[0], cotangent[0]

    fourth = 2 * side + core
    who = jnp.stack([section, core, fourth]).astype(jnp.int32)
    att_part, mlp_part = pl.pallas_call(
        parts_kernel,
        out_shape=[jax.ShapeDtypeStruct((2 * features, features), BF)] * 2,
        in_specs=[SMEM, ANY, ANY],
        out_specs=[ANY, ANY],
        scratch_shapes=[pltpu.VMEM((2 * features, features), BF)] * 2 + [pltpu.SemaphoreType.DMA((9,))],
        compiler_params=pltpu.CompilerParams(vmem_limit_bytes=LIMIT),
    )(who, wide_w, down_w)
    att_first = send(att_part, ATT_WAYS, 0, 1)
    near = [swap_section(vector, bits) for bits in (1, 2, 3)]
    mlp_first = send(mlp_part, MLP_WAYS, 0, 1)
    x_sib = swap_core(x)
    every_vector = jnp.stack([vector] + near)
    avec, mvec = pick(every_vector, section), pick(every_vector, section ^ 1)
    att_second = send(after(att_part, every_vector, mlp_first), ATT_WAYS, 0, 2)
    att_last = send(att_first, ATT_WAYS, 1, 3)
    mlp_second = send(after(mlp_part, every_vector, att_first, x_sib), MLP_WAYS, 0, 2)
    mlp_last = send(after(mlp_first, att_first), MLP_WAYS, 1, 3)

    grid = lambda values: values.reshape(-1, SEG, features)
    heads = lambda values: grid(values)[:, 0]
    count = sections * (rows // SEG)
    is_cls = (jnp.arange(rows) % SEG == 0)[:, None]
    b_own = after(jnp.where(is_cls, jnp.zeros_like(cot), cot), every_vector)
    b_next = swap_dp(b_own, 2)
    b_sib, b_far = swap_core(b_own), swap_core(b_next)
    layout = row_layout(seg_counts[0])

    bf = lambda *shape: (shape, BF)
    att_who = jnp.stack([place_of(ATT_WAYS, section, core), section]).astype(jnp.int32)
    att_choices = [att_part, att_first, att_second, att_last]
    att_weights = [pltpu.VMEM((features, 3 * half), BF), pltpu.VMEM((half, features), BF)]
    triple, a, give0, keep0 = call(
        att_fwd_kernel,
        [bf(2 * rows, 3 * half), bf(2 * rows, half), bf(rows, features), bf(rows, features)],
        [att_who, after(x, b_sib, b_far), x_sib, avec, *att_choices],
        att_weights
        + [pltpu.VMEM((2, rows, 3 * half), BF), pltpu.VMEM((2, rows, half), BF), pltpu.VMEM((2, rows, features), BF)]
        + [pltpu.SemaphoreType.DMA((10,))],
        scalars=1,
        anywhere=4,
        outside=True,
    )
    core0 = swap_core(give0)

    def hop(values, start, end):
        return permute(values, lambda s, r: (end, r), lambda s, r: s == start)

    def on(column, run):
        return lax.cond(section == column, lambda: run()[0], lambda: jnp.zeros((count, 2 * features), BF))

    branch = heads(keep0).astype(F32) + heads(core0).astype(F32)
    cls1_own = (heads(x).astype(F32) + branch + avec[2:3]).astype(BF)
    cls1 = jnp.concatenate(to_column(jnp.concatenate([cls1_own, heads(cot)], 1), 1), 0)
    h1, u_own = call(att_join_kernel, [bf(rows, features)] * 2, [x, keep0, after(core0, cls1_own), avec, mvec])
    u_own = after(u_own, cls1)
    u_next, u_sib = swap_dp(u_own, 2), swap_core(u_own)
    cls2 = on(1, lambda: cls_step("out", cls1, cls1, wide_w, down_w, vector))
    cls2_at2 = hop(cls2, 1, 2)

    square = bf(features, features)
    scratch = [pltpu.VMEM((2 * rows, features), BF)] * 4 + [pltpu.VMEM(*square)] * 2
    scratch += [pltpu.VMEM((2, 2 * rows, features), BF)] + [pltpu.VMEM((2, features, features), BF)] * 2
    scratch += [pltpu.SemaphoreType.DMA((18,))]
    mlp_who = jnp.stack([place_of(MLP_WAYS, section, core), section // 2]).astype(jnp.int32)
    mlp_choices = [mlp_part, mlp_first, mlp_second, mlp_last]
    keep1, give1, dw, dv = call(
        partial(mlp_kernel, False),
        [bf(2 * rows, features)] * 2 + [square] * 2,
        [mlp_who, after(u_own, cls2), u_sib, b_own, b_sib, *mlp_choices],
        scratch,
        scalars=1,
        anywhere=8,
        outside=True,
    )
    u_far = swap_core(after(u_next, dw))
    keep2, give2, near_half, far_half = call(
        partial(mlp_kernel, True),
        [bf(2 * rows, features)] * 2 + [bf(2, half, features)] * 2,
        [mlp_who, after(u_next, cls2_at2), u_far, b_next, b_far, *mlp_choices, dw, dv],
        scratch,
        scalars=1,
        anywhere=10,
        outside=True,
    )
    core1, core2 = swap_core(give1), swap_core(give2)

    shape = [bf(count, 2 * features)]
    near_row = swap_section(far_half, 2)
    cls2_at2 = after(cls2_at2, far_half)
    blanks = lambda: [jnp.zeros((count, 2 * features), BF), jnp.zeros((count, 3 * features), BF)]
    cls3, cls_triple = lax.cond(
        section == 2,
        lambda: list(
            call(
                cls_att_fwd_kernel,
                shape + [bf(count, 3 * features)],
                [cls2_at2, *layout, wide_w, vector],
                [pltpu.VMEM((features, 4 * features), BF), pltpu.SemaphoreType.DMA((4,))],
                inside=4,
            )
        ),
        blanks,
    )
    cls3_at3 = hop(cls3, 2, 3)
    dcls3 = on(3, lambda: cls_step("both", cls3_at3, cls3_at3, wide_w, down_w, vector))
    dcls3_at2 = hop(dcls3, 3, 2)
    pair = pair_sum(keep2, after(core2, cls3))
    du_next = swap_dp(pair[:rows], 2)
    dcls2 = on(
        2, lambda: call(
            partial(cls_att_bwd_kernel, False),
            shape,
            [cls2_at2, dcls3_at2, cls_triple, *layout, wide_w, vector],
            [pltpu.VMEM((features, 4 * features), BF), pltpu.SemaphoreType.DMA((4,))],
            inside=6,
        )
    )
    dh1, mlp_small = call(
        mlp_done_kernel,
        [bf(rows, features), ((8, features), F32)],
        [h1, b_own, keep1, core1, du_next, mvec],
    )
    dcls2_at1 = after(hop(dcls2, 2, 1), dh1, near_row)
    out_next = swap_dp(after(pair[rows:], du_next), 2)
    dcls1 = on(1, lambda: cls_step("back", cls1, dcls2_at1, wide_w, down_w, vector))

    mine_in = jnp.where(section == 1, cls1, jnp.where(section == 2, cls2_at2, cls3_at3))
    mine_grad = jnp.where(section == 1, dcls2_at1[:, :features], dcls3_at2[:, :features])
    mine_grad = jnp.where(section == 3, cls3_at3[:, features:], mine_grad)
    marks = jnp.pad(jnp.concatenate([layout[0][:, :1], layout[1][:, :1] % (SEGS + 1)], 1), ((0, 0), (0, features - 2)))
    everything = jnp.concatenate([mine_in[:, :features], mine_grad, marks.astype(BF)], 0)
    split = dcls1.reshape(sections, rows // SEG, 2 * features)
    arrived = [hop(split[1 ^ bits], 1, 1 ^ bits) for bits in (1, 2, 3)]
    back_rows = jnp.where(section == 1, split[1], arrived[0] + arrived[1] + arrived[2])

    place = lambda values, cls: lax.dynamic_update_slice(grid(values), cls[:, None], (0, 0, 0)).reshape(rows, features)
    dh1 = place(dh1, back_rows[:, :features])
    dh1_sib = swap_core(dh1)


    xbit = section % 2
    mlp_half = pair_sum(near_half, near_row)
    near_block = swap_section(after(pick(mlp_half, 1 - xbit), dcls1), 1)
    mlp_block = pair_sum(pick(mlp_half, xbit), near_block)
    mlp_sum, bits = mlp_block, 4
    while bits < replicas:
        other = swap_dp(jnp.concatenate([mlp_sum, everything], 0), bits)
        mlp_sum = pair_sum(mlp_sum, other[:half])
        everything = ordered(everything, other[half:], replica & bits != 0)
        bits *= 2

    *att_grads, du0_own, du0_sib = call(
        att_bwd_kernel,
        [bf(half + 16, features)] * 4 + [bf(rows, features)] * 2,
        [att_who, avec, mlp_small, after(x, out_next, mlp_block), x_sib, dh1, dh1_sib, triple, a, *att_choices],
        [pltpu.VMEM((2 * rows, features), BF)] * 2
        + [pltpu.VMEM((2 * rows, 3 * half), BF), pltpu.VMEM((2 * rows, half), BF), *att_weights]
        + [pltpu.VMEM((2 * rows, features), BF), pltpu.VMEM((2 * rows, 3 * half), BF)]
        + [pltpu.VMEM((2, rows, features), BF), pltpu.VMEM((4, half + 16, features), BF)]
        + [pltpu.SemaphoreType.DMA((26,))],
        scalars=1,
        anywhere=10,
        outside=True,
        cost=17,
    )
    du0_core = swap_core(du0_sib)
    (input_grad,) = call(att_done_kernel, [bf(rows, features)], [x, dh1, du0_own, du0_core, avec])

    branch = keep1[rows:].astype(F32) + core1[rows:].astype(F32) + out_next.astype(F32)
    h2 = (h1.astype(F32) + branch + mvec[2:3]).astype(BF)
    layer_out = place(h2, back_rows[:, features:])
    other = swap_dp(jnp.concatenate([mlp_sum, everything], 0), 2)
    mlp_next, everything = other[:half], ordered(everything, other[half:], replica & 2 != 0)
    everything = ordered(everything, swap_core(everything), replica & 1 != 0).reshape(-1, 3, count, features)
    received, layer_out, input_grad = lax.optimization_barrier((section_parts(att_grads), layer_out, input_grad))
    att_block = section_sum(att_grads, received)
    mlp_blocks = jnp.stack(after([mlp_sum, mlp_next], att_block))
    att_block = pair_sum(att_block, swap_dp(att_block, 2))
    all_in, all_grad, marks = [everything[:, k].reshape(-1, features) for k in range(3)]
    all_pos, all_doc = marks[:, :1].astype(jnp.int32), marks[:, 1:2].astype(jnp.int32)
    all_doc += jnp.arange(all_doc.shape[0], dtype=jnp.int32)[:, None] // SEGS * (SEGS + 1)
    all_layout = (wide_column(all_pos), wide_column(all_doc), all_doc.reshape(1, -1))
    total = all_in.shape[0]
    none = lambda: [blank((total, features), BF)] + [blank((total, wide_w.shape[1]), BF) for _ in range(2)]

    def first_column():
        return [jnp.zeros(vector.shape, F32), blank(wide_w.shape), jnp.zeros(down_w.shape, F32), *none()]

    def second_column():
        sums, *factors = cls_mlp("factors", all_in, all_grad, wide_w, down_w, vector)
        return [sums, blank(wide_w.shape), blank(down_w.shape), *factors]

    def third_column():
        sums, wide_sum = cls_att_weights(all_in, all_grad, all_layout, wide_w, vector)
        return [sums, wide_sum, blank(down_w.shape), *none()]

    def fourth_column():
        return [*cls_mlp("weights", all_in, all_grad, wide_w, down_w, vector), *none()]

    vector_sum, wide_sum, down_sum, u_cls, dh_cls, act_cls = lax.switch(
        section, [first_column, second_column, third_column, fourth_column]
    )
    mlp_own = to_column(mlp_blocks, 1)
    att_block = pair_sum(att_block, after(swap_dp(att_block, 4), u_cls, mlp_own))
    att_block = dp_sum(att_block, 8)
    small = att_block[half:]
    small = (small.astype(F32) + swap_core(small).astype(F32))[:3]
    mine_small = jnp.where(section < 2, small, 0.0)
    vector_sum = vector_sum + jnp.pad(mine_small, ((0, vector.shape[0] - 3), (0, 0)))
    att_own, vector_sum = lax.optimization_barrier((to_column(att_block[:half], 0), vector_sum))
    att_other = [swap_core(piece) for piece in att_own]
    mlp_own = after(mlp_own, att_own)
    mlp_other = [swap_core(piece) for piece in mlp_own]
    wide_like, down_like = jax.ShapeDtypeStruct(wide_w.shape, F32), jax.ShapeDtypeStruct(down_w.shape, F32)
    for part, (att_pieces, mlp_pieces) in enumerate(((att_own, mlp_own), (att_other, mlp_other))):
        if part:
            att_pieces, mlp_pieces = after([att_pieces, mlp_pieces], wide_sum)
        wide_sum = pl.pallas_call(
            partial(att_place_kernel, part),
            out_shape=wide_like,
            in_specs=[SMEM] + [ANY] * 5,
            out_specs=ANY,
            scratch_shapes=[
                pltpu.VMEM((4, half, features), BF),
                pltpu.VMEM((features, 3 * half), F32),
                pltpu.VMEM((half, features), F32),
                pltpu.SemaphoreType.DMA((4,)),
                pltpu.SemaphoreType.DMA((4,)),
            ],
            input_output_aliases={5: 0},
            cost_estimate=estimate(0),
            compiler_params=pltpu.CompilerParams(vmem_limit_bytes=LIMIT),
        )(who, *att_pieces, wide_sum)
        wide_sum, down_sum = pl.pallas_call(
            partial(mlp_place_kernel, part),
            out_shape=[wide_like, down_like],
            in_specs=[SMEM] + [VMEM] * 4 + [ANY] * 6,
            out_specs=[ANY, ANY],
            scratch_shapes=[
                pltpu.VMEM((4, 2, half, features), BF),
                pltpu.VMEM((2, features, features), F32),
                pltpu.VMEM((2, features, features), F32),
                pltpu.SemaphoreType.DMA((4,)),
                pltpu.SemaphoreType.DMA((4,)),
            ],
            input_output_aliases={9: 0, 10: 1},
            cost_estimate=estimate(0),
            compiler_params=pltpu.CompilerParams(vmem_limit_bytes=LIMIT),
        )(who, u_cls, all_grad, dh_cls, act_cls, *mlp_pieces, wide_sum, down_sum)
    return layer_out[None], input_grad[None], wide_sum[None], down_sum[None], vector_sum[None]


def solution(mesh):
    return jax.shard_map(
        local,
        mesh=mesh,
        in_specs=(
            P("section", "dp", None),
            P("section", "dp", None),
            P("section", None, None),
            P("section", None, None),
            P("section", None, None),
            P("dp", None, None),
        ),
        out_specs=(
            P("section", "dp", None),
            P("section", "dp", None),
            P("section", None, None),
            P("section", None, None),
            P("section", None, None),
        ),
        check_vma=False,
    )
```

```python
from functools import partial

import jax
import jax.numpy as jnp
from jax import lax
from jax.experimental import pallas as pl
from jax.experimental.pallas import tpu as pltpu
from jax.sharding import PartitionSpec as P

HEADS = 12
SEG = 128
SEGS = 4
EPSILON = 1e-05
SCORE_SCALE = 0.125
MASKED = -1e30
AXES = ("section", "dp")
BF = jnp.bfloat16
F32 = jnp.float32

NN = (((1,), (0,)), ((), ()))
NT = (((1,), (1,)), ((), ()))
TN = (((0,), (0,)), ((), ()))

GELU_A = 0.7978845608028654
GELU_B = 0.044715

ATT_WAYS = ((0, 1, 2, 3), (0, 2, 1, 3))
MLP_WAYS = ((1, 0, 3, 2), (1, 3, 0, 2))


def mm(left, right, dims=NN):
    return lax.dot_general(left, right, dims, preferred_element_type=F32)


def permute(shard, move, keep=lambda s, r: True):
    sections, replicas = lax.axis_size("section"), lax.axis_size("dp")
    pairs = []
    for s in range(sections):
        for r in range(replicas):
            if keep(s, r):
                t, q = move(s, r)
                pairs.append((s * replicas + r, t * replicas + q))
    return lax.ppermute(shard, AXES, pairs)


def swap_core(shard):
    return permute(shard, lambda s, r: (s, r ^ 1))


def swap_section(shard, bits):
    return permute(shard, lambda s, r: (s ^ bits, r))


def swap_dp(shard, bits):
    return permute(shard, lambda s, r: (s, r ^ bits))


def send(values, ways, start, end):
    return permute(values, lambda s, r: (ways[r & 1][end], r), lambda s, r: ways[r & 1][start] == s)


def after(value, *marks):
    return lax.optimization_barrier((value, marks))[0]


def place_of(ways, section, core):
    position = jnp.int32(0)
    for c in range(2):
        for k, s in enumerate(ways[c]):
            position = jnp.where((section == s) & (core == c), k, position)
    return position


def pick(stack, index):
    return lax.dynamic_index_in_dim(stack, index, 0, keepdims=False)


def section_parts(parts):
    return [swap_section(parts[bits], bits) for bits in (1, 2, 3)]


def section_sum(parts, others=None):
    others = others or section_parts(parts)
    return sum([other.astype(F32) for other in others], parts[0].astype(F32)).astype(BF)


def dp_sum(value, bits):
    while bits < lax.axis_size("dp"):
        value = pair_sum(value, swap_dp(value, bits))
        bits *= 2
    return value


def pair_sum(mine, other):
    return (mine.astype(F32) + other.astype(F32)).astype(BF)


def ordered(first, second, swapped):
    return jnp.where(swapped, jnp.concatenate([second, first], 0), jnp.concatenate([first, second], 0))


def to_column(value, owner):
    arrived = [permute(value, lambda s, r: (owner, r), lambda s, r: s == owner ^ bits) for bits in (1, 2, 3)]
    columns = [None] * 4
    columns[owner] = value
    for bits, other in zip((1, 2, 3), arrived):
        columns[owner ^ bits] = other
    return columns


def fetch(sources, targets, sems):
    return [pltpu.make_async_copy(source, target, sems.at[i]) for i, (source, target) in enumerate(zip(sources, targets))]


def norm_parts(values):
    center = values - jnp.mean(values, -1, keepdims=True)
    spread = jnp.mean(center * center, -1, keepdims=True)
    scale = lax.rsqrt(spread + EPSILON)
    return center * scale, scale


def norm_rows(values, vec_ref):
    hat, _ = norm_parts(values)
    return hat * vec_ref[0:1, :] + vec_ref[1:2, :]


def norm_back(values, grad_normed, vec_ref):
    hat, scale = norm_parts(values)
    inner = grad_normed * vec_ref[0:1, :]
    first = jnp.mean(inner, -1, keepdims=True)
    second = jnp.mean(inner * hat, -1, keepdims=True)
    return scale * (inner - first - hat * second), grad_normed * hat


def column_sum(values):
    return jnp.sum(values, 0, keepdims=True)


def gelu_parts(hidden):
    square = hidden * hidden
    inner = GELU_A * hidden * (1.0 + GELU_B * square)
    t = jnp.tanh(inner)
    half = 0.5 * (1.0 + t)
    slope = half + 0.5 * hidden * (1.0 - t * t) * (GELU_A * (1.0 + 3.0 * GELU_B * square))
    return hidden * half, slope


def two_heads(pair):
    low = lax.broadcasted_iota(jnp.int32, pair.shape, 1) < 64
    zero = jnp.zeros_like(pair)
    return jnp.concatenate([jnp.where(low, pair, zero), jnp.where(low, zero, pair)], 0)


def join_heads(both):
    rows = both.shape[0] // 2
    low = lax.broadcasted_iota(jnp.int32, (rows, both.shape[1]), 1) < 64
    return jnp.where(low, both[:rows], both[rows:])


def softmax_rows(scores):
    powers = jnp.exp(scores - jnp.max(scores, -1, keepdims=True))
    return powers / jnp.sum(powers, -1, keepdims=True)


def softmax_columns(scores):
    powers = jnp.exp(scores - jnp.max(scores, 0, keepdims=True))
    return powers * (1.0 / jnp.sum(powers, 0, keepdims=True))


def head_pairs(q, k, v, out):
    for seg in range(q.shape[0] // SEG):
        at = slice(seg * SEG, (seg + 1) * SEG)
        mixed = []
        for pair in range(q.shape[1] // 128):
            lanes = slice(pair * 128, (pair + 1) * 128)
            probs = softmax_columns(mm(k[at, lanes], two_heads(q[at, lanes]), NT) * SCORE_SCALE)
            mixed.append(join_heads(mm(probs.astype(BF), v[at, lanes], TN)).astype(BF))
        out.append(jnp.concatenate(mixed, 1))


class Copies:
    def __init__(self, sems):
        self.sems, self.used = sems, 0

    def next(self):
        self.used += 1
        return self.sems.at[self.used - 1]

    def start(self, source, target):
        sem = self.next()
        send_parts(source, target, sem)
        return pltpu.make_async_copy(source, target, sem)

    def choose(self, which, sources, target):
        sem = self.next()
        for k, source in enumerate(sources):

            @pl.when(which == k)
            def _():
                send_parts(source, target, sem)

        return pltpu.make_async_copy(sources[0], target, sem)


def send_parts(source, target, sem):
    rows = source.shape[0]
    step = rows // 4 if rows % 64 == 0 else rows
    for start in range(0, rows, step):
        part = pl.ds(start, step)
        pltpu.make_async_copy(source.at[part], target.at[part], sem).start()


def wait(*copies):
    for copy in copies:
        copy.wait()


def load_triple(copies, place, choices, wt, half):
    features, left, right = wt.shape[0], pl.ds(0, half), pl.ds(half, half)
    return [
        copies.choose(place, [c.at[pl.ds(0, features), :] for c in choices], wt.at[:, pl.ds(0, features)]),
        copies.choose(place, [c.at[pl.ds(features, half), left] for c in choices], wt.at[left, pl.ds(features, half)]),
        copies.choose(place, [c.at[pl.ds(features, half), right] for c in choices], wt.at[right, pl.ds(features, half)]),
    ]


def att_fwd_kernel(place_ref, own_ref, sib_ref, vec_ref, *refs):
    choices, (triple_ref, a_ref, give_ref, keep_ref, wt, wo, triples, mixes, outs, sems) = refs[:4], refs[4:]
    rows, features = own_ref.shape
    half = a_ref.shape[1]
    copies = Copies(sems)
    wt_in = load_triple(copies, place_ref[0], choices, wt, half)
    wo_in = [copies.choose(place_ref[0], [c.at[pl.ds(features + half, half), :] for c in choices], wo)]
    done = []
    for pack, (ref, out) in enumerate(((sib_ref, give_ref), (own_ref, keep_ref))):
        span = pl.ds((1 - pack) * rows, rows)
        u = norm_rows(ref[...].astype(F32), vec_ref).astype(BF)
        if pack == 0:
            wait(*wt_in)
        triple = mm(u, wt[...]).astype(BF)
        triples[pack] = triple
        done.append(copies.start(triples.at[pack], triple_ref.at[span, :]))
        mixed = []
        head_pairs(triple[:, :half], triple[:, half : 2 * half], triple[:, 2 * half :], mixed)
        a = jnp.concatenate(mixed, 0)
        mixes[pack] = a
        done.append(copies.start(mixes.at[pack], a_ref.at[span, :]))
        if pack == 0:
            wait(*wo_in)
        outs[pack] = mm(a, wo[...]).astype(BF)
        done.append(copies.start(outs.at[pack], out))
    wait(*done)


def att_bwd_kernel(place_ref, vec_ref, small_ref, *refs):
    own_ref, sib_ref, gown_ref, gsib_ref, triple_ref, a_ref, *choices = refs[:10]
    grad_refs, (duown_ref, dusib_ref, xs, gs, triple, mixes, wt, wo, u, dt, dus, piece, sems) = refs[10:14], refs[14:]
    rows = own_ref.shape[0]
    half = a_ref.shape[1]
    part = half // 4
    copies = Copies(sems)
    gs_in = [copies.start(gown_ref, gs.at[pl.ds(0, rows), :])]
    early = copies.choose(place_ref[0], [c.at[pl.ds(wt.shape[0] + half, half), :] for c in choices], wo)
    triple_in = [copies.start(triple_ref.at[pl.ds(k * rows, rows), :], triple.at[pl.ds(k * rows, rows), :]) for k in range(2)]
    xs_in = [copies.start(own_ref, xs.at[pl.ds(0, rows), :])]
    wt_in = load_triple(copies, place_ref[0], choices, wt, half)
    gs_in.append(copies.start(gsib_ref, gs.at[pl.ds(rows, rows), :]))
    xs_in.append(copies.start(sib_ref, xs.at[pl.ds(rows, rows), :]))
    a_in = copies.start(a_ref, mixes)
    done = []
    gain = shift = 0.0
    for pack, out in enumerate((duown_ref, dusib_ref)):
        span = slice(pack * rows, (pack + 1) * rows)
        wait(gs_in[pack])
        if pack == 0:
            wait(early)
        da = mm(gs[span, :], wo[...], NT).astype(BF)
        wait(triple_in[pack])
        for seg in range(rows // SEG):
            at = slice(seg * SEG, (seg + 1) * SEG)
            to = slice(pack * rows + seg * SEG, pack * rows + (seg + 1) * SEG)
            for pair in range(half // 128):
                lanes = [slice(kind * half + pair * 128, kind * half + (pair + 1) * 128) for kind in range(3)]
                q2, k, v = two_heads(triple[to, lanes[0]]), triple[to, lanes[1]], triple[to, lanes[2]]
                da2 = two_heads(da[at, lanes[0]])
                probs = softmax_columns(mm(k, q2, NT) * SCORE_SCALE)
                dy = mm(v, da2, NT)
                ds = (probs * (dy - jnp.sum(dy * probs, 0, keepdims=True))).astype(BF)
                dt[to, lanes[2]] = mm(probs.astype(BF), da2).astype(BF)
                dt[to, lanes[0]] = (join_heads(mm(ds, k, TN)) * SCORE_SCALE).astype(BF)
                dt[to, lanes[1]] = (mm(ds, q2) * SCORE_SCALE).astype(BF)
        wait(xs_in[pack])
        hat, _ = norm_parts(xs[span, :].astype(F32))
        u[span, :] = (hat * vec_ref[0:1, :] + vec_ref[1:2, :]).astype(BF)
        if pack == 0:
            wait(*wt_in)
        du = mm(dt[span, :], wt[...], NT)
        dus[pack] = du.astype(BF)
        done.append(copies.start(dus.at[pack], out))
        gain = gain + column_sum(du * hat)
        shift = shift + column_sum(du)

    def send(start, count):
        at = pl.ds(start, count)
        for bits, ref in enumerate(grad_refs):
            done.append(copies.start(piece.at[place_ref[1] ^ bits, at, :], ref.at[at, :]))

    dw = mm(u[...], dt[:, : 2 * half], TN)
    for quarter in range(4):
        piece[quarter, : 2 * part, :] = dw[quarter * 2 * part : (quarter + 1) * 2 * part, :].astype(BF)
    send(0, 2 * part)
    dw = mm(u[...], dt[:, 2 * half :], TN)
    for quarter in range(4):
        for side in range(2):
            piece[quarter, 2 * part : 3 * part, side * half : (side + 1) * half] = dw[
                side * half + quarter * part : side * half + (quarter + 1) * part, :
            ].astype(BF)
    send(2 * part, part)
    wait(a_in)
    dw = mm(mixes[...], gs[...], TN)
    piece[:, 4 * part :, :] = jnp.zeros((4, 16, piece.shape[2]), BF)
    rest = jnp.zeros((13, piece.shape[2]), F32)
    sums = [gain, shift, column_sum(gs[:rows, :].astype(F32)), rest]
    piece[0, 4 * part :, :] = jnp.concatenate(sums, 0).astype(BF)
    piece[1, 4 * part :, :] = jnp.concatenate([small_ref[...], small_ref[...]], 0).astype(BF)
    for quarter in range(4):
        piece[quarter, 3 * part : 4 * part, :] = dw[quarter * part : (quarter + 1) * part, :].astype(BF)
    send(3 * part, part + 16)
    wait(*done)


def att_done_kernel(x_ref, g_ref, duown_ref, dusib_ref, vec_ref, out_ref):
    du = duown_ref[...].astype(F32) + dusib_ref[...].astype(F32)
    back, _ = norm_back(x_ref[...].astype(F32), du, vec_ref)
    out_ref[...] = (g_ref[...].astype(F32) + back).astype(BF)


def att_join_kernel(x_ref, keep_ref, core_ref, avec_ref, mvec_ref, h_ref, u_ref):
    branch = keep_ref[...].astype(F32) + core_ref[...].astype(F32)
    out = (x_ref[...].astype(F32) + branch + avec_ref[2:3, :]).astype(BF)
    h_ref[...] = out
    u_ref[...] = norm_rows(out.astype(F32), mvec_ref).astype(BF)


def mlp_kernel(last, who_ref, *refs):
    uown_ref, usib_ref, bown_ref, bsib_ref, *choices = refs[:8]
    before, refs = refs[8 : 10 if last else 8], refs[10 if last else 8 :]
    keep_ref, give_ref, first_ref, second_ref, u, b, act, dhs, w, v, outs, dws, held, sems = refs
    rows = uown_ref.shape[0]
    size = w.shape[0]
    copies = Copies(sems)
    us_in, bs_in, done = [None, None], [None, None], []
    us_in[1] = copies.start(usib_ref, u.at[pl.ds(rows, rows), :])
    w_in = copies.choose(who_ref[0], [c.at[pl.ds(0, size), :] for c in choices], w)
    bs_in[1] = copies.start(bsib_ref, b.at[pl.ds(rows, rows), :])
    v_in = copies.choose(who_ref[0], [c.at[pl.ds(size, size), :] for c in choices], v)
    for pack, out in ((1, give_ref), (0, keep_ref)):
        at = slice(pack * rows, (pack + 1) * rows)
        wait(us_in[pack])
        if pack == 1:
            wait(w_in)
            us_in[0] = copies.start(uown_ref, u.at[pl.ds(0, rows), :])
            bs_in[0] = copies.start(bown_ref, b.at[pl.ds(0, rows), :])
        active, slope = gelu_parts(mm(u[at, :], w[...]))
        act[at, :] = active.astype(BF)
        wait(bs_in[pack])
        if pack == 1:
            wait(v_in)
            before_in = [copies.start(ref, held.at[k]) for k, ref in enumerate(before)]
        dhs[at, :] = (mm(b[at, :], v[...], NT) * slope).astype(BF)
        outs[pack, :rows, :] = mm(dhs[at, :], w[...], NT).astype(BF)
        outs[pack, rows:, :] = mm(act[at, :], v[...]).astype(BF)
        done.append(copies.start(outs.at[pack], out))
    quarter = size // 4
    for kind, (left, right) in enumerate(((u, dhs), (act, b))):
        dw = mm(left[...], right[...], TN)
        if not last:
            dws[kind] = dw.astype(BF)
            done.append(copies.start(dws.at[kind], (first_ref, second_ref)[kind]))
            continue
        wait(before_in[kind])
        dws[kind] = (dw + held[kind].astype(F32)).astype(BF)
        for k in range(2):
            sem = copies.next()
            target = (first_ref, second_ref)[k].at[:, pl.ds(kind * quarter, quarter), :]
            for y in range(2):
                source = dws.at[kind, pl.ds((y ^ k) * 2 * quarter, 2 * quarter), :].reshape(2, quarter, size)

                @pl.when(who_ref[1] == y)
                def _():
                    pltpu.make_async_copy(source, target, sem).start()

            done.append(pltpu.make_async_copy(source, target, sem))
    wait(*done)


def mlp_done_kernel(h_ref, b_ref, keep_ref, core_ref, z_ref, vec_ref, grad_ref, small_ref):
    rows = h_ref.shape[0]
    du = keep_ref[:rows, :].astype(F32) + core_ref[:rows, :].astype(F32) + z_ref[...].astype(F32)
    grad = b_ref[...].astype(F32)
    back, gain = norm_back(h_ref[...].astype(F32), du, vec_ref)
    grad_ref[...] = (grad + back).astype(BF)
    small_ref[...] = jnp.zeros_like(small_ref)
    small_ref[0:1, :] = column_sum(gain)
    small_ref[1:2, :] = column_sum(du)
    small_ref[2:3, :] = column_sum(grad)


def cls_step_kernel(mode, h_ref, b_ref, vec_ref, w_ref, v_ref, out_ref, w, v, sems):
    forward, backward = mode in ("out", "both"), mode in ("back", "both")
    features, hidden = w_ref.shape
    copies = Copies(sems)
    spans = [slice(start, start + features) for start in range(0, hidden, features)]
    loads = []
    for span in spans:
        at = pl.ds(span.start, features)
        loads.append((copies.start(w_ref.at[:, at], w.at[:, at]), copies.start(v_ref.at[at, :], v.at[at, :])))
    values = h_ref[:, :features].astype(F32)
    u = norm_rows(values, vec_ref).astype(BF)
    b = b_ref[:, -features:] if mode == "both" else b_ref[:, :features]
    out = du = 0.0
    for span, (w_in, v_in) in zip(spans, loads):
        w_in.wait()
        active, slope = gelu_parts(mm(u, w[:, span]))
        v_in.wait()
        if forward:
            out = out + mm(active.astype(BF), v[span, :])
        if backward:
            dh = (mm(b, v[span, :], NT) * slope).astype(BF)
            du = du + mm(dh, w[:, span], NT)
    if forward:
        out = (values + out + vec_ref[2:3, :]).astype(BF)
    if backward:
        back, _ = norm_back(values, du, vec_ref)
        back = (b.astype(F32) + back).astype(BF)
    out_ref[:, :features] = back if backward else out
    out_ref[:, features:] = {"out": h_ref, "back": b_ref}[mode][:, features:] if mode != "both" else out


def cls_mlp_kernel(mode, h_ref, b_ref, w_ref, v_ref, vec_ref, *refs):
    features = w_ref.shape[0]
    forward, backward = mode in ("out", "both"), mode in ("back", "both")
    weights, factors = mode == "weights", mode == "factors"
    j = pl.program_id(0)
    if weights:
        small_ref, dw_ref, dv_ref, u_ref, out_acc, du_acc = refs
    elif factors:
        small_ref, u_ref, dh_ref, act_ref, out_acc, du_acc = refs
    else:
        out_ref, u_ref, out_acc, du_acc = refs

    @pl.when(j == 0)
    def _():
        u_ref[...] = norm_rows(h_ref[:, :features].astype(F32), vec_ref).astype(BF)
        out_acc[...] = jnp.zeros_like(out_acc)
        du_acc[...] = jnp.zeros_like(du_acc)

    u = u_ref[...]
    active, slope = gelu_parts(mm(u, w_ref[...]))
    active = active.astype(BF)
    if forward:
        out_acc[...] += mm(active, v_ref[...])
    if not forward or backward:
        b = b_ref[:, -features:] if mode == "both" else b_ref[:, :features]
        dh = (mm(b, v_ref[...], NT) * slope).astype(BF)
        du_acc[...] += mm(dh, w_ref[...], NT)
    if weights:
        dw_ref[...] = mm(u, dh, TN)
        dv_ref[...] = mm(active, b, TN)
    if factors:
        dh_ref[...] = dh
        act_ref[...] = active

    @pl.when(j == pl.num_programs(0) - 1)
    def _():
        values = h_ref[:, :features].astype(F32)
        if forward:
            out = (values + out_acc[...] + vec_ref[2:3, :]).astype(BF)
        if not forward or backward:
            grad = b.astype(F32)
            back, gain = norm_back(values, du_acc[...], vec_ref)
            back = (grad + back).astype(BF)
        if mode == "out":
            out_ref[:, :features] = out
            out_ref[:, features:] = h_ref[:, features:]
        if mode == "both":
            out_ref[:, :features] = back
            out_ref[:, features:] = out
        if mode == "back":
            out_ref[:, :features] = back
            out_ref[:, features:] = b_ref[:, features:]
        if weights or factors:
            small_ref[...] = jnp.zeros_like(small_ref)
            small_ref[0:1, :] = column_sum(gain)
            small_ref[1:2, :] = column_sum(du_acc[...])
            small_ref[2:3, :] = column_sum(grad)


def lifted_rows(h_ref, pos_ref, vec_ref):
    values = h_ref[:, : vec_ref.shape[1]].astype(F32)
    pos = pos_ref[:, :1]
    for p in range(SEGS):
        values = values + jnp.where(pos == p, vec_ref[3 + p : 4 + p, :], 0.0)
    return values


def cls_att_heads(triple, col_ref, row_ref):
    features = triple.shape[1] // 3
    column = jnp.concatenate([col_ref[:, :1], col_ref[:, :1]], 0)
    mask = column == row_ref[...]
    probs, mixed = [], []
    for pair in range(features // 128):
        lanes = slice(pair * 128, (pair + 1) * 128)
        q2 = two_heads(triple[:, lanes])
        k = triple[:, features + pair * 128 : features + (pair + 1) * 128]
        v = triple[:, 2 * features + pair * 128 : 2 * features + (pair + 1) * 128]
        scores = jnp.where(mask, mm(q2, k, NT) * SCORE_SCALE, MASKED)
        probs.append(softmax_rows(scores))
        mixed.append(join_heads(mm(probs[-1].astype(BF), v)).astype(BF))
    return probs, jnp.concatenate(mixed, 1)


def cls_att_fwd_kernel(h_ref, pos_ref, col_ref, row_ref, w_ref, vec_ref, out_ref, triple_ref, w, sems):
    features = vec_ref.shape[1]
    copies = Copies(sems)
    parts = [pl.ds(k * features, features) for k in range(4)]
    loads = [copies.start(w_ref.at[:, part], w.at[:, part]) for part in parts]
    values = lifted_rows(h_ref, pos_ref, vec_ref)
    u = norm_rows(values, vec_ref).astype(BF)
    for part, load in zip(parts[:3], loads):
        load.wait()
        triple_ref[:, part] = mm(u, w[:, part]).astype(BF)
    _, mixed = cls_att_heads(triple_ref[...], col_ref, row_ref)
    loads[3].wait()
    out_ref[:, :features] = (values + mm(mixed, w[:, 3 * features :]) + vec_ref[2:3, :]).astype(BF)
    out_ref[:, features:] = h_ref[:, features:]


def cls_att_bwd_kernel(weights_too, h_ref, g_ref, *refs):
    if weights_too:
        pos_ref, col_ref, row_ref, w_ref, vec_ref, *refs = refs
    else:
        triple_ref, pos_ref, col_ref, row_ref, source_ref, vec_ref, out_ref, w_ref, sems = refs
        features = vec_ref.shape[1]
        copies = Copies(sems)
        parts = [pl.ds(k * features, features) for k in (3, 0, 1, 2)]
        loads = [copies.start(source_ref.at[:, part], w_ref.at[:, part]) for part in parts]
    values = lifted_rows(h_ref, pos_ref, vec_ref)
    features = values.shape[1]
    if weights_too:
        u = norm_rows(values, vec_ref).astype(BF)
        triple = mm(u, w_ref[:, : 3 * features]).astype(BF)
    else:
        triple = triple_ref[...]
    probs, mixed = cls_att_heads(triple, col_ref, row_ref)
    b = g_ref[:, :features]
    if not weights_too:
        wait(loads[0])
    da = mm(b, w_ref[:, 3 * features :], NT).astype(BF)
    dqs, dks, dvs = [], [], []
    for pair in range(features // 128):
        lanes = slice(pair * 128, (pair + 1) * 128)
        q2 = two_heads(triple[:, lanes])
        k = triple[:, features + pair * 128 : features + (pair + 1) * 128]
        v = triple[:, 2 * features + pair * 128 : 2 * features + (pair + 1) * 128]
        da2 = two_heads(da[:, lanes])
        y = probs[pair]
        dy = mm(da2, v, NT)
        ds = (y * (dy - jnp.sum(dy * y, -1, keepdims=True))).astype(BF)
        dvs.append(mm(y.astype(BF), da2, TN).astype(BF))
        dqs.append((join_heads(mm(ds, k)) * SCORE_SCALE).astype(BF))
        dks.append((mm(ds, q2, TN) * SCORE_SCALE).astype(BF))
    dtriple = jnp.concatenate(dqs + dks + dvs, 1)
    if not weights_too:
        wait(*loads[1:])
    du = mm(dtriple, w_ref[:, : 3 * features], NT)
    back, gain = norm_back(values, du, vec_ref)
    grad = b.astype(F32)
    total = grad + back
    if weights_too:
        small_ref, dw_ref = refs

        @pl.when(pl.program_id(0) == 0)
        def _():
            small_ref[...] = jnp.zeros_like(small_ref)
            dw_ref[...] = jnp.zeros_like(dw_ref)

        small_ref[0:1, :] += column_sum(gain)
        small_ref[1:2, :] += column_sum(du)
        small_ref[2:3, :] += column_sum(grad)
        pos = pos_ref[:, :1]
        for p in range(SEGS):
            small_ref[3 + p : 4 + p, :] += column_sum(jnp.where(pos == p, total, 0.0))
        for part in range(3):
            span = slice(part * features, (part + 1) * features)
            dw_ref[:, span] += mm(u, dtriple[:, span], TN)
        dw_ref[:, 3 * features :] += mm(mixed, b, TN)
    else:
        out_ref[:, :features] = total.astype(BF)
        out_ref[:, features:] = g_ref[:, features:]


def parts_kernel(who_ref, wide_ref, down_ref, att_ref, mlp_ref, att, mlp, sems):
    features = down_ref.shape[1]
    half = features // 2
    lane = lambda kind: pl.ds(pl.multiple_of(kind * features + who_ref[1] * half, 128), half)
    quarter = pl.ds(pl.multiple_of(who_ref[2] * features, features), features)
    left, right, low, high = pl.ds(0, half), pl.ds(half, half), pl.ds(0, features), pl.ds(features, features)
    copies = Copies(sems)
    att_in = [
        copies.start(wide_ref.at[:, lane(0)], att.at[low, left]),
        copies.start(wide_ref.at[:, lane(1)], att.at[low, right]),
        copies.start(wide_ref.at[left, lane(2)], att.at[pl.ds(features, half), left]),
        copies.start(wide_ref.at[right, lane(2)], att.at[pl.ds(features, half), right]),
        copies.start(
            wide_ref.at[pl.ds(pl.multiple_of(who_ref[1] * half, half), half), pl.ds(3 * features, features)],
            att.at[pl.ds(features + half, half), :],
        ),
    ]
    mlp_in = [copies.start(wide_ref.at[:, quarter], mlp.at[low, :]), copies.start(down_ref.at[quarter, :], mlp.at[high, :])]
    wait(*att_in)
    done = [copies.start(att, att_ref)]
    wait(*mlp_in)
    done.append(copies.start(mlp, mlp_ref))
    wait(*done)


def att_place_kernel(part, who_ref, *refs):
    sources, (_, out_ref, held, triple, rest, sems, out_sems) = refs[:4], refs[4:]
    half = held.shape[1]
    step = half // 4

    @pl.when(who_ref[0] == 0)
    def _():
        core = who_ref[1] if part == 0 else 1 - who_ref[1]
        inward, outward = Copies(sems), Copies(out_sems)
        waits = [inward.start(source, held.at[k]) for k, source in enumerate(sources)]
        done = []
        for quarter in range(4):
            waits[quarter].wait()
            rows = slice(quarter * 2 * step, (quarter + 1) * 2 * step)
            triple[rows, : 2 * half] = held[quarter, : 2 * step, :].astype(F32)
            for side in range(2):
                row = side * half + quarter * step
                triple[row : row + step, 2 * half :] = held[
                    quarter, 2 * step : 3 * step, side * half : (side + 1) * half
                ].astype(F32)
            rest[quarter * step : (quarter + 1) * step, :] = held[quarter, 3 * step :, :].astype(F32)
        for kind in range(3):
            lanes = pl.ds(pl.multiple_of((2 * kind + core) * half, 128), half)
            done.append(outward.start(triple.at[:, pl.ds(kind * half, half)], out_ref.at[:, lanes]))
        rows = pl.ds(pl.multiple_of(core * half, half), half)
        done.append(outward.start(rest, out_ref.at[rows, pl.ds(6 * half, 2 * half)]))
        wait(*done)


def mlp_place_kernel(part, who_ref, u_ref, b_ref, dh_ref, act_ref, *refs):
    sources, (_, _, wide_ref, down_ref, held, dws, dvs, sems, out_sems) = refs[:4], refs[4:]
    size = dws.shape[1]
    step = size // 4

    if part == 0:

        @pl.when(who_ref[0] == 2)
        def _():
            dvs[0] = jnp.zeros_like(dvs[0])
            copies = fetch([dvs.at[0]] * 4, [down_ref.at[pl.ds(k * size, size), :] for k in range(4)], out_sems)
            for copy in copies:
                copy.start()
            wait(*copies)

    @pl.when(who_ref[0] == 1)
    def _():
        inward, outward = Copies(sems), Copies(out_sems)
        waits = [inward.start(source, held.at[k]) for k, source in enumerate(sources)]
        done = []
        for k in range(2):
            at = pl.ds(pl.multiple_of((who_ref[2] ^ (part + 2 * k)) * size, size), size)
            dws[k] = mm(u_ref[...], dh_ref[:, at], TN)
            dvs[k] = mm(act_ref[:, at], b_ref[...], TN)
            for quarter in range(4):
                if k == 0:
                    waits[quarter].wait()
                rows = slice(quarter * step, (quarter + 1) * step)
                dws[k, rows, :] += held[quarter, k, :step, :].astype(F32)
                dvs[k, rows, :] += held[quarter, k, step:, :].astype(F32)
            done.append(outward.start(dws.at[k], wide_ref.at[:, at]))
            done.append(outward.start(dvs.at[k], down_ref.at[at, :]))
        wait(*done)


VMEM = pl.BlockSpec(memory_space=pltpu.VMEM)
SMEM = pl.BlockSpec(memory_space=pltpu.SMEM)
ANY = pl.BlockSpec(memory_space=pl.ANY)
LIMIT = 58 * 2**20


def whole(shape):
    return pl.BlockSpec(shape, lambda i: (0,) * len(shape))


def estimate(microseconds):
    return pl.CostEstimate(flops=int(microseconds * 1.1e9), bytes_accessed=0, transcendentals=0)


def call(kernel, out_shapes, args, scratch=(), anywhere=0, scalars=0, outside=False, inside=None, cost=0):
    return pl.pallas_call(
        kernel,
        grid=(1,),
        out_shape=[jax.ShapeDtypeStruct(*shape) for shape in out_shapes],
        in_specs=[
            SMEM if k < scalars else ANY if k >= len(args) - anywhere or k == inside else whole(arg.shape)
            for k, arg in enumerate(args)
        ],
        out_specs=[ANY if outside else whole(shape[0]) for shape in out_shapes],
        scratch_shapes=list(scratch),
        compiler_params=pltpu.CompilerParams(vmem_limit_bytes=LIMIT),
        cost_estimate=estimate(cost),
    )(*args)


def blank(shape, dtype=F32):
    return pl.pallas_call(lambda out_ref: None, out_shape=jax.ShapeDtypeStruct(shape, dtype), out_specs=ANY)()


def cls_mlp(mode, rows, grads, wide_w, down_w, vector):
    count = rows.shape[0]
    features, hidden = wide_w.shape
    tile = features
    wide_block = pl.BlockSpec((features, tile), lambda j: (0, j))
    down_block = pl.BlockSpec((tile, features), lambda j: (j, 0))
    sums = jax.ShapeDtypeStruct(vector.shape, F32)
    scratch = [pltpu.VMEM((count, features), BF)] + [pltpu.VMEM((count, features), F32)] * 2
    if mode == "weights":
        out_shape = [sums, jax.ShapeDtypeStruct(wide_w.shape, F32), jax.ShapeDtypeStruct(down_w.shape, F32)]
        out_specs = [whole(vector.shape), wide_block, down_block]
    elif mode == "factors":
        out_shape = [sums, jax.ShapeDtypeStruct((count, features), BF)] + [jax.ShapeDtypeStruct((count, hidden), BF)] * 2
        out_specs = [whole(vector.shape), whole((count, features))] + [pl.BlockSpec((count, tile), lambda j: (0, j))] * 2
        scratch = scratch[1:]
    else:
        out_shape = [jax.ShapeDtypeStruct(rows.shape, BF)]
        out_specs = [whole(rows.shape)]
    return pl.pallas_call(
        partial(cls_mlp_kernel, mode),
        grid=(hidden // tile,),
        in_specs=[whole(rows.shape), whole(grads.shape), wide_block, down_block, whole(vector.shape)],
        out_specs=out_specs,
        out_shape=out_shape,
        scratch_shapes=scratch,
        compiler_params=pltpu.CompilerParams(vmem_limit_bytes=LIMIT),
    )(rows, grads, wide_w, down_w, vector)


def cls_step(mode, rows, grads, wide_w, down_w, vector):
    weights = [pltpu.VMEM(wide_w.shape, BF), pltpu.VMEM(down_w.shape, BF)]
    sems = pltpu.SemaphoreType.DMA((2 * wide_w.shape[1] // wide_w.shape[0],))
    return call(
        partial(cls_step_kernel, mode),
        [(rows.shape, BF)],
        [rows, grads, vector, wide_w, down_w],
        weights + [sems],
        anywhere=2,
    )


def cls_att_weights(rows, grads, layout, wide_w, vector):
    count, features = rows.shape
    block = min(count, 128)
    by_row = lambda width: pl.BlockSpec((block, width), lambda i: (i, 0))
    return pl.pallas_call(
        partial(cls_att_bwd_kernel, True),
        grid=(count // block,),
        in_specs=[
            by_row(features), by_row(features), by_row(128), by_row(128),
            pl.BlockSpec((1, block), lambda i: (0, i)), whole(wide_w.shape), whole(vector.shape),
        ],
        out_specs=[whole(vector.shape), whole(wide_w.shape)],
        out_shape=[jax.ShapeDtypeStruct(vector.shape, F32), jax.ShapeDtypeStruct(wide_w.shape, F32)],
        compiler_params=pltpu.CompilerParams(vmem_limit_bytes=LIMIT),
    )(rows, grads, *layout, wide_w, vector)


def documents(counts):
    ends = jnp.cumsum(counts, -1)
    places = jnp.arange(SEGS, dtype=jnp.int32)
    doc = jnp.sum((places[:, None] >= ends[..., None, :]).astype(jnp.int32), -1)
    slots = jnp.arange(counts.shape[-1], dtype=jnp.int32)
    first = jnp.sum(jnp.where(doc[..., None] == slots, (ends - counts)[..., None, :], 0), -1)
    return doc, places - first


def row_layout(counts):
    doc, pos = documents(counts)
    packs = counts.shape[0]
    label = doc + jnp.arange(packs, dtype=jnp.int32)[:, None] * (counts.shape[1] + 1)
    return wide_column(pos), wide_column(label), label.reshape(1, -1)


def wide_column(values):
    return jnp.broadcast_to(values.reshape(-1, 1), (values.size, 128))


def local(inputs, cotangent, wide, down, vectors, seg_counts):
    sections = lax.axis_size("section")
    replicas = lax.axis_size("dp")
    section = lax.axis_index("section")
    replica = lax.axis_index("dp")
    core, side = replica % 2, replica // 2 % 2
    rows, features = inputs.shape[1:]
    half = features // 2
    wide_w, down_w, vector = wide[0], down[0], vectors[0]
    x, cot = inputs[0], cotangent[0]

    fourth = 2 * side + core
    who = jnp.stack([section, core, fourth]).astype(jnp.int32)
    att_part, mlp_part = pl.pallas_call(
        parts_kernel,
        out_shape=[jax.ShapeDtypeStruct((2 * features, features), BF)] * 2,
        in_specs=[SMEM, ANY, ANY],
        out_specs=[ANY, ANY],
        scratch_shapes=[pltpu.VMEM((2 * features, features), BF)] * 2 + [pltpu.SemaphoreType.DMA((9,))],
        compiler_params=pltpu.CompilerParams(vmem_limit_bytes=LIMIT),
    )(who, wide_w, down_w)
    att_first = send(att_part, ATT_WAYS, 0, 1)
    near = [swap_section(vector, bits) for bits in (1, 2, 3)]
    mlp_first = send(mlp_part, MLP_WAYS, 0, 1)
    x_sib = swap_core(x)
    every_vector = jnp.stack([vector] + near)
    avec, mvec = pick(every_vector, section), pick(every_vector, section ^ 1)
    att_second = send(after(att_part, every_vector, mlp_first), ATT_WAYS, 0, 2)
    att_last = send(att_first, ATT_WAYS, 1, 3)
    mlp_second = send(after(mlp_part, every_vector, att_first, x_sib), MLP_WAYS, 0, 2)
    mlp_last = send(after(mlp_first, att_first), MLP_WAYS, 1, 3)

    grid = lambda values: values.reshape(-1, SEG, features)
    heads = lambda values: grid(values)[:, 0]
    count = sections * (rows // SEG)
    is_cls = (jnp.arange(rows) % SEG == 0)[:, None]
    b_own = after(jnp.where(is_cls, jnp.zeros_like(cot), cot), every_vector)
    b_next = swap_dp(b_own, 2)
    b_sib, b_far = swap_core(b_own), swap_core(b_next)
    layout = row_layout(seg_counts[0])

    bf = lambda *shape: (shape, BF)
    att_who = jnp.stack([place_of(ATT_WAYS, section, core), section]).astype(jnp.int32)
    att_choices = [att_part, att_first, att_second, att_last]
    att_weights = [pltpu.VMEM((features, 3 * half), BF), pltpu.VMEM((half, features), BF)]
    triple, a, give0, keep0 = call(
        att_fwd_kernel,
        [bf(2 * rows, 3 * half), bf(2 * rows, half), bf(rows, features), bf(rows, features)],
        [att_who, after(x, b_sib, b_far), x_sib, avec, *att_choices],
        att_weights
        + [pltpu.VMEM((2, rows, 3 * half), BF), pltpu.VMEM((2, rows, half), BF), pltpu.VMEM((2, rows, features), BF)]
        + [pltpu.SemaphoreType.DMA((10,))],
        scalars=1,
        anywhere=4,
        outside=True,
    )
    core0 = swap_core(give0)

    def hop(values, start, end):
        return permute(values, lambda s, r: (end, r), lambda s, r: s == start)

    def on(column, run):
        return lax.cond(section == column, lambda: run()[0], lambda: jnp.zeros((count, 2 * features), BF))

    branch = heads(keep0).astype(F32) + heads(core0).astype(F32)
    cls1_own = (heads(x).astype(F32) + branch + avec[2:3]).astype(BF)
    cls1 = jnp.concatenate(to_column(jnp.concatenate([cls1_own, heads(cot)], 1), 1), 0)
    h1, u_own = call(att_join_kernel, [bf(rows, features)] * 2, [x, keep0, after(core0, cls1_own), avec, mvec])
    u_sent = u_own
    u_own = after(u_own, cls1)
    u_next, u_sib = swap_dp(u_sent, 2), swap_core(u_own)
    cls2 = on(1, lambda: cls_step("out", cls1, cls1, wide_w, down_w, vector))
    cls2_at2 = hop(cls2, 1, 2)

    square = bf(features, features)
    scratch = [pltpu.VMEM((2 * rows, features), BF)] * 4 + [pltpu.VMEM(*square)] * 2
    scratch += [pltpu.VMEM((2, 2 * rows, features), BF)] + [pltpu.VMEM((2, features, features), BF)] * 2
    scratch += [pltpu.SemaphoreType.DMA((18,))]
    mlp_who = jnp.stack([place_of(MLP_WAYS, section, core), section // 2]).astype(jnp.int32)
    mlp_choices = [mlp_part, mlp_first, mlp_second, mlp_last]
    keep1, give1, dw, dv = call(
        partial(mlp_kernel, False),
        [bf(2 * rows, features)] * 2 + [square] * 2,
        [mlp_who, after(u_own, cls2), u_sib, b_own, b_sib, *mlp_choices],
        scratch,
        scalars=1,
        anywhere=8,
        outside=True,
    )
    u_far = swap_core(after(u_next, dw))
    keep2, give2, near_half, far_half = call(
        partial(mlp_kernel, True),
        [bf(2 * rows, features)] * 2 + [bf(2, half, features)] * 2,
        [mlp_who, after(u_next, cls2_at2), u_far, b_next, b_far, *mlp_choices, dw, dv],
        scratch,
        scalars=1,
        anywhere=10,
        outside=True,
    )
    core1, core2 = swap_core(give1), swap_core(give2)

    shape = [bf(count, 2 * features)]
    near_row = swap_section(far_half, 2)
    cls2_at2 = after(cls2_at2, far_half)
    blanks = lambda: [jnp.zeros((count, 2 * features), BF), jnp.zeros((count, 3 * features), BF)]
    cls3, cls_triple = lax.cond(
        section == 2,
        lambda: list(
            call(
                cls_att_fwd_kernel,
                shape + [bf(count, 3 * features)],
                [cls2_at2, *layout, wide_w, vector],
                [pltpu.VMEM((features, 4 * features), BF), pltpu.SemaphoreType.DMA((4,))],
                inside=4,
            )
        ),
        blanks,
    )
    cls3_at3 = hop(cls3, 2, 3)
    dcls3 = on(3, lambda: cls_step("both", cls3_at3, cls3_at3, wide_w, down_w, vector))
    dcls3_at2 = hop(dcls3, 3, 2)
    pair = pair_sum(keep2, after(core2, cls3))
    du_next = swap_dp(pair[:rows], 2)
    dcls2 = on(
        2, lambda: call(
            partial(cls_att_bwd_kernel, False),
            shape,
            [cls2_at2, dcls3_at2, cls_triple, *layout, wide_w, vector],
            [pltpu.VMEM((features, 4 * features), BF), pltpu.SemaphoreType.DMA((4,))],
            inside=6,
        )
    )
    dh1, mlp_small = call(
        mlp_done_kernel,
        [bf(rows, features), ((8, features), F32)],
        [h1, b_own, keep1, core1, du_next, mvec],
    )
    dcls2_at1 = after(hop(dcls2, 2, 1), dh1, near_row)
    out_next = swap_dp(after(pair[rows:], du_next), 2)
    dcls1 = on(1, lambda: cls_step("back", cls1, dcls2_at1, wide_w, down_w, vector))

    mine_in = jnp.where(section == 1, cls1, jnp.where(section == 2, cls2_at2, cls3_at3))
    mine_grad = jnp.where(section == 1, dcls2_at1[:, :features], dcls3_at2[:, :features])
    mine_grad = jnp.where(section == 3, cls3_at3[:, features:], mine_grad)
    marks = jnp.pad(jnp.concatenate([layout[0][:, :1], layout[1][:, :1] % (SEGS + 1)], 1), ((0, 0), (0, features - 2)))
    everything = jnp.concatenate([mine_in[:, :features], mine_grad, marks.astype(BF)], 0)
    split = dcls1.reshape(sections, rows // SEG, 2 * features)
    arrived = [hop(split[1 ^ bits], 1, 1 ^ bits) for bits in (1, 2, 3)]
    back_rows = jnp.where(section == 1, split[1], arrived[0] + arrived[1] + arrived[2])

    place = lambda values, cls: lax.dynamic_update_slice(grid(values), cls[:, None], (0, 0, 0)).reshape(rows, features)
    dh1 = place(dh1, back_rows[:, :features])
    dh1_sib = swap_core(dh1)


    xbit = section % 2
    mlp_half = pair_sum(near_half, near_row)
    near_block = swap_section(after(pick(mlp_half, 1 - xbit), dcls1), 1)
    mlp_block = pair_sum(pick(mlp_half, xbit), near_block)
    mlp_sum, bits = mlp_block, 4
    while bits < replicas:
        other = swap_dp(jnp.concatenate([mlp_sum, everything], 0), bits)
        mlp_sum = pair_sum(mlp_sum, other[:half])
        everything = ordered(everything, other[half:], replica & bits != 0)
        bits *= 2

    *att_grads, du0_own, du0_sib = call(
        att_bwd_kernel,
        [bf(half + 16, features)] * 4 + [bf(rows, features)] * 2,
        [att_who, avec, mlp_small, after(x, out_next, mlp_block), x_sib, dh1, dh1_sib, triple, a, *att_choices],
        [pltpu.VMEM((2 * rows, features), BF)] * 2
        + [pltpu.VMEM((2 * rows, 3 * half), BF), pltpu.VMEM((2 * rows, half), BF), *att_weights]
        + [pltpu.VMEM((2 * rows, features), BF), pltpu.VMEM((2 * rows, 3 * half), BF)]
        + [pltpu.VMEM((2, rows, features), BF), pltpu.VMEM((4, half + 16, features), BF)]
        + [pltpu.SemaphoreType.DMA((26,))],
        scalars=1,
        anywhere=10,
        outside=True,
        cost=17,
    )
    du0_core = swap_core(du0_sib)
    (input_grad,) = call(att_done_kernel, [bf(rows, features)], [x, dh1, du0_own, du0_core, avec])

    branch = keep1[rows:].astype(F32) + core1[rows:].astype(F32) + out_next.astype(F32)
    h2 = (h1.astype(F32) + branch + mvec[2:3]).astype(BF)
    layer_out = place(h2, back_rows[:, features:])
    other = swap_dp(jnp.concatenate([mlp_sum, everything], 0), 2)
    mlp_next, everything = other[:half], ordered(everything, other[half:], replica & 2 != 0)
    everything = ordered(everything, swap_core(everything), replica & 1 != 0).reshape(-1, 3, count, features)
    received, layer_out, input_grad = lax.optimization_barrier((section_parts(att_grads), layer_out, input_grad))
    att_block = section_sum(att_grads, received)
    mlp_blocks = jnp.stack(after([mlp_sum, mlp_next], received))
    att_block = pair_sum(att_block, swap_dp(att_block, 2))
    all_in, all_grad, marks = [everything[:, k].reshape(-1, features) for k in range(3)]
    all_pos, all_doc = marks[:, :1].astype(jnp.int32), marks[:, 1:2].astype(jnp.int32)
    all_doc += jnp.arange(all_doc.shape[0], dtype=jnp.int32)[:, None] // SEGS * (SEGS + 1)
    all_layout = (wide_column(all_pos), wide_column(all_doc), all_doc.reshape(1, -1))
    total = all_in.shape[0]
    none = lambda: [blank((total, features), BF)] + [blank((total, wide_w.shape[1]), BF) for _ in range(2)]

    def first_column():
        return [jnp.zeros(vector.shape, F32), blank(wide_w.shape), jnp.zeros(down_w.shape, F32), *none()]

    def second_column():
        sums, *factors = cls_mlp("factors", all_in, all_grad, wide_w, down_w, vector)
        return [sums, blank(wide_w.shape), blank(down_w.shape), *factors]

    def third_column():
        sums, wide_sum = cls_att_weights(all_in, all_grad, all_layout, wide_w, vector)
        return [sums, wide_sum, blank(down_w.shape), *none()]

    def fourth_column():
        return [*cls_mlp("weights", all_in, all_grad, wide_w, down_w, vector), *none()]

    vector_sum, wide_sum, down_sum, u_cls, dh_cls, act_cls = lax.switch(
        section, [first_column, second_column, third_column, fourth_column]
    )
    mlp_own = to_column(mlp_blocks, 1)
    att_block = pair_sum(att_block, after(swap_dp(att_block, 4), u_cls, mlp_own))
    att_block = dp_sum(att_block, 8)
    small = att_block[half:]
    small = (small.astype(F32) + swap_core(small).astype(F32))[:3]
    mine_small = jnp.where(section < 2, small, 0.0)
    vector_sum = vector_sum + jnp.pad(mine_small, ((0, vector.shape[0] - 3), (0, 0)))
    att_own, vector_sum = lax.optimization_barrier((to_column(att_block[:half], 0), vector_sum))
    att_other = [swap_core(piece) for piece in att_own]
    mlp_own = after(mlp_own, att_own)
    mlp_other = [swap_core(piece) for piece in mlp_own]
    wide_like, down_like = jax.ShapeDtypeStruct(wide_w.shape, F32), jax.ShapeDtypeStruct(down_w.shape, F32)
    for part, (att_pieces, mlp_pieces) in enumerate(((att_own, mlp_own), (att_other, mlp_other))):
        if part:
            att_pieces, mlp_pieces = after([att_pieces, mlp_pieces], wide_sum)
        wide_sum = pl.pallas_call(
            partial(att_place_kernel, part),
            out_shape=wide_like,
            in_specs=[SMEM] + [ANY] * 5,
            out_specs=ANY,
            scratch_shapes=[
                pltpu.VMEM((4, half, features), BF),
                pltpu.VMEM((features, 3 * half), F32),
                pltpu.VMEM((half, features), F32),
                pltpu.SemaphoreType.DMA((4,)),
                pltpu.SemaphoreType.DMA((4,)),
            ],
            input_output_aliases={5: 0},
            cost_estimate=estimate(0),
            compiler_params=pltpu.CompilerParams(vmem_limit_bytes=LIMIT),
        )(who, *att_pieces, wide_sum)
        wide_sum, down_sum = pl.pallas_call(
            partial(mlp_place_kernel, part),
            out_shape=[wide_like, down_like],
            in_specs=[SMEM] + [VMEM] * 4 + [ANY] * 6,
            out_specs=[ANY, ANY],
            scratch_shapes=[
                pltpu.VMEM((4, 2, half, features), BF),
                pltpu.VMEM((2, features, features), F32),
                pltpu.VMEM((2, features, features), F32),
                pltpu.SemaphoreType.DMA((4,)),
                pltpu.SemaphoreType.DMA((4,)),
            ],
            input_output_aliases={9: 0, 10: 1},
            cost_estimate=estimate(0),
            compiler_params=pltpu.CompilerParams(vmem_limit_bytes=LIMIT),
        )(who, u_cls, all_grad, dh_cls, act_cls, *mlp_pieces, wide_sum, down_sum)
    return layer_out[None], input_grad[None], wide_sum[None], down_sum[None], vector_sum[None]


def solution(mesh):
    return jax.shard_map(
        local,
        mesh=mesh,
        in_specs=(
            P("section", "dp", None),
            P("section", "dp", None),
            P("section", None, None),
            P("section", None, None),
            P("section", None, None),
            P("dp", None, None),
        ),
        out_specs=(
            P("section", "dp", None),
            P("section", "dp", None),
            P("section", None, None),
            P("section", None, None),
            P("section", None, None),
        ),
        check_vma=False,
    )
```
